512 devices in a mesh: plane: 128 (over z, y, core), layer: 4 (over x).
Axes of the slice: x: 4, y: 8, z: 8, core: 2. Of those that a mesh axis runs over, the one named last changes fastest.
Arguments:
- nodal_motion_vector: float32 [3, 32, 2048, 256], P(None, 'layer', 'plane'), may hold values from -6 to 6
- nodal_speed_vector: float32 [3, 32, 2048, 256], P(None, 'layer', 'plane'), may hold values from -6 to 6
- element_heating_increment: float32 [32, 2048, 256], P('layer', 'plane'), may hold values from -2 to -0.5
- element_medium_label: int32 [32, 2048, 256], P('layer', 'plane'), may hold values from 0 to 3
- medium_parameter_matrix: float32 [4, 4], replicated, may hold values from 0.5 to 2
- solder_vertex_position: int32 [128, 5, 128], P('plane'), may hold values from 0 to 4095
- landing_vertex_position: int32 [128, 5, 128], P('plane'), may hold values from 0 to 4095
- link_spring_coefficient: float32 [128, 5, 128], P('plane'), may hold values from 0.5 to 2
- active_link_tally: int32 [128, 5], P('plane'), may hold values from 0 to 128, as said below
Outputs:
- displacement_out: float32 [3, 32, 2048, 256], P(None, 'layer', 'plane')
- velocity_out: float32 [3, 32, 2048, 256], P(None, 'layer', 'plane')
The draws below stay inside these ranges and needn't reach their ends.
Inputs may be any that keep to these rules, and one draw needn't show every extreme that they name: `active_link_tally`: the live slots of a bucket are its first ones; in every draw some pad block receives 128 live pairs from every bump block within 2 blocks of it.
All inputs are finite; a program needn't handle non-finite values.
Results may differ from the reference program's by a relative error of at most 0.0001.
Values sent between devices are 32-bit elements; how exact they have to be, the bound alone decides.
No kernel may reach another device: no remote copies, remote signals or barrier semaphores. Data moves between devices by JAX's collectives and lax.ppermute only.
A program may use at most 64 MiB of HBM per device.

```python
import math
import jax
import jax.numpy as jnp
import numpy as np
from jax import lax

CX = 16
CY = 256
CAP = 128
HALF = 2
STEPS = 2
MATS = 4
BAND = 5
BLOCKS = 128
FACE = 4096
DEPTHWISE_POINTS = 32
DIVIDED_POINTS = 2048
LATERAL_POINTS = 256
PAD_Z = 19
BUMP_Z = 20
N_PLANE = 128


def draw_active_link_tally(key, part):
    key = jax.random.fold_in(key, 7)
    keys = jax.random.split(key, 3)
    blocks = DIVIDED_POINTS // CX
    base = jax.random.randint(keys[0], (blocks, BAND), 0, CAP + 1)
    hottest = jax.random.randint(keys[1], (), 0, blocks)
    owner = jnp.arange(blocks)[:, None]
    offset = jnp.arange(BAND)[None, :] - HALF
    toward = owner + offset == hottest
    heavy = jax.random.randint(keys[2], (blocks, 1), 0, 4) == 0
    return jnp.where(toward | heavy, CAP, base).astype(jnp.int32)


def plant(result, rng, low, high):
    spot = [jax.random.randint(jax.random.fold_in(rng, axis), (), 0, length) for axis, length in enumerate(result.shape)]
    longest = result.shape.index(max(result.shape))
    next_to = spot[:longest] + [(spot[longest] + 1) % result.shape[longest]] + spot[longest + 1:]
    return result.at[tuple(spot)].set(low).at[tuple(next_to)].set(high)


def steps_of(rng, dims, cuts, least, top_value):
    factor_of = 1.0
    for axis_at, parts in cuts:
        draws = jax.random.uniform(jax.random.fold_in(jax.random.fold_in(rng, 6), axis_at), (parts,), jnp.float32, least / len(cuts), top_value / len(cuts))
        factor_of = factor_of * jnp.repeat(jnp.exp(draws), dims[axis_at] // parts).reshape((-1,) + (1,) * (len(dims) - 1 - axis_at))
    return factor_of


def normal_values(own_key, extent, scale, reach, pieces=(), dtype=jnp.bfloat16):
    values = scale * jax.random.normal(own_key, extent, jnp.float32)
    if pieces:
        values = values * steps_of(own_key, extent, pieces, -0.22, 0.18)
    return jnp.clip(values, -reach, reach).astype(dtype)


def setup_inputs(seed: int = 0) -> dict:
    key_of = jax.random.split(jax.random.key(seed), 10)
    return {
        "nodal_motion_vector": normal_values(key_of[0], (3, DEPTHWISE_POINTS, DIVIDED_POINTS, LATERAL_POINTS), 1.0, 6.0, ((1, 4), (2, 128)), jnp.float32),
        "nodal_speed_vector": normal_values(key_of[1], (3, DEPTHWISE_POINTS, DIVIDED_POINTS, LATERAL_POINTS), 1.0, 6.0, ((1, 4), (2, 128)), jnp.float32),
        "element_heating_increment": jnp.clip(-2.0 + 1.5 * jax.random.uniform(key_of[2], (DEPTHWISE_POINTS, DIVIDED_POINTS, LATERAL_POINTS), jnp.float32) ** steps_of(key_of[2], (DEPTHWISE_POINTS, DIVIDED_POINTS, LATERAL_POINTS), ((0, 4), (1, 128)), -0.2, 0.2), -2.0, -0.5),
        "element_medium_label": plant(jax.random.randint(key_of[3], (DEPTHWISE_POINTS, DIVIDED_POINTS, LATERAL_POINTS), 0, MATS), jax.random.fold_in(key_of[3], 1), 0, MATS - 1).astype(jnp.int32),
        "medium_parameter_matrix": jnp.clip(jnp.exp(jax.random.uniform(key_of[4], (4, MATS), jnp.float32, math.log(0.5), math.log(2.0))), 0.5, 2.0),
        "solder_vertex_position": plant(jax.random.randint(key_of[5], (BLOCKS, BAND, CAP), 0, FACE), jax.random.fold_in(key_of[5], 1), 0, FACE - 1).astype(jnp.int32),
        "landing_vertex_position": plant(jax.random.randint(key_of[6], (BLOCKS, BAND, CAP), 0, FACE), jax.random.fold_in(key_of[6], 1), 0, FACE - 1).astype(jnp.int32),
        "link_spring_coefficient": jnp.clip(jnp.exp(math.log(2.0) - 1.3862944 * jax.random.uniform(key_of[7], (BLOCKS, BAND, CAP), jnp.float32) ** steps_of(key_of[7], (BLOCKS, BAND, CAP), ((0, 128),), -0.2, 0.2)), 0.5, 2.0),
        "active_link_tally": draw_active_link_tally(jax.random.fold_in(key_of[9], 71), 0),
    }


time_step = 0.05
lumped_extra = 0.25

def element_tables():
    points = [0.5 - 0.5 / math.sqrt(3.0), 0.5 + 0.5 / math.sqrt(3.0)]
    corner_bits = [(dz, dx, dy) for dz in (0, 1) for dx in (0, 1) for dy in (0, 1)]
    first = np.zeros((24, 24))
    second = np.zeros((24, 24))
    thermal = np.zeros(24)
    for point_z in points:
        for point_x in points:
            for point_y in points:
                point = (point_z, point_x, point_y)
                grads = np.zeros((8, 3))
                for corner, bit in enumerate(corner_bits):
                    for axis in range(3):
                        value = 1.0
                        for other in range(3):
                            if other == axis:
                                factor = 1.0 if bit[other] else -1.0
                            else:
                                factor = point[other] if bit[other] else 1.0 - point[other]
                            value = value * factor
                        grads[corner, axis] = value
                for a in range(3):
                    for c in range(8):
                        thermal[a * 8 + c] += 0.125 * grads[c, a]
                        for b in range(3):
                            for e in range(8):
                                first[a * 8 + c, b * 8 + e] += 0.125 * grads[c, a] * grads[e, b]
                                same = 1.0 if a == b else 0.0
                                second[a * 8 + c, b * 8 + e] += 0.125 * (same * np.dot(grads[c], grads[e]) + grads[c, b] * grads[e, a])
    both = np.concatenate([first, second], axis=1)
    return (jnp.asarray(both, jnp.float32), jnp.asarray(thermal, jnp.float32))

def element_medium_entries(element_medium_label, medium_parameter_matrix, element_heating_increment):
    fields = jnp.zeros((4,) + element_medium_label.shape, jnp.float32)
    for which in range(medium_parameter_matrix.shape[1]):
        chosen = (element_medium_label == which)[None]
        fields = fields + jnp.where(chosen, medium_parameter_matrix[:, which][:, None, None, None], jnp.float32(0.0))
    lambda_elastic_parameter, rigidity_parameter, heating_dilation_measure, density = (fields[0], fields[1], fields[2], fields[3])
    dilation_coefficient_value = (3.0 * lambda_elastic_parameter + 2.0 * rigidity_parameter) * heating_dilation_measure * element_heating_increment
    return jnp.stack([lambda_elastic_parameter, rigidity_parameter, dilation_coefficient_value, density])

def cell_mask(z_start, x_start, total_z, total_x, depth, width, length, gap_z):
    glob_z = z_start + jnp.arange(depth + 1) - 1
    glob_x = x_start + jnp.arange(width + 1) - 1
    inside_z = (glob_z >= 0) & (glob_z <= total_z - 2) & (glob_z != gap_z)
    inside_x = (glob_x >= 0) & (glob_x <= total_x - 2)
    inside_y = jnp.arange(length) < length - 1
    return (inside_z[:, None, None] & inside_x[None, :, None] & inside_y[None, None, :]).astype(jnp.float32)

def node_mass(cells):
    density = cells[3]
    depth = density.shape[0] - 1
    width = density.shape[1] - 1
    total = jnp.zeros((depth, width, density.shape[2]), jnp.float32)
    for dz in (0, 1):
        for dx in (0, 1):
            for dy in (0, 1):
                piece = density[1 - dz:1 - dz + depth, 1 - dx:1 - dx + width, :]
                if dy:
                    piece = jnp.roll(piece, 1, axis=2)
                total = total + piece
    return total * 0.125 + lumped_extra

def element_forces(padded_u, cells, stiff_both, thermal_g):
    width = cells.shape[2] - 1
    length = cells.shape[3]
    depth = cells.shape[1] - 1
    start = jnp.zeros(padded_u.shape, jnp.float32)

    def slab(k, total):
        rows = lax.dynamic_slice_in_dim(padded_u, k, 2, 1)
        cell = lax.dynamic_slice_in_dim(cells, k, 1, 1)[:, 0].reshape(4, -1)
        corners = []
        for dz in (0, 1):
            for dx in (0, 1):
                for dy in (0, 1):
                    piece = rows[:, dz, dx:dx + width + 1, :]
                    if dy:
                        piece = jnp.roll(piece, -1, axis=2)
                    corners.append(piece)
        cell_disp = jnp.stack(corners, 1).reshape(24, -1)
        stacked = jnp.concatenate([cell_disp * cell[0], cell_disp * cell[1]], 0)
        inner = jnp.dot(stiff_both, stacked, precision=lax.Precision.HIGHEST, preferred_element_type=jnp.float32)
        cell_force = (thermal_g[:, None] * cell[2] - inner).reshape(3, 8, width + 1, length)
        contrib = jnp.zeros((3, 2, width + 2, length), jnp.float32)
        corner = 0
        for dz in (0, 1):
            for dx in (0, 1):
                for dy in (0, 1):
                    value = cell_force[:, corner]
                    if dy:
                        value = jnp.roll(value, 1, axis=2)
                    contrib = contrib.at[:, dz, dx:dx + width + 1, :].add(value)
                    corner = corner + 1
        old = lax.dynamic_slice_in_dim(total, k, 2, 1)
        return lax.dynamic_update_slice_in_dim(total, old + contrib, k, 1)
    return lax.fori_loop(0, depth + 1, slab, start)

def reference(nodal_motion_vector, nodal_speed_vector, element_heating_increment, element_medium_label, medium_parameter_matrix, solder_vertex_position, landing_vertex_position, link_spring_coefficient, active_link_tally):
    stiff_both, thermal_g = element_tables()
    parameter_entries = element_medium_entries(element_medium_label, medium_parameter_matrix, element_heating_increment)
    cells = jnp.pad(parameter_entries, ((0, 0), (1, 0), (1, 0), (0, 0)))
    cells = cells * cell_mask(0, 0, DEPTHWISE_POINTS, DIVIDED_POINTS, DEPTHWISE_POINTS, DIVIDED_POINTS, LATERAL_POINTS, PAD_Z)[None]
    masses = node_mass(cells)
    owner = jnp.arange(N_PLANE)[:, None, None]
    offset = jnp.arange(BAND)[None, :, None] - HALF
    target = owner + offset
    valid = (target >= 0) & (target < N_PLANE)
    pad_block = jnp.clip(target, 0, N_PLANE - 1)
    live = (jnp.arange(CAP)[None, None, :] < active_link_tally[..., None]) & valid
    stiffness = jnp.where(live, link_spring_coefficient, jnp.float32(0.0)).reshape(-1)
    bump_glob = ((BUMP_Z * DIVIDED_POINTS + owner * CX + solder_vertex_position // CY) * LATERAL_POINTS + solder_vertex_position % CY).reshape(-1).astype(jnp.int32)
    pad_glob = ((PAD_Z * DIVIDED_POINTS + pad_block * CX + landing_vertex_position // CY) * LATERAL_POINTS + landing_vertex_position % CY).reshape(-1).astype(jnp.int32)
    for step in range(STEPS):
        padded = jnp.pad(nodal_motion_vector, ((0, 0), (1, 1), (1, 1), (0, 0)))
        forces = element_forces(padded, cells, stiff_both, thermal_g)[:, 1:-1, 1:-1, :]
        flat = nodal_motion_vector.reshape(3, -1)
        spring = stiffness * (flat[:, pad_glob] - flat[:, bump_glob])
        contact = jnp.zeros(flat.shape, jnp.float32).at[:, bump_glob].add(spring).at[:, pad_glob].add(-spring)
        forces = forces + contact.reshape(nodal_motion_vector.shape)
        nodal_speed_vector = nodal_speed_vector + time_step * forces / masses
        nodal_motion_vector = nodal_motion_vector + time_step * nodal_speed_vector
    return (nodal_motion_vector, nodal_speed_vector)
```

```python
import functools

import jax
import jax.numpy as jnp
from jax import lax
from jax.experimental import pallas as pl
from jax.experimental.pallas import tpu as pltpu
from jax.sharding import PartitionSpec as P

DT = 0.05
LUMPED = 0.25
F32 = jnp.float32
BF16 = jnp.bfloat16
QUADS = ((0, 0), (0, 1), (1, 0), (1, 1))

COL_U, COL_LAB, COL_DT, LISTS, FACES, R1_ROWS = 0, 24, 32, 40, 48, 144
R2_LISTS, R2_FACES, R2_ROWS = 0, 8, 104
ZU_U, ZU_V, ZU_LAB, ZU_DT, ZU_CL, ZU_CH, ZU_CLAB, ZU_CDT, ZU_ROWS = 0, 96, 144, 176, 208, 214, 220, 222, 224
ZD_U, ZD_V, ZD_LAB, ZD_DT, ZD_CL, ZD_CH, ZD_CLAB, ZD_CDT, ZD_ROWS = 0, 96, 144, 160, 176, 182, 188, 189, 192
S1_ROWS, S1_VALS = 40, 32


def iota(shape, dim):
    return lax.broadcasted_iota(jnp.int32, shape, dim)


def masked_stiffness(k, half, stiff_ref, tally_ref, blocks):
    target = lax.axis_index("plane") + (k - half)
    valid = (target >= 0) & (target < blocks)
    count = jnp.where(valid, tally_ref[0, k], 0)
    row = stiff_ref[0, k : k + 1, :]
    return jnp.where(iota(row.shape, 1) < count, row, 0.0)


def pack_plane(blocks, u, dt, lab, sol, land, stiff, tally, up, dn, up2, dn2):
    pad_z = u.shape[1] // 2 - 1
    for out, x in ((up, 15), (dn, 0)):
        for c in range(3):
            out[COL_U + 8 * c : COL_U + 8 * c + 8, :] = u[c, :, x, :]
        out[COL_LAB : COL_LAB + 8, :] = lab[:, x, :].astype(F32)
        out[COL_DT : COL_DT + 8, :] = dt[:, x, :]
    for out, k, lists, faces in (
        (up, 3, LISTS, FACES),
        (dn, 1, LISTS, FACES),
        (up2, 4, R2_LISTS, R2_FACES),
        (dn2, 0, R2_LISTS, R2_FACES),
    ):
        out[lists : lists + 8, :] = jnp.zeros((8, 256), F32)
        out[lists : lists + 1, 0:128] = sol[0, k : k + 1, :].astype(F32)
        out[lists + 1 : lists + 2, 0:128] = land[0, k : k + 1, :].astype(F32)
        out[lists + 2 : lists + 3, 0:128] = masked_stiffness(k, 2, stiff, tally, blocks)
        for c in range(3):
            for face in (0, 1):
                row = faces + 48 * face + 16 * c
                out[row : row + 16, :] = u[c, pad_z + face]


def pack_layer(u, v, dt, lab, lo, hi, up, dn):
    for c in range(3):
        for zz in (0, 1):
            row = 16 * (2 * c + zz)
            up[ZU_U + row : ZU_U + row + 16, :] = u[c, 6 + zz]
            dn[ZD_U + row : ZD_U + row + 16, :] = u[c, zz]
        up[ZU_V + 16 * c : ZU_V + 16 * c + 16, :] = v[c, 7]
        dn[ZD_V + 16 * c : ZD_V + 16 * c + 16, :] = v[c, 0]
        row = COL_U + 8 * c
        up[ZU_CL + 2 * c : ZU_CL + 2 * c + 2, :] = lo[row + 6 : row + 8, :]
        up[ZU_CH + 2 * c : ZU_CH + 2 * c + 2, :] = hi[row + 6 : row + 8, :]
        dn[ZD_CL + 2 * c : ZD_CL + 2 * c + 2, :] = lo[row : row + 2, :]
        dn[ZD_CH + 2 * c : ZD_CH + 2 * c + 2, :] = hi[row : row + 2, :]
    for zz in (0, 1):
        up[ZU_LAB + 16 * zz : ZU_LAB + 16 * zz + 16, :] = lab[6 + zz].astype(F32)
        up[ZU_DT + 16 * zz : ZU_DT + 16 * zz + 16, :] = dt[6 + zz]
    up[ZU_CLAB : ZU_CLAB + 2, :] = lo[COL_LAB + 6 : COL_LAB + 8, :]
    up[ZU_CDT : ZU_CDT + 2, :] = lo[COL_DT + 6 : COL_DT + 8, :]
    dn[ZD_LAB : ZD_LAB + 16, :] = lab[0].astype(F32)
    dn[ZD_DT : ZD_DT + 16, :] = dt[0]
    dn[ZD_CLAB : ZD_CLAB + 1, :] = lo[COL_LAB : COL_LAB + 1, :]
    dn[ZD_CDT : ZD_CDT + 1, :] = lo[COL_DT : COL_DT + 1, :]
    dn[ZD_CDT + 1 : ZD_ROWS, :] = jnp.zeros((ZD_ROWS - ZD_CDT - 1, 256), F32)


def material_scalars(par):
    out = []
    for m in range(4):
        lam, mu, alpha, rho = par[0, m], par[1, m], par[2, m], par[3, m]
        out.append(
            (
                lam * (1.0 / 16.0),
                mu * (1.0 / 16.0),
                (lam + 4.0 * mu) * (1.0 / 144.0),
                (3.0 * lam + 2.0 * mu) * alpha * 0.25,
                rho * 0.125,
            )
        )
    return out


def cell_fields(mats, lab, dt, mask, with_mass):
    is0, is1, is2 = lab == 0.0, lab == 1.0, lab == 2.0

    def pick(i):
        rest = jnp.where(is2, mats[2][i], mats[3][i])
        return jnp.where(is0, mats[0][i], jnp.where(is1, mats[1][i], rest)) * mask

    return pick(0), pick(1), pick(2), pick(3) * dt, pick(4) if with_mass else None


def plane_modes(u, ux):
    s, d = u + ux, ux - u
    sy, dy = pltpu.roll(s, 255, 1), pltpu.roll(d, 255, 1)
    return [s + sy, sy - s, d + dy, dy - d]


def cell_forces(lower, upper, l1, m1, k3, th):
    z, x, y = (
        {
            (i, j, k): (upper[c][q] - lower[c][q]) if i else (upper[c][q] + lower[c][q])
            for q, (j, k) in enumerate(QUADS)
            for i in (0, 1)
            if i + j + k
        }
        for c in range(3)
    )
    l2, m2 = l1 * (1.0 / 3.0), m1 * (1.0 / 3.0)
    p0 = l1 * (z[1, 0, 0] + x[0, 1, 0] + y[0, 0, 1]) - th
    m1x2 = m1 + m1
    zx = m1 * (x[1, 0, 0] + z[0, 1, 0])
    zy = m1 * (y[1, 0, 0] + z[0, 0, 1])
    xy = m1 * (y[0, 1, 0] + x[0, 0, 1])
    pz = l2 * (x[1, 1, 0] + y[1, 0, 1])
    px = l2 * (z[1, 1, 0] + y[0, 1, 1])
    py = l2 * (z[1, 0, 1] + x[0, 1, 1])
    tw = z[0, 1, 1] + x[1, 0, 1] + y[1, 1, 0]
    fz = {
        (1, 0, 0): p0 + m1x2 * z[1, 0, 0],
        (0, 1, 0): zx,
        (0, 0, 1): zy,
        (1, 1, 0): px + m1 * z[1, 1, 0],
        (1, 0, 1): py + m1 * z[1, 0, 1],
        (0, 1, 1): m2 * (tw + z[0, 1, 1]),
        (1, 1, 1): k3 * z[1, 1, 1],
    }
    fx = {
        (0, 1, 0): p0 + m1x2 * x[0, 1, 0],
        (1, 0, 0): zx,
        (0, 0, 1): xy,
        (1, 1, 0): pz + m1 * x[1, 1, 0],
        (0, 1, 1): py + m1 * x[0, 1, 1],
        (1, 0, 1): m2 * (tw + x[1, 0, 1]),
        (1, 1, 1): k3 * x[1, 1, 1],
    }
    fy = {
        (0, 0, 1): p0 + m1x2 * y[0, 0, 1],
        (1, 0, 0): zy,
        (0, 1, 0): xy,
        (1, 0, 1): pz + m1 * y[1, 0, 1],
        (0, 1, 1): px + m1 * y[0, 1, 1],
        (1, 1, 0): m2 * (tw + y[1, 1, 0]),
        (1, 1, 1): k3 * y[1, 1, 1],
    }
    low, high = [], []
    for f in (fz, fx, fy):
        low_c, high_c = [], []
        for j, k in QUADS:
            d = f[1, j, k]
            if j + k:
                s = f[0, j, k]
                low_c.append(s - d)
                high_c.append(s + d)
            else:
                low_c.append(-d)
                high_c.append(d)
        low.append(low_c)
        high.append(high_c)
    return low, high


def fold_y(a, b):
    return (a - b) + pltpu.roll(a + b, 1, 1)


def column_forces(blocks, layers, zbase, mats, col_lo, col_own, col_lab, col_dt, col_f, col_m):
    rows = col_lab.shape[0]
    shape = (rows, 256)
    zg = iota(shape, 0) + zbase
    gap = layers // 2 * 8 + 3
    ok = (zg >= 0) & (zg <= layers * 8 - 2) & (zg != gap) & (iota(shape, 1) < 255)
    mask = jnp.where(ok & (lax.axis_index("plane") > 0), 1.0, 0.0)
    l1, m1, k3, th, rho = cell_fields(mats, col_lab[...], col_dt[...], mask, col_m is not None)
    lower = [plane_modes(col_lo[c], col_own[c]) for c in range(3)]
    upper = [[pltpu.roll(a, rows - 1, 0) for a in comp] for comp in lower]
    low, high = cell_forces(lower, upper, l1, m1, k3, th)
    for c in range(3):
        node = [low[c][q] + pltpu.roll(high[c][q], 1, 0) for q in range(4)]
        col_f[c] = fold_y(node[0], node[1]) + fold_y(node[2], node[3])
    if col_m is not None:
        rho = rho + pltpu.roll(rho, 1, 1)
        col_m[...] = rho + pltpu.roll(rho, 1, 0)


def elastic_steps(
    blocks, layers, cells, zbase, mats, u, lab, dt, col_hi, col_f, col_m, modes, saved, saved_m, finish
):
    shape = (16, 256)
    row, lane = iota(shape, 0), iota(shape, 1)
    last = jnp.where(lax.axis_index("plane") == blocks - 1, 15, 16)
    in_plane = jnp.where((lane < 255) & (row < last), 1.0, 0.0)
    gap = layers // 2 * 8 + 3
    first_row, last_row = row == 0, row == 15

    def forward(e, c):
        a = u[c, e]
        halo = jnp.broadcast_to(col_hi[c, pl.ds(e, 1), :], shape)
        return plane_modes(a, jnp.where(last_row, halo, pltpu.roll(a, 15, 0)))

    for c in range(3):
        for q, value in enumerate(forward(0, c)):
            modes[4 * c + q] = value

    def body(e, carry):
        zg = zbase + e
        ok = (zg >= 0) & (zg <= layers * 8 - 2) & (zg != gap)
        scale = jnp.where(ok, 1.0, 0.0)
        l1, m1, k3, th, rho = cell_fields(mats, lab[e], dt[e], in_plane * scale, col_m is not None)
        lower = [[modes[4 * c + q] for q in range(4)] for c in range(3)]
        upper = [forward(e + 1, c) for c in range(3)]
        for c in range(3):
            for q in range(4):
                modes[4 * c + q] = upper[c][q]
        low, high = cell_forces(lower, upper, l1, m1, k3, th)
        force = []
        for c in range(3):
            node = [low[c][q] + saved[4 * c + q] for q in range(4)]
            for q in range(4):
                saved[4 * c + q] = high[c][q]
            t0, t1 = fold_y(node[0], node[1]), fold_y(node[2], node[3])
            halo = jnp.broadcast_to(col_f[c, pl.ds(e, 1), :], shape)
            force.append((t0 - t1) + jnp.where(first_row, halo, pltpu.roll(t0 + t1, 1, 0)))
        mass = None
        if col_m is not None:
            rho = rho + pltpu.roll(rho, 1, 1)
            rho = rho + jnp.where(first_row, 0.0, pltpu.roll(rho, 1, 0))
            halo = jnp.broadcast_to(col_m[pl.ds(e, 1), :], shape)
            mass = LUMPED + (rho + saved_m[...]) + jnp.where(first_row, halo, 0.0)
            saved_m[...] = rho
        finish(e, force, mass)
        return carry

    lax.fori_loop(0, cells, body, 0)


def split3(a):
    hi = a.astype(BF16)
    rest = a - hi.astype(F32)
    mid = rest.astype(BF16)
    lo = (rest - mid.astype(F32)).astype(BF16)
    return jnp.concatenate([hi, mid, lo], axis=0)


def join3(a):
    n = a.shape[0] // 3
    return (a[:n] + a[n : 2 * n]) + a[2 * n :]


def one_hots(position):
    pos = position.astype(jnp.int32)
    n = pos.shape[1]
    y, x = pos & 255, pos >> 8
    ohy = jnp.where(iota((256, n), 0) == y, 1.0, 0.0).astype(BF16)
    ohx = jnp.where(iota((16, n), 0) == x, 1.0, 0.0)
    return ohy, ohx


def gather(face, ohy, ohx):
    n = ohx.shape[1]
    rows = join3(jnp.dot(split3(face), ohy, preferred_element_type=F32))
    return jnp.sum(rows.reshape(3, 16, n) * ohx[None], axis=1)


def scatter(values, ohy, ohx):
    n = ohx.shape[1]
    rows = (values[:, None, :] * ohx[None]).reshape(48, n)
    out = lax.dot_general(split3(rows), ohy, (((1,), (1,)), ((), ())), preferred_element_type=F32)
    return join3(out).reshape(3, 16, 256)


def fill_lists(blocks, sol, land, stiff, tally, r_lo, r_hi, q_lo, q_hi, lists):
    for k in range(5):
        cols = slice(128 * k, 128 * k + 128)
        lists[0:1, cols] = sol[0, k : k + 1, :].astype(F32)
        lists[1:2, cols] = land[0, k : k + 1, :].astype(F32)
        lists[2:3, cols] = masked_stiffness(k, 2, stiff, tally, blocks)
    for j, ref, row in ((0, q_lo, R2_LISTS), (1, r_lo, LISTS), (3, r_hi, LISTS), (4, q_hi, R2_LISTS)):
        lists[3:6, 128 * j : 128 * j + 128] = ref[row : row + 3, 0:128]
    lists[3:6, 256:384] = lists[0:3, 256:384]


def first_step(
    blocks, layers,
    u, v, dt, lab, par, sol, land, stiff, tally, r_lo, r_hi, q_lo, q_hi, zb, za,
    u1, v1, dtm, up, dn, up2, dn2, vals,
    ue, le, de, col_lo, col_own, col_hi, col_lab, col_dt, col_f, col_m, modes, saved, saved_m, lists,
):
    layer = lax.axis_index("layer")
    zbase = layer * 8 - 2
    zeros = jnp.zeros((8, 256), F32)
    for c in range(3):
        for zz in (0, 1):
            row = 16 * (2 * c + zz)
            ue[c, zz] = zb[ZU_U + row : ZU_U + row + 16, :]
            ue[c, 10 + zz] = za[ZD_U + row : ZD_U + row + 16, :]
        ue[c, 2:10] = u[c]
        v1[c, 0] = zb[ZU_V + 16 * c : ZU_V + 16 * c + 16, :]
        v1[c, 9] = za[ZD_V + 16 * c : ZD_V + 16 * c + 16, :]
        v1[c, 1:9] = v[c]
        for col, src, zu, zd in ((col_lo, r_lo, ZU_CL, ZD_CL), (col_hi, r_hi, ZU_CH, ZD_CH)):
            col[c, 8:16, :] = zeros
            col[c, 0:2, :] = zb[zu + 2 * c : zu + 2 * c + 2, :]
            col[c, 2:10, :] = src[COL_U + 8 * c : COL_U + 8 * c + 8, :]
            col[c, 10:12, :] = za[zd + 2 * c : zd + 2 * c + 2, :]
        col_own[c, 8:16, :] = zeros
        col_own[c, 0:8, :] = ue[c, 0:8, 0, :]
        col_own[c, 8:12, :] = ue[c, 8:12, 0, :]
    for zz in (0, 1):
        le[zz] = zb[ZU_LAB + 16 * zz : ZU_LAB + 16 * zz + 16, :]
        de[zz] = zb[ZU_DT + 16 * zz : ZU_DT + 16 * zz + 16, :]
    le[2:10] = lab[...].astype(F32)
    de[2:10] = dt[...]
    le[10] = za[ZD_LAB : ZD_LAB + 16, :]
    de[10] = za[ZD_DT : ZD_DT + 16, :]
    for col, src, zu, zd in ((col_lab, COL_LAB, ZU_CLAB, ZD_CLAB), (col_dt, COL_DT, ZU_CDT, ZD_CDT)):
        col[8:16, :] = zeros
        col[0:2, :] = zb[zu : zu + 2, :]
        col[2:10, :] = r_lo[src : src + 8, :]
        col[10:11, :] = za[zd : zd + 1, :]

    mats = material_scalars(par)
    column_forces(blocks, layers, zbase, mats, col_lo, col_own, col_lab, col_dt, col_f, col_m)

    def finish(e, force, mass):
        at = jnp.maximum(e - 1, 0)
        rate = DT / mass
        dtm[at] = rate
        for c in range(3):
            speed = v1[c, at] - rate * force[c]
            u1[c, at] = ue[c, e] + DT * speed

            @pl.when(e > 0)
            def _():
                v1[c, at] = speed

    elastic_steps(
        blocks, layers, 11, zbase, mats, ue, le, de, col_hi, col_f, col_m, modes, saved, saved_m, finish
    )

    @pl.when(layer == layers // 2)
    def _():
        fill_lists(blocks, sol, land, stiff, tally, r_lo, r_hi, q_lo, q_hi, lists)
        sol_y, sol_x = one_hots(lists[0:1, :])
        land_y, land_x = one_hots(lists[4:5, :])
        other_land_y, other_land_x = one_hots(lists[1:2, :])
        other_sol_y, other_sol_x = one_hots(lists[3:4, :])

        def face_of(k, face):
            if k == 2:
                return jnp.concatenate([u[c, 3 + face] for c in range(3)], axis=0)
            ref, row = ((q_lo, R2_FACES), (r_lo, FACES), None, (r_hi, FACES), (q_hi, R2_FACES))[k]
            return ref[row + 48 * face : row + 48 * face + 48, :]

        bump = gather(face_of(2, 1), sol_y, sol_x)
        pad = gather(face_of(2, 0), land_y, land_x)
        far_pad, far_bump = [], []
        for k in range(5):
            cols = slice(128 * k, 128 * k + 128)
            far_pad.append(gather(face_of(k, 0), other_land_y[:, cols], other_land_x[:, cols]))
            far_bump.append(gather(face_of(k, 1), other_sol_y[:, cols], other_sol_x[:, cols]))
        on_bump = lists[2:3, :] * (jnp.concatenate(far_pad, axis=1) - bump)
        on_pad = lists[5:6, :] * (jnp.concatenate(far_bump, axis=1) - pad)
        bump_force = scatter(on_bump, sol_y, sol_x)
        pad_force = scatter(on_pad, land_y, land_x)
        for c in range(3):
            for at, extra in ((4, pad_force[c]), (5, bump_force[c])):
                change = dtm[at] * extra
                v1[c, at] = v1[c, at] + change
                u1[c, at] = u1[c, at] + DT * change
        new_pad = jnp.concatenate([u1[c, 4] for c in range(3)], axis=0)
        new_bump = jnp.concatenate([u1[c, 5] for c in range(3)], axis=0)
        vals[0:3, :] = gather(new_bump, sol_y, sol_x)
        vals[3:6, :] = gather(new_pad, land_y, land_x)
        for out, k, row in ((up, 3, S1_VALS), (dn, 1, S1_VALS), (up2, 4, 0), (dn2, 0, 0)):
            out[row : row + 6, 0:128] = vals[0:6, 128 * k : 128 * k + 128]

    for out, x in ((up, 15), (dn, 0)):
        for c in range(3):
            out[10 * c : 10 * c + 8, :] = u1[c, 0:8, x, :]
            out[10 * c + 8 : 10 * c + 10, :] = u1[c, 8:10, x, :]


def second_step(
    blocks, layers,
    u, v, dtm, dt, lab, par, sol, land, stiff, tally, r_lo, r_hi, q_lo, q_hi, zb, vals, own, s_lo, s_hi, t_lo, t_hi,
    u2, v2,
    le, de, col_lo, col_own, col_hi, col_lab, col_dt, col_f, modes, saved, lists,
):
    layer = lax.axis_index("layer")
    zbase = layer * 8 - 1
    zeros = jnp.zeros((8, 256), F32)
    for c in range(3):
        for col, src in ((col_lo, s_lo), (col_hi, s_hi), (col_own, own)):
            col[c, 8:16, :] = zeros
            col[c, 0:10, :] = src[10 * c : 10 * c + 10, :]
    le[0] = zb[ZU_LAB + 16 : ZU_LAB + 32, :]
    de[0] = zb[ZU_DT + 16 : ZU_DT + 32, :]
    le[1:9] = lab[...].astype(F32)
    de[1:9] = dt[...]
    for col, src, zu in ((col_lab, COL_LAB, ZU_CLAB), (col_dt, COL_DT, ZU_CDT)):
        col[8:16, :] = zeros
        col[0:1, :] = zb[zu + 1 : zu + 2, :]
        col[1:9, :] = r_lo[src : src + 8, :]

    mats = material_scalars(par)
    column_forces(blocks, layers, zbase, mats, col_lo, col_own, col_lab, col_dt, col_f, None)

    def finish(e, force, mass):
        at = jnp.maximum(e - 1, 0)
        rate = dtm[e]
        for c in range(3):
            speed = v[c, e] - rate * force[c]
            v2[c, at] = speed
            u2[c, at] = u[c, e] + DT * speed

    elastic_steps(blocks, layers, 9, zbase, mats, u, le, de, col_hi, col_f, None, modes, saved, None, finish)

    @pl.when(layer == layers // 2)
    def _():
        fill_lists(blocks, sol, land, stiff, tally, r_lo, r_hi, q_lo, q_hi, lists)
        sol_y, sol_x = one_hots(lists[0:1, :])
        land_y, land_x = one_hots(lists[4:5, :])

        def far(first):
            parts = [
                t_lo[first : first + 3, 0:128],
                s_lo[S1_VALS + first : S1_VALS + first + 3, 0:128],
                vals[first : first + 3, 256:384],
                s_hi[S1_VALS + first : S1_VALS + first + 3, 0:128],
                t_hi[first : first + 3, 0:128],
            ]
            return jnp.concatenate(parts, axis=1)

        on_bump = lists[2:3, :] * (far(3) - vals[0:3, :])
        on_pad = lists[5:6, :] * (far(0) - vals[3:6, :])
        bump_force = scatter(on_bump, sol_y, sol_x)
        pad_force = scatter(on_pad, land_y, land_x)
        for c in range(3):
            for at, extra in ((3, pad_force[c]), (4, bump_force[c])):
                change = dtm[at + 1] * extra
                v2[c, at] = v2[c, at] + change
                u2[c, at] = u2[c, at] + DT * change


VM = pl.BlockSpec(memory_space=pltpu.VMEM)
SM = pl.BlockSpec(memory_space=pltpu.SMEM)


def call(kernel, in_specs, outs, scratch, name, flops):
    return pl.pallas_call(
        kernel,
        out_shape=[jax.ShapeDtypeStruct(shape, F32) for shape in outs],
        in_specs=in_specs,
        out_specs=[VM] * len(outs),
        scratch_shapes=[pltpu.VMEM(shape, F32) for shape in scratch],
        compiler_params=pltpu.CompilerParams(vmem_limit_bytes=32 * 1024 * 1024),
        cost_estimate=pl.CostEstimate(flops=flops, bytes_accessed=2_000_000, transcendentals=0),
        name=name,
    )


def local(u, v, dt, lab, par, sol, land, stiff, tally):
    blocks, layers = lax.axis_size("plane"), lax.axis_size("layer")
    face_layer = layers // 2

    def along_plane(value, steps):
        pairs = [(s, s + steps) for s in range(blocks) if 0 <= s + steps < blocks]
        return lax.ppermute(value, "plane", pairs)

    def along_face(value, steps):
        pairs = [
            (s * layers + face_layer, (s + steps) * layers + face_layer)
            for s in range(blocks)
            if 0 <= s + steps < blocks
        ]
        return lax.ppermute(value, ("plane", "layer"), pairs)

    def along_layer(value, steps):
        pairs = [(s, s + steps) for s in range(layers) if 0 <= s + steps < layers]
        return lax.ppermute(value, "layer", pairs)

    up, dn, up2, dn2 = call(
        functools.partial(pack_plane, blocks),
        [VM] * 6 + [SM],
        [(R1_ROWS, 256), (R1_ROWS, 256), (R2_ROWS, 256), (R2_ROWS, 256)],
        [],
        "pack_plane",
        100_000,
    )(u, dt, lab, sol, land, stiff, tally)
    r_lo, r_hi = along_plane(up, 1), along_plane(dn, -1)
    q_lo, q_hi = along_face(up2, 2), along_face(dn2, -2)
    zu, zd = call(pack_layer, [VM] * 6, [(ZU_ROWS, 256), (ZD_ROWS, 256)], [], "pack_layer", 100_000)(
        u, v, dt, lab, r_lo, r_hi
    )
    zb, za = along_layer(zu, 1), along_layer(zd, -1)

    col, plane = (3, 16, 256), (16, 256)
    u1, v1, dtm, up, dn, up2, dn2, vals = call(
        functools.partial(first_step, blocks, layers),
        [VM] * 4 + [SM] + [VM] * 3 + [SM] + [VM] * 6,
        [(3, 10, 16, 256), (3, 10, 16, 256), (10, 16, 256)]
        + [(S1_ROWS, 256)] * 2 + [(8, 128)] * 2 + [(8, 640)],
        [(3, 12, 16, 256), (11, 16, 256), (11, 16, 256), col, col, col, plane, plane, col, plane]
        + [(12, 16, 256), (12, 16, 256), plane, (8, 640)],
        "first_step",
        50_000_000,
    )(u, v, dt, lab, par, sol, land, stiff, tally, r_lo, r_hi, q_lo, q_hi, zb, za)
    s_lo, s_hi = along_plane(up, 1), along_plane(dn, -1)
    t_lo, t_hi = along_face(up2, 2), along_face(dn2, -2)
    return tuple(
        call(
            functools.partial(second_step, blocks, layers),
            [VM] * 5 + [SM] + [VM] * 3 + [SM] + [VM] * 11,
            [(3, 8, 16, 256), (3, 8, 16, 256)],
            [(9, 16, 256), (9, 16, 256), col, col, col, plane, plane, col]
            + [(12, 16, 256), (12, 16, 256), (8, 640)],
            "second_step",
            50_000_000,
        )(u1, v1, dtm, dt, lab, par, sol, land, stiff, tally, r_lo, r_hi, q_lo, q_hi, zb, vals, dn, s_lo, s_hi, t_lo, t_hi)
    )


def solution(mesh):
    in_specs = (
        P(None, "layer", "plane", None),
        P(None, "layer", "plane", None),
        P("layer", "plane", None),
        P("layer", "plane", None),
        P(),
        P("plane", None, None),
        P("plane", None, None),
        P("plane", None, None),
        P("plane", None),
    )
    out_specs = (P(None, "layer", "plane", None), P(None, "layer", "plane", None))
    return jax.shard_map(local, mesh=mesh, in_specs=in_specs, out_specs=out_specs, check_vma=False)
```

```python
import functools

import jax
import jax.numpy as jnp
from jax import lax
from jax.experimental import pallas as pl
from jax.experimental.pallas import tpu as pltpu
from jax.sharding import PartitionSpec as P

DT = 0.05
LUMPED = 0.25
F32 = jnp.float32
BF16 = jnp.bfloat16
QUADS = ((0, 0), (0, 1), (1, 0), (1, 1))

COL_HI, COL_LO, LISTS, PAD, EXPORT_ROWS = 0, 40, 64, 88, 136
OWN_LISTS, MATE_LISTS, OWN_PAD, MATE_PAD, CROSS_ROWS = 40, 64, 88, 136, 184
COL_LAB, COL_DT, COL_BEYOND, COLS_ROWS = 24, 32, 40, 64
ZU_U, ZU_V, ZU_LAB, ZU_DT, ZU_CL, ZU_CH, ZU_CLAB, ZU_CDT, ZU_ROWS = 0, 96, 144, 176, 208, 214, 220, 222, 224
ZD_U, ZD_V, ZD_LAB, ZD_DT, ZD_CL, ZD_CH, ZD_CLAB, ZD_CDT, ZD_ROWS = 0, 96, 144, 160, 176, 182, 188, 189, 192
NEW_HI, NEW_LO, NEW_VALS, NEW_ROWS = 0, 32, 64, 88
CROSS_OWN, CROSS_MATE, CROSS_ON, NEW_CROSS_ROWS = 32, 36, 40, 48
NEAR, FAR1, OWN, FAR2, OPP2 = range(5)
OFFSETS = (1, -1, 0, -2, 2)


def iota(shape, dim):
    return lax.broadcasted_iota(jnp.int32, shape, dim)


def on_even():
    return lax.rem(lax.axis_index("plane"), 2) == 0


def role_offset(role):
    return jnp.where(on_even(), OFFSETS[role], -OFFSETS[role])


def pack_export(
    blocks, layers,
    u_hbm, dt_hbm, lab_hbm, sol_hbm, land_hbm, stiff_hbm, tally_hbm,
    out,
    u, dt, lab, sol, land, stiff, tally, pos, sems,
):
    copies = [
        pltpu.make_async_copy(src, dst, sems.at[i])
        for i, (src, dst) in enumerate(
            (
                (u_hbm, u), (dt_hbm, dt), (lab_hbm, lab), (sol_hbm, sol),
                (land_hbm, land), (stiff_hbm, stiff), (tally_hbm, tally),
            )
        )
    ]
    for copy in copies:
        copy.start()
    for copy in copies:
        copy.wait()
    pad_z = u.shape[1] // 2 - 1
    here = lax.axis_index("plane")
    for x, row in ((15, COL_HI), (0, COL_LO)):
        for c in range(3):
            out[row + 8 * c : row + 8 * c + 8, :] = u[c, :, x, :]
    out[COL_HI + COL_LAB : COL_HI + COL_LAB + 8, :] = lab[:, 15, :].astype(F32)
    out[COL_HI + COL_DT : COL_HI + COL_DT + 8, :] = dt[:, 15, :]

    @pl.when(lax.axis_index("layer") == layers // 2)
    def _():
        out[LISTS : LISTS + 24, :] = jnp.zeros((24, 256), F32)
        for k in range(5):
            row = LISTS + 4 * k
            target = here + (k - 2)
            count = jnp.where((target >= 0) & (target < blocks), tally[0, k], 0)
            live = iota((1, 128), 1) < count
            out[row : row + 1, 0:128] = sol[k].astype(F32)
            out[row : row + 1, 128:256] = land[k].astype(F32)
            out[row + 1 : row + 2, 0:128] = jnp.where(live, stiff[k], 0.0)
            pos[0:1, 128 * k : 128 * k + 128] = sol[k]
        bump = gather(jnp.concatenate([u[c, pad_z + 1] for c in range(3)], axis=0), *one_hots(pos[0:1, :]))
        for k in range(5):
            row, cols = LISTS + 4 * k, slice(128 * k, 128 * k + 128)
            out[row + 1 : row + 2, 128:256] = bump[0:1, cols]
            out[row + 2 : row + 3, 0:128] = bump[1:2, cols]
            out[row + 2 : row + 3, 128:256] = bump[2:3, cols]
        for c in range(3):
            out[PAD + 16 * c : PAD + 16 * c + 16, :] = u[c, pad_z]


def pack_cross(own, mate, out):
    out[24:40, :] = mate[COL_HI + 24 : COL_HI + 40, :]
    out[0:24, :] = jnp.where(on_even(), mate[COL_HI : COL_HI + 24, :], mate[COL_LO : COL_LO + 24, :])
    out[OWN_LISTS : OWN_LISTS + 24, :] = own[LISTS : LISTS + 24, :]
    out[MATE_LISTS : MATE_LISTS + 24, :] = mate[LISTS : LISTS + 24, :]
    out[OWN_PAD : OWN_PAD + 48, :] = own[PAD : PAD + 48, :]
    out[MATE_PAD : MATE_PAD + 48, :] = mate[PAD : PAD + 48, :]


def pack_new_cross(own, mate, out):
    out[0:32, :] = jnp.where(on_even(), mate[NEW_HI : NEW_HI + 32, :], mate[NEW_LO : NEW_LO + 32, :])
    for row, src, role in ((CROSS_OWN, own, OPP2), (CROSS_MATE, mate, FAR1), (CROSS_ON, mate, FAR2)):
        out[row : row + 4, :] = src[NEW_VALS + 4 * role : NEW_VALS + 4 * role + 4, :]
    out[44:48, :] = jnp.zeros((4, 256), F32)


def pack_layer(u, v, dt, lab, near, far, up, dn, cols):
    even = on_even()
    cols[0:40, :] = jnp.where(even, far[0:40, :], near[COL_HI : COL_HI + 40, :])
    cols[COL_BEYOND : COL_BEYOND + 24, :] = jnp.where(even, near[COL_LO : COL_LO + 24, :], far[0:24, :])
    for c in range(3):
        for zz in (0, 1):
            row = 16 * (2 * c + zz)
            up[ZU_U + row : ZU_U + row + 16, :] = u[c, 6 + zz]
            dn[ZD_U + row : ZD_U + row + 16, :] = u[c, zz]
        up[ZU_V + 16 * c : ZU_V + 16 * c + 16, :] = v[c, 7]
        dn[ZD_V + 16 * c : ZD_V + 16 * c + 16, :] = v[c, 0]
        lo, hi = 8 * c, COL_BEYOND + 8 * c
        up[ZU_CL + 2 * c : ZU_CL + 2 * c + 2, :] = cols[lo + 6 : lo + 8, :]
        up[ZU_CH + 2 * c : ZU_CH + 2 * c + 2, :] = cols[hi + 6 : hi + 8, :]
        dn[ZD_CL + 2 * c : ZD_CL + 2 * c + 2, :] = cols[lo : lo + 2, :]
        dn[ZD_CH + 2 * c : ZD_CH + 2 * c + 2, :] = cols[hi : hi + 2, :]
    for zz in (0, 1):
        up[ZU_LAB + 16 * zz : ZU_LAB + 16 * zz + 16, :] = lab[6 + zz].astype(F32)
        up[ZU_DT + 16 * zz : ZU_DT + 16 * zz + 16, :] = dt[6 + zz]
    up[ZU_CLAB : ZU_CLAB + 2, :] = cols[COL_LAB + 6 : COL_LAB + 8, :]
    up[ZU_CDT : ZU_CDT + 2, :] = cols[COL_DT + 6 : COL_DT + 8, :]
    dn[ZD_LAB : ZD_LAB + 16, :] = lab[0].astype(F32)
    dn[ZD_DT : ZD_DT + 16, :] = dt[0]
    dn[ZD_CLAB : ZD_CLAB + 1, :] = cols[COL_LAB : COL_LAB + 1, :]
    dn[ZD_CDT : ZD_CDT + 1, :] = cols[COL_DT : COL_DT + 1, :]
    dn[ZD_CDT + 1 : ZD_ROWS, :] = jnp.zeros((ZD_ROWS - ZD_CDT - 1, 256), F32)


def material_scalars(par):
    out = []
    for m in range(4):
        lam, mu, alpha, rho = par[0, m], par[1, m], par[2, m], par[3, m]
        out.append(
            (
                lam * (1.0 / 16.0),
                mu * (1.0 / 16.0),
                (lam + 4.0 * mu) * (1.0 / 144.0),
                (3.0 * lam + 2.0 * mu) * alpha * 0.25,
                rho * 0.125,
            )
        )
    return out


def cell_fields(mats, lab, dt, mask, with_mass):
    is0, is1, is2 = lab == 0.0, lab == 1.0, lab == 2.0

    def pick(i):
        rest = jnp.where(is2, mats[2][i], mats[3][i])
        return jnp.where(is0, mats[0][i], jnp.where(is1, mats[1][i], rest)) * mask

    return pick(0), pick(1), pick(2), pick(3) * dt, pick(4) if with_mass else None


def plane_modes(u, ux):
    s, d = u + ux, ux - u
    sy, dy = pltpu.roll(s, 255, 1), pltpu.roll(d, 255, 1)
    return [s + sy, sy - s, d + dy, dy - d]


def cell_forces(lower, upper, l1, m1, k3, th):
    z, x, y = (
        {
            (i, j, k): (upper[c][q] - lower[c][q]) if i else (upper[c][q] + lower[c][q])
            for q, (j, k) in enumerate(QUADS)
            for i in (0, 1)
            if i + j + k
        }
        for c in range(3)
    )
    l2, m2 = l1 * (1.0 / 3.0), m1 * (1.0 / 3.0)
    p0 = l1 * (z[1, 0, 0] + x[0, 1, 0] + y[0, 0, 1]) - th
    m1x2 = m1 + m1
    zx = m1 * (x[1, 0, 0] + z[0, 1, 0])
    zy = m1 * (y[1, 0, 0] + z[0, 0, 1])
    xy = m1 * (y[0, 1, 0] + x[0, 0, 1])
    pz = l2 * (x[1, 1, 0] + y[1, 0, 1])
    px = l2 * (z[1, 1, 0] + y[0, 1, 1])
    py = l2 * (z[1, 0, 1] + x[0, 1, 1])
    tw = z[0, 1, 1] + x[1, 0, 1] + y[1, 1, 0]
    fz = {
        (1, 0, 0): p0 + m1x2 * z[1, 0, 0],
        (0, 1, 0): zx,
        (0, 0, 1): zy,
        (1, 1, 0): px + m1 * z[1, 1, 0],
        (1, 0, 1): py + m1 * z[1, 0, 1],
        (0, 1, 1): m2 * (tw + z[0, 1, 1]),
        (1, 1, 1): k3 * z[1, 1, 1],
    }
    fx = {
        (0, 1, 0): p0 + m1x2 * x[0, 1, 0],
        (1, 0, 0): zx,
        (0, 0, 1): xy,
        (1, 1, 0): pz + m1 * x[1, 1, 0],
        (0, 1, 1): py + m1 * x[0, 1, 1],
        (1, 0, 1): m2 * (tw + x[1, 0, 1]),
        (1, 1, 1): k3 * x[1, 1, 1],
    }
    fy = {
        (0, 0, 1): p0 + m1x2 * y[0, 0, 1],
        (1, 0, 0): zy,
        (0, 1, 0): xy,
        (1, 0, 1): pz + m1 * y[1, 0, 1],
        (0, 1, 1): px + m1 * y[0, 1, 1],
        (1, 1, 0): m2 * (tw + y[1, 1, 0]),
        (1, 1, 1): k3 * y[1, 1, 1],
    }
    low, high = [], []
    for f in (fz, fx, fy):
        low_c, high_c = [], []
        for j, k in QUADS:
            d = f[1, j, k]
            if j + k:
                s = f[0, j, k]
                low_c.append(s - d)
                high_c.append(s + d)
            else:
                low_c.append(-d)
                high_c.append(d)
        low.append(low_c)
        high.append(high_c)
    return low, high


def fold_y(a, b):
    return (a - b) + pltpu.roll(a + b, 1, 1)


def column_forces(blocks, layers, zbase, mats, col_lo, col_own, col_lab, col_dt, col_f, col_m):
    rows = col_lab.shape[0]
    shape = (rows, 256)
    zg = iota(shape, 0) + zbase
    gap = layers // 2 * 8 + 3
    ok = (zg >= 0) & (zg <= layers * 8 - 2) & (zg != gap) & (iota(shape, 1) < 255)
    mask = jnp.where(ok & (lax.axis_index("plane") > 0), 1.0, 0.0)
    l1, m1, k3, th, rho = cell_fields(mats, col_lab[...], col_dt[...], mask, col_m is not None)
    lower = [plane_modes(col_lo[c], col_own[c]) for c in range(3)]
    upper = [[pltpu.roll(a, rows - 1, 0) for a in comp] for comp in lower]
    low, high = cell_forces(lower, upper, l1, m1, k3, th)
    for c in range(3):
        node = [low[c][q] + pltpu.roll(high[c][q], 1, 0) for q in range(4)]
        col_f[c] = fold_y(node[0], node[1]) + fold_y(node[2], node[3])
    if col_m is not None:
        rho = rho + pltpu.roll(rho, 1, 1)
        col_m[...] = rho + pltpu.roll(rho, 1, 0)


def elastic_steps(
    blocks, layers, cells, zbase, mats, u, lab, dt, col_hi, col_f, col_m, modes, saved, saved_m, finish
):
    shape = (16, 256)
    row, lane = iota(shape, 0), iota(shape, 1)
    last = jnp.where(lax.axis_index("plane") == blocks - 1, 15, 16)
    in_plane = jnp.where((lane < 255) & (row < last), 1.0, 0.0)
    gap = layers // 2 * 8 + 3
    first_row, last_row = row == 0, row == 15

    def forward(e, c):
        a = u[c, e]
        halo = jnp.broadcast_to(col_hi[c, pl.ds(e, 1), :], shape)
        return plane_modes(a, jnp.where(last_row, halo, pltpu.roll(a, 15, 0)))

    for c in range(3):
        for q, value in enumerate(forward(0, c)):
            modes[4 * c + q] = value

    def body(e, carry):
        zg = zbase + e
        ok = (zg >= 0) & (zg <= layers * 8 - 2) & (zg != gap)
        scale = jnp.where(ok, 1.0, 0.0)
        l1, m1, k3, th, rho = cell_fields(mats, lab[e], dt[e], in_plane * scale, col_m is not None)
        lower = [[modes[4 * c + q] for q in range(4)] for c in range(3)]
        upper = [forward(e + 1, c) for c in range(3)]
        for c in range(3):
            for q in range(4):
                modes[4 * c + q] = upper[c][q]
        low, high = cell_forces(lower, upper, l1, m1, k3, th)
        force = []
        for c in range(3):
            node = [low[c][q] + saved[4 * c + q] for q in range(4)]
            for q in range(4):
                saved[4 * c + q] = high[c][q]
            t0, t1 = fold_y(node[0], node[1]), fold_y(node[2], node[3])
            halo = jnp.broadcast_to(col_f[c, pl.ds(e, 1), :], shape)
            force.append((t0 - t1) + jnp.where(first_row, halo, pltpu.roll(t0 + t1, 1, 0)))
        mass = None
        if col_m is not None:
            rho = rho + pltpu.roll(rho, 1, 1)
            rho = rho + jnp.where(first_row, 0.0, pltpu.roll(rho, 1, 0))
            halo = jnp.broadcast_to(col_m[pl.ds(e, 1), :], shape)
            mass = LUMPED + (rho + saved_m[...]) + jnp.where(first_row, halo, 0.0)
            saved_m[...] = rho
        finish(e, force, mass)
        return carry

    lax.fori_loop(0, cells, body, 0)


def split3(a):
    hi = a.astype(BF16)
    rest = a - hi.astype(F32)
    mid = rest.astype(BF16)
    lo = (rest - mid.astype(F32)).astype(BF16)
    return jnp.concatenate([hi, mid, lo], axis=0)


def join3(a):
    n = a.shape[0] // 3
    return (a[:n] + a[n : 2 * n]) + a[2 * n :]


def one_hots(position):
    pos = position.astype(jnp.int32)
    n = pos.shape[1]
    y, x = pos & 255, pos >> 8
    ohy = jnp.where(iota((256, n), 0) == y, 1.0, 0.0).astype(BF16)
    ohx = jnp.where(iota((16, n), 0) == x, 1.0, 0.0)
    return ohy, ohx


def gather(face, ohy, ohx):
    n = ohx.shape[1]
    rows = join3(jnp.dot(split3(face), ohy, preferred_element_type=F32))
    return jnp.sum(rows.reshape(3, 16, n) * ohx[None], axis=1)


def scatter(values, ohy, ohx):
    n = ohx.shape[1]
    rows = (values[:, None, :] * ohx[None]).reshape(48, n)
    out = lax.dot_general(split3(rows), ohy, (((1,), (1,)), ((), ())), preferred_element_type=F32)
    return join3(out).reshape(3, 16, 256)


def fill_lists(own, near, far, opp, lists):
    sources = {
        NEAR: (near, LISTS), FAR1: (far, MATE_LISTS), OWN: (own, LISTS), FAR2: (far, OWN_LISTS), OPP2: (opp, MATE_LISTS)
    }
    for role, (ref, base) in sources.items():
        cols = slice(128 * role, 128 * role + 128)
        offset = role_offset(role)
        row = LISTS + 4 * (2 + offset)
        for i in range(3):
            line = own[pl.ds(row + i, 1), :]
            for half in (0, 1):
                lists[2 * i + half : 2 * i + half + 1, cols] = line[:, 128 * half : 128 * half + 128]
        row = base + 4 * (2 - offset)
        for i in range(3):
            line = ref[pl.ds(row + i, 1), :]
            for half in (0, 1):
                if i + half:
                    lists[5 + 2 * i + half : 6 + 2 * i + half, cols] = line[:, 128 * half : 128 * half + 128]


def first_step(
    blocks, layers,
    u, v, dt, lab, par, own, near, far, opp, cols, zb, za,
    u1, v1, dtm, out, lists,
    ue, le, de, col_lo, col_own, col_hi, col_lab, col_dt, col_f, col_m, modes, saved, saved_m,
):
    layer = lax.axis_index("layer")
    zbase = layer * 8 - 2
    zeros = jnp.zeros((8, 256), F32)
    for c in range(3):
        for zz in (0, 1):
            row = 16 * (2 * c + zz)
            ue[c, zz] = zb[ZU_U + row : ZU_U + row + 16, :]
            ue[c, 10 + zz] = za[ZD_U + row : ZD_U + row + 16, :]
        ue[c, 2:10] = u[c]
        v1[c, 0] = zb[ZU_V + 16 * c : ZU_V + 16 * c + 16, :]
        v1[c, 9] = za[ZD_V + 16 * c : ZD_V + 16 * c + 16, :]
        v1[c, 1:9] = v[c]
        for col, src, zu, zd in ((col_lo, 0, ZU_CL, ZD_CL), (col_hi, COL_BEYOND, ZU_CH, ZD_CH)):
            col[c, 8:16, :] = zeros
            col[c, 0:2, :] = zb[zu + 2 * c : zu + 2 * c + 2, :]
            col[c, 2:10, :] = cols[src + 8 * c : src + 8 * c + 8, :]
            col[c, 10:12, :] = za[zd + 2 * c : zd + 2 * c + 2, :]
        col_own[c, 8:16, :] = zeros
        col_own[c, 0:8, :] = ue[c, 0:8, 0, :]
        col_own[c, 8:12, :] = ue[c, 8:12, 0, :]
    for zz in (0, 1):
        le[zz] = zb[ZU_LAB + 16 * zz : ZU_LAB + 16 * zz + 16, :]
        de[zz] = zb[ZU_DT + 16 * zz : ZU_DT + 16 * zz + 16, :]
    le[2:10] = lab[...].astype(F32)
    de[2:10] = dt[...]
    le[10] = za[ZD_LAB : ZD_LAB + 16, :]
    de[10] = za[ZD_DT : ZD_DT + 16, :]
    for col, src, zu, zd in ((col_lab, COL_LAB, ZU_CLAB, ZD_CLAB), (col_dt, COL_DT, ZU_CDT, ZD_CDT)):
        col[8:16, :] = zeros
        col[0:2, :] = zb[zu : zu + 2, :]
        col[2:10, :] = cols[src : src + 8, :]
        col[10:11, :] = za[zd : zd + 1, :]

    mats = material_scalars(par)
    column_forces(blocks, layers, zbase, mats, col_lo, col_own, col_lab, col_dt, col_f, col_m)

    def finish(e, force, mass):
        at = jnp.maximum(e - 1, 0)
        rate = DT / mass
        dtm[at] = rate
        for c in range(3):
            speed = v1[c, at] - rate * force[c]
            u1[c, at] = ue[c, e] + DT * speed

            @pl.when(e > 0)
            def _():
                v1[c, at] = speed

    elastic_steps(
        blocks, layers, 11, zbase, mats, ue, le, de, col_hi, col_f, col_m, modes, saved, saved_m, finish
    )

    @pl.when(layer == layers // 2)
    def _():
        fill_lists(own, near, far, opp, lists)
        sol_y, sol_x = one_hots(lists[0:1, :])
        land_y, land_x = one_hots(lists[6:7, :])
        far_y, far_x = one_hots(lists[1:2, :])
        own_pad = own[PAD : PAD + 48, :]
        pads = {
            NEAR: near[PAD : PAD + 48, :],
            FAR1: far[MATE_PAD : MATE_PAD + 48, :],
            OWN: own_pad,
            FAR2: far[OWN_PAD : OWN_PAD + 48, :],
            OPP2: opp[MATE_PAD : MATE_PAD + 48, :],
        }
        far_pad = []
        for role in range(5):
            part = slice(128 * role, 128 * role + 128)
            far_pad.append(gather(pads[role], far_y[:, part], far_x[:, part]))
        on_bump = lists[2:3, :] * (jnp.concatenate(far_pad, axis=1) - lists[3:6, :])
        on_pad = lists[7:8, :] * (lists[8:11, :] - gather(own_pad, land_y, land_x))
        bump_force = scatter(on_bump, sol_y, sol_x)
        pad_force = scatter(on_pad, land_y, land_x)
        for c in range(3):
            for at, extra in ((4, pad_force[c]), (5, bump_force[c])):
                change = dtm[at] * extra
                v1[c, at] = v1[c, at] + change
                u1[c, at] = u1[c, at] + DT * change
        new_pad = jnp.concatenate([u1[c, 4] for c in range(3)], axis=0)
        new_bump = jnp.concatenate([u1[c, 5] for c in range(3)], axis=0)
        lists[3:6, :] = gather(new_bump, sol_y, sol_x)
        lists[8:11, :] = gather(new_pad, land_y, land_x)
        for role in range(5):
            part = slice(128 * role, 128 * role + 128)
            for i, row in enumerate((3, 4, 5, 8, 9, 10)):
                at, half = NEW_VALS + 4 * role + i // 2, i % 2
                out[at : at + 1, 128 * half : 128 * half + 128] = lists[row : row + 1, part]

    for x, row in ((15, NEW_HI), (0, NEW_LO)):
        for c in range(3):
            out[row + 10 * c : row + 10 * c + 8, :] = u1[c, 0:8, x, :]
            out[row + 10 * c + 8 : row + 10 * c + 10, :] = u1[c, 8:10, x, :]


def second_step(
    blocks, layers,
    u, v, dtm, dt, lab, par, lists, cols, zb, own, near, far, opp,
    u2, v2,
    le, de, col_lo, col_own, col_hi, col_lab, col_dt, col_f, modes, saved,
):
    layer = lax.axis_index("layer")
    zbase = layer * 8 - 1
    zeros = jnp.zeros((8, 256), F32)
    even = on_even()
    for c in range(3):
        at, hi, lo = 10 * c, NEW_HI + 10 * c, NEW_LO + 10 * c
        col_lo[c, 8:16, :] = zeros
        col_hi[c, 8:16, :] = zeros
        col_own[c, 8:16, :] = zeros
        col_lo[c, 0:10, :] = jnp.where(even, far[at : at + 10, :], near[hi : hi + 10, :])
        col_hi[c, 0:10, :] = jnp.where(even, near[lo : lo + 10, :], far[at : at + 10, :])
        col_own[c, 0:10, :] = own[lo : lo + 10, :]
    le[0] = zb[ZU_LAB + 16 : ZU_LAB + 32, :]
    de[0] = zb[ZU_DT + 16 : ZU_DT + 32, :]
    le[1:9] = lab[...].astype(F32)
    de[1:9] = dt[...]
    for col, src, zu in ((col_lab, COL_LAB, ZU_CLAB), (col_dt, COL_DT, ZU_CDT)):
        col[8:16, :] = zeros
        col[0:1, :] = zb[zu + 1 : zu + 2, :]
        col[1:9, :] = cols[src : src + 8, :]

    mats = material_scalars(par)
    column_forces(blocks, layers, zbase, mats, col_lo, col_own, col_lab, col_dt, col_f, None)

    def finish(e, force, mass):
        at = jnp.maximum(e - 1, 0)
        rate = dtm[e]
        for c in range(3):
            speed = v[c, e] - rate * force[c]
            v2[c, at] = speed
            u2[c, at] = u[c, e] + DT * speed

    elastic_steps(blocks, layers, 9, zbase, mats, u, le, de, col_hi, col_f, None, modes, saved, None, finish)

    @pl.when(layer == layers // 2)
    def _():
        sol_y, sol_x = one_hots(lists[0:1, :])
        land_y, land_x = one_hots(lists[6:7, :])

        def values(i):
            half = slice(128 * (i % 2), 128 * (i % 2) + 128)
            own_row = (3, 4, 5, 8, 9, 10)[i]
            places = (
                (near, NEW_VALS + 4 * NEAR), (far, CROSS_MATE), None, (far, CROSS_OWN), (opp, CROSS_ON)
            )
            parts = [
                lists[own_row : own_row + 1, 256:384] if place is None
                else place[0][place[1] + i // 2 : place[1] + i // 2 + 1, half]
                for place in places
            ]
            return jnp.concatenate(parts, axis=1)

        far_bump = jnp.concatenate([values(i) for i in range(3)], axis=0)
        far_pad = jnp.concatenate([values(i) for i in range(3, 6)], axis=0)
        on_bump = lists[2:3, :] * (far_pad - lists[3:6, :])
        on_pad = lists[7:8, :] * (far_bump - lists[8:11, :])
        bump_force = scatter(on_bump, sol_y, sol_x)
        pad_force = scatter(on_pad, land_y, land_x)
        for c in range(3):
            for at, extra in ((3, pad_force[c]), (4, bump_force[c])):
                change = dtm[at + 1] * extra
                v2[c, at] = v2[c, at] + change
                u2[c, at] = u2[c, at] + DT * change


VM = pl.BlockSpec(memory_space=pltpu.VMEM)
SM = pl.BlockSpec(memory_space=pltpu.SMEM)
HBM = pl.BlockSpec(memory_space=pltpu.HBM)


def call(kernel, in_specs, outs, scratch, name, flops):
    return pl.pallas_call(
        kernel,
        out_shape=[jax.ShapeDtypeStruct(shape, F32) for shape in outs],
        in_specs=in_specs,
        out_specs=[VM] * len(outs),
        scratch_shapes=[pltpu.VMEM(s, F32) if isinstance(s, tuple) else s for s in scratch],
        compiler_params=pltpu.CompilerParams(vmem_limit_bytes=32 * 1024 * 1024),
        cost_estimate=pl.CostEstimate(flops=flops, bytes_accessed=2_000_000, transcendentals=0),
        name=name,
    )


def local(u, v, dt, lab, par, sol, land, stiff, tally):
    blocks, layers = lax.axis_size("plane"), lax.axis_size("layer")
    swaps = [(s, s ^ 1) for s in range(blocks)]
    crossings = [(s, s + 2 - 4 * (s % 2)) for s in range(blocks) if 0 <= s + 2 - 4 * (s % 2) < blocks]
    face_swaps = [(a * layers + layers // 2, b * layers + layers // 2) for a, b in swaps]

    def along_layer(value, steps):
        pairs = [(s, s + steps) for s in range(layers) if 0 <= s + steps < layers]
        return lax.ppermute(value, "layer", pairs)

    own = call(
        functools.partial(pack_export, blocks, layers),
        [HBM] * 7,
        [(EXPORT_ROWS, 256)],
        [u.shape, dt.shape, pltpu.VMEM(lab.shape, jnp.int32)]
        + [pltpu.VMEM((5, 1, 128), jnp.int32)] * 2
        + [(5, 1, 128), pltpu.SMEM((1, 5), jnp.int32), pltpu.VMEM((8, 640), jnp.int32), pltpu.SemaphoreType.DMA((7,))],
        "pack_export",
        100_000,
    )(u, dt, lab, sol.reshape(5, 1, 128), land.reshape(5, 1, 128), stiff.reshape(5, 1, 128), tally)[0]
    near = lax.ppermute(own, "plane", swaps)
    cross = call(pack_cross, [VM] * 2, [(CROSS_ROWS, 256)], [], "pack_cross", 100_000)(own, near)[0]
    far = lax.ppermute(cross, "plane", crossings)
    up, dn, cols = call(
        pack_layer, [VM] * 6, [(ZU_ROWS, 256), (ZD_ROWS, 256), (COLS_ROWS, 256)], [], "pack_layer", 100_000
    )(u, v, dt, lab, near, far)
    zb, za = along_layer(up, 1), along_layer(dn, -1)
    opp = lax.ppermute(far, ("plane", "layer"), face_swaps)

    col, plane = (3, 16, 256), (16, 256)
    u1, v1, dtm, own, lists = call(
        functools.partial(first_step, blocks, layers),
        [VM] * 4 + [SM] + [VM] * 7,
        [(3, 10, 16, 256), (3, 10, 16, 256), (10, 16, 256), (NEW_ROWS, 256), (16, 640)],
        [(3, 12, 16, 256), (11, 16, 256), (11, 16, 256), col, col, col, plane, plane, col, plane]
        + [(12, 16, 256), (12, 16, 256), plane],
        "first_step",
        50_000_000,
    )(u, v, dt, lab, par, own, near, far, opp, cols, zb, za)
    near = lax.ppermute(own, "plane", swaps)
    cross = call(pack_new_cross, [VM] * 2, [(NEW_CROSS_ROWS, 256)], [], "pack_new_cross", 100_000)(own, near)[0]
    far = lax.ppermute(cross, "plane", crossings)
    opp = lax.ppermute(far, ("plane", "layer"), face_swaps)
    return tuple(
        call(
            functools.partial(second_step, blocks, layers),
            [VM] * 5 + [SM] + [VM] * 7,
            [(3, 8, 16, 256), (3, 8, 16, 256)],
            [(9, 16, 256), (9, 16, 256), col, col, col, plane, plane, col] + [(12, 16, 256), (12, 16, 256)],
            "second_step",
            50_000_000,
        )(u1, v1, dtm, dt, lab, par, lists, cols, zb, own, near, far, opp)
    )


def solution(mesh):
    in_specs = (
        P(None, "layer", "plane", None),
        P(None, "layer", "plane", None),
        P("layer", "plane", None),
        P("layer", "plane", None),
        P(),
        P("plane", None, None),
        P("plane", None, None),
        P("plane", None, None),
        P("plane", None),
    )
    out_specs = (P(None, "layer", "plane", None), P(None, "layer", "plane", None))
    return jax.shard_map(local, mesh=mesh, in_specs=in_specs, out_specs=out_specs, check_vma=False)
```

```python
import functools

import jax
import jax.numpy as jnp
from jax import lax
from jax.experimental import pallas as pl
from jax.experimental.pallas import tpu as pltpu
from jax.sharding import PartitionSpec as P

DT = 0.05
LUMPED = 0.25
F32 = jnp.float32
BF16 = jnp.bfloat16
QUADS = ((0, 0), (0, 1), (1, 0), (1, 1))

COL_HI, COL_LO, LISTS, PAD, EXPORT_ROWS = 0, 40, 64, 88, 136
OWN_LISTS, MATE_LISTS, OWN_PAD, MATE_PAD, CROSS_ROWS = 40, 64, 88, 136, 184
COL_LAB, COL_DT, COL_BEYOND, COLS_ROWS = 24, 32, 40, 64
ZU_U, ZU_V, ZU_LAB, ZU_DT, ZU_CL, ZU_CH, ZU_CLAB, ZU_CDT, ZU_ROWS = 0, 96, 144, 176, 208, 214, 220, 222, 224
ZD_U, ZD_V, ZD_LAB, ZD_DT, ZD_CL, ZD_CH, ZD_CLAB, ZD_CDT, ZD_ROWS = 0, 96, 144, 160, 176, 182, 188, 189, 192
NEW_HI, NEW_LO, NEW_VALS, NEW_ROWS = 0, 32, 64, 88
CROSS_OWN, CROSS_MATE, CROSS_ON, NEW_CROSS_ROWS = 32, 36, 40, 48
NEAR, FAR1, OWN, FAR2, OPP2 = range(5)
OFFSETS = (1, -1, 0, -2, 2)


def iota(shape, dim):
    return lax.broadcasted_iota(jnp.int32, shape, dim)


def on_even():
    return lax.rem(lax.axis_index("plane"), 2) == 0


def role_offset(role):
    return jnp.where(on_even(), OFFSETS[role], -OFFSETS[role])


def pack_export(
    blocks, layers,
    u_hbm, dt_hbm, lab_hbm, sol_hbm, land_hbm, stiff_hbm, tally_hbm,
    out,
    u, dt, lab, sol, land, stiff, tally, pos, ohy, ohx, sems,
):
    copies = [
        pltpu.make_async_copy(src, dst, sems.at[i])
        for i, (src, dst) in enumerate(
            (
                (u_hbm, u), (dt_hbm, dt), (lab_hbm, lab), (sol_hbm, sol),
                (land_hbm, land), (stiff_hbm, stiff), (tally_hbm, tally),
            )
        )
    ]
    for copy in copies:
        copy.start()
    for copy in copies[3:]:
        copy.wait()
    pad_z = u.shape[1] // 2 - 1
    here = lax.axis_index("plane")
    on_face = lax.axis_index("layer") == layers // 2

    @pl.when(on_face)
    def _():
        out[LISTS : LISTS + 24, :] = jnp.zeros((24, 256), F32)
        for k in range(5):
            row = LISTS + 4 * k
            target = here + (k - 2)
            count = jnp.where((target >= 0) & (target < blocks), tally[0, k], 0)
            live = iota((1, 128), 1) < count
            out[row : row + 1, 0:128] = sol[k].astype(F32)
            out[row : row + 1, 128:256] = land[k].astype(F32)
            out[row + 1 : row + 2, 0:128] = jnp.where(live, stiff[k], 0.0)
            pos[0:1, 128 * k : 128 * k + 128] = sol[k]
        ohy[...], ohx[...] = one_hots(pos[0:1, :])

    for copy in copies[:3]:
        copy.wait()
    for x, row in ((15, COL_HI), (0, COL_LO)):
        for c in range(3):
            out[row + 8 * c : row + 8 * c + 8, :] = u[c, :, x, :]
    out[COL_HI + COL_LAB : COL_HI + COL_LAB + 8, :] = lab[:, 15, :].astype(F32)
    out[COL_HI + COL_DT : COL_HI + COL_DT + 8, :] = dt[:, 15, :]

    @pl.when(on_face)
    def _():
        bump = gather(jnp.concatenate([u[c, pad_z + 1] for c in range(3)], axis=0), ohy[...], ohx[...])
        for k in range(5):
            row, cols = LISTS + 4 * k, slice(128 * k, 128 * k + 128)
            out[row + 1 : row + 2, 128:256] = bump[0:1, cols]
            out[row + 2 : row + 3, 0:128] = bump[1:2, cols]
            out[row + 2 : row + 3, 128:256] = bump[2:3, cols]
        for c in range(3):
            out[PAD + 16 * c : PAD + 16 * c + 16, :] = u[c, pad_z]


def stage(src, dst, sem):
    copy = pltpu.make_async_copy(src, dst, sem)
    copy.start()
    copy.wait()


def pack_cross(own, mate, out):
    out[24:40, :] = mate[COL_HI + 24 : COL_HI + 40, :]
    out[0:24, :] = jnp.where(on_even(), mate[COL_HI : COL_HI + 24, :], mate[COL_LO : COL_LO + 24, :])
    out[OWN_LISTS : OWN_LISTS + 24, :] = own[LISTS : LISTS + 24, :]
    out[MATE_LISTS : MATE_LISTS + 24, :] = mate[LISTS : LISTS + 24, :]
    out[OWN_PAD : OWN_PAD + 48, :] = own[PAD : PAD + 48, :]
    out[MATE_PAD : MATE_PAD + 48, :] = mate[PAD : PAD + 48, :]


def pack_new_cross(own, mate, out):
    out[0:32, :] = jnp.where(on_even(), mate[NEW_HI : NEW_HI + 32, :], mate[NEW_LO : NEW_LO + 32, :])
    for row, src, role in ((CROSS_OWN, own, OPP2), (CROSS_MATE, mate, FAR1), (CROSS_ON, mate, FAR2)):
        out[row : row + 4, :] = src[NEW_VALS + 4 * role : NEW_VALS + 4 * role + 4, :]
    out[44:48, :] = jnp.zeros((4, 256), F32)


def pack_layer(u, v, dt, lab, near, far, up, dn, cols):
    even = on_even()
    cols[0:40, :] = jnp.where(even, far[0:40, :], near[COL_HI : COL_HI + 40, :])
    cols[COL_BEYOND : COL_BEYOND + 24, :] = jnp.where(even, near[COL_LO : COL_LO + 24, :], far[0:24, :])
    for c in range(3):
        for zz in (0, 1):
            row = 16 * (2 * c + zz)
            up[ZU_U + row : ZU_U + row + 16, :] = u[c, 6 + zz]
            dn[ZD_U + row : ZD_U + row + 16, :] = u[c, zz]
        up[ZU_V + 16 * c : ZU_V + 16 * c + 16, :] = v[c, 7]
        dn[ZD_V + 16 * c : ZD_V + 16 * c + 16, :] = v[c, 0]
        lo, hi = 8 * c, COL_BEYOND + 8 * c
        up[ZU_CL + 2 * c : ZU_CL + 2 * c + 2, :] = cols[lo + 6 : lo + 8, :]
        up[ZU_CH + 2 * c : ZU_CH + 2 * c + 2, :] = cols[hi + 6 : hi + 8, :]
        dn[ZD_CL + 2 * c : ZD_CL + 2 * c + 2, :] = cols[lo : lo + 2, :]
        dn[ZD_CH + 2 * c : ZD_CH + 2 * c + 2, :] = cols[hi : hi + 2, :]
    for zz in (0, 1):
        up[ZU_LAB + 16 * zz : ZU_LAB + 16 * zz + 16, :] = lab[6 + zz].astype(F32)
        up[ZU_DT + 16 * zz : ZU_DT + 16 * zz + 16, :] = dt[6 + zz]
    up[ZU_CLAB : ZU_CLAB + 2, :] = cols[COL_LAB + 6 : COL_LAB + 8, :]
    up[ZU_CDT : ZU_CDT + 2, :] = cols[COL_DT + 6 : COL_DT + 8, :]
    dn[ZD_LAB : ZD_LAB + 16, :] = lab[0].astype(F32)
    dn[ZD_DT : ZD_DT + 16, :] = dt[0]
    dn[ZD_CLAB : ZD_CLAB + 1, :] = cols[COL_LAB : COL_LAB + 1, :]
    dn[ZD_CDT : ZD_CDT + 1, :] = cols[COL_DT : COL_DT + 1, :]
    dn[ZD_CDT + 1 : ZD_ROWS, :] = jnp.zeros((ZD_ROWS - ZD_CDT - 1, 256), F32)


def material_scalars(par):
    out = []
    for m in range(4):
        lam, mu, alpha, rho = par[0, m], par[1, m], par[2, m], par[3, m]
        out.append(
            (
                lam * (1.0 / 16.0),
                mu * (1.0 / 16.0),
                (lam + 4.0 * mu) * (1.0 / 144.0),
                (3.0 * lam + 2.0 * mu) * alpha * 0.25,
                rho * 0.125,
            )
        )
    return out


def cell_fields(mats, lab, dt, mask, with_mass):
    is0, is1, is2 = lab == 0.0, lab == 1.0, lab == 2.0

    def pick(i):
        rest = jnp.where(is2, mats[2][i], mats[3][i])
        return jnp.where(is0, mats[0][i], jnp.where(is1, mats[1][i], rest)) * mask

    return pick(0), pick(1), pick(2), pick(3) * dt, pick(4) if with_mass else None


def plane_modes(u, ux):
    s, d = u + ux, ux - u
    sy, dy = pltpu.roll(s, 255, 1), pltpu.roll(d, 255, 1)
    return [s + sy, sy - s, d + dy, dy - d]


def cell_forces(lower, upper, l1, m1, k3, th):
    z, x, y = (
        {
            (i, j, k): (upper[c][q] - lower[c][q]) if i else (upper[c][q] + lower[c][q])
            for q, (j, k) in enumerate(QUADS)
            for i in (0, 1)
            if i + j + k
        }
        for c in range(3)
    )
    l2, m2 = l1 * (1.0 / 3.0), m1 * (1.0 / 3.0)
    p0 = l1 * (z[1, 0, 0] + x[0, 1, 0] + y[0, 0, 1]) - th
    m1x2 = m1 + m1
    zx = m1 * (x[1, 0, 0] + z[0, 1, 0])
    zy = m1 * (y[1, 0, 0] + z[0, 0, 1])
    xy = m1 * (y[0, 1, 0] + x[0, 0, 1])
    pz = l2 * (x[1, 1, 0] + y[1, 0, 1])
    px = l2 * (z[1, 1, 0] + y[0, 1, 1])
    py = l2 * (z[1, 0, 1] + x[0, 1, 1])
    tw = z[0, 1, 1] + x[1, 0, 1] + y[1, 1, 0]
    fz = {
        (1, 0, 0): p0 + m1x2 * z[1, 0, 0],
        (0, 1, 0): zx,
        (0, 0, 1): zy,
        (1, 1, 0): px + m1 * z[1, 1, 0],
        (1, 0, 1): py + m1 * z[1, 0, 1],
        (0, 1, 1): m2 * (tw + z[0, 1, 1]),
        (1, 1, 1): k3 * z[1, 1, 1],
    }
    fx = {
        (0, 1, 0): p0 + m1x2 * x[0, 1, 0],
        (1, 0, 0): zx,
        (0, 0, 1): xy,
        (1, 1, 0): pz + m1 * x[1, 1, 0],
        (0, 1, 1): py + m1 * x[0, 1, 1],
        (1, 0, 1): m2 * (tw + x[1, 0, 1]),
        (1, 1, 1): k3 * x[1, 1, 1],
    }
    fy = {
        (0, 0, 1): p0 + m1x2 * y[0, 0, 1],
        (1, 0, 0): zy,
        (0, 1, 0): xy,
        (1, 0, 1): pz + m1 * y[1, 0, 1],
        (0, 1, 1): px + m1 * y[0, 1, 1],
        (1, 1, 0): m2 * (tw + y[1, 1, 0]),
        (1, 1, 1): k3 * y[1, 1, 1],
    }
    low, high = [], []
    for f in (fz, fx, fy):
        low_c, high_c = [], []
        for j, k in QUADS:
            d = f[1, j, k]
            if j + k:
                s = f[0, j, k]
                low_c.append(s - d)
                high_c.append(s + d)
            else:
                low_c.append(-d)
                high_c.append(d)
        low.append(low_c)
        high.append(high_c)
    return low, high


def fold_y(a, b):
    return (a - b) + pltpu.roll(a + b, 1, 1)


def column_forces(layers, zbase, mats, inside, side, left, right, lab, dt, with_mass):
    rows = lab.shape[0]
    shape = (rows, 256)
    zg = iota(shape, 0) + zbase
    ok = (zg >= 0) & (zg <= layers * 8 - 2) & (zg != layers // 2 * 8 + 3) & (iota(shape, 1) < 255)
    mask = jnp.where(ok & inside, 1.0, 0.0)
    l1, m1, k3, th, rho = cell_fields(mats, lab, dt, mask, with_mass)
    lower = [plane_modes(left[c], right[c]) for c in range(3)]
    upper = [[pltpu.roll(a, rows - 1, 0) for a in comp] for comp in lower]
    low, high = cell_forces(lower, upper, l1, m1, k3, th)
    forces = []
    for c in range(3):
        node = [low[c][q] + pltpu.roll(high[c][q], 1, 0) for q in range(4)]
        t0, t1 = fold_y(node[0], node[1]), fold_y(node[2], node[3])
        forces.append(t0 + t1 if side > 0 else t0 - t1)
    if with_mass:
        rho = rho + pltpu.roll(rho, 1, 1)
        rho = rho + pltpu.roll(rho, 1, 0)
    return forces, rho


def block_forces(layers, cells, zbase, mats, u, lab, dt, modes, saved, saved_m, force, mass):
    shape = (16, 256)
    row, lane = iota(shape, 0), iota(shape, 1)
    in_plane = jnp.where((lane < 255) & (row < 15), 1.0, 0.0)

    def forward(e, c):
        a = u[c, e]
        return plane_modes(a, pltpu.roll(a, 15, 0))

    for c in range(3):
        for q, value in enumerate(forward(0, c)):
            modes[4 * c + q] = value
            saved[4 * c + q] = jnp.zeros(shape, F32)
    if mass is not None:
        saved_m[...] = jnp.zeros(shape, F32)

    def fold(e, node):
        for c in range(3):
            t0, t1 = fold_y(node[c][0], node[c][1]), fold_y(node[c][2], node[c][3])
            force[c, e] = (t0 - t1) + pltpu.roll(t0 + t1, 1, 0)

    def body(e, carry):
        zg = zbase + e
        ok = (zg >= 0) & (zg <= layers * 8 - 2) & (zg != layers // 2 * 8 + 3)
        mask = in_plane * jnp.where(ok, 1.0, 0.0)
        l1, m1, k3, th, rho = cell_fields(mats, lab[e].astype(F32), dt[e], mask, mass is not None)
        lower = [[modes[4 * c + q] for q in range(4)] for c in range(3)]
        upper = [forward(e + 1, c) for c in range(3)]
        for c in range(3):
            for q in range(4):
                modes[4 * c + q] = upper[c][q]
        low, high = cell_forces(lower, upper, l1, m1, k3, th)
        fold(e, [[low[c][q] + saved[4 * c + q] for q in range(4)] for c in range(3)])
        for c in range(3):
            for q in range(4):
                saved[4 * c + q] = high[c][q]
        if mass is not None:
            rho = rho + pltpu.roll(rho, 1, 1)
            rho = rho + pltpu.roll(rho, 1, 0)
            mass[e] = rho + saved_m[...]
            saved_m[...] = rho
        return carry

    lax.fori_loop(0, cells, body, 0)
    fold(cells, [[saved[4 * c + q] for q in range(4)] for c in range(3)])
    if mass is not None:
        mass[cells] = saved_m[...]


def with_columns(a, first, last):
    row = iota((8, 256), 0)
    top = a[0:8] + jnp.where(row == 0, jnp.broadcast_to(first, (8, 256)), 0.0)
    bottom = a[8:16] + jnp.where(row == 7, jnp.broadcast_to(last, (8, 256)), 0.0)
    return jnp.concatenate([top, bottom], axis=0)


def split3(a):
    hi = a.astype(BF16)
    rest = a - hi.astype(F32)
    mid = rest.astype(BF16)
    lo = (rest - mid.astype(F32)).astype(BF16)
    return jnp.concatenate([hi, mid, lo], axis=0)


def join3(a):
    n = a.shape[0] // 3
    return (a[:n] + a[n : 2 * n]) + a[2 * n :]


def one_hots(position):
    pos = position.astype(jnp.int32)
    n = pos.shape[1]
    y, x = pos & 255, pos >> 8
    ohy = jnp.where(iota((256, n), 0) == y, 1.0, 0.0).astype(BF16)
    ohx = jnp.where(iota((16, n), 0) == x, 1.0, 0.0)
    return ohy, ohx


def gather(face, ohy, ohx):
    n = ohx.shape[1]
    rows = join3(jnp.dot(split3(face), ohy, preferred_element_type=F32))
    return jnp.sum(rows.reshape(3, 16, n) * ohx[None], axis=1)


def scatter(values, ohy, ohx):
    n = ohx.shape[1]
    rows = (values[:, None, :] * ohx[None]).reshape(48, n)
    out = lax.dot_general(split3(rows), ohy, (((1,), (1,)), ((), ())), preferred_element_type=F32)
    return join3(out).reshape(3, 16, 256)


def fill_lists(own, near, far, opp, lists):
    sources = {
        NEAR: (near, LISTS), FAR1: (far, MATE_LISTS), OWN: (own, LISTS), FAR2: (far, OWN_LISTS), OPP2: (opp, MATE_LISTS)
    }
    for role, (ref, base) in sources.items():
        cols = slice(128 * role, 128 * role + 128)
        offset = role_offset(role)
        row = LISTS + 4 * (2 + offset)
        for i in range(3):
            line = own[pl.ds(row + i, 1), :]
            for half in (0, 1):
                lists[2 * i + half : 2 * i + half + 1, cols] = line[:, 128 * half : 128 * half + 128]
        row = base + 4 * (2 - offset)
        for i in range(3):
            line = ref[pl.ds(row + i, 1), :]
            for half in (0, 1):
                if i + half:
                    lists[5 + 2 * i + half : 6 + 2 * i + half, cols] = line[:, 128 * half : 128 * half + 128]


def first_block(layers, u, dt, lab, par, force, mass, modes, saved, saved_m):
    zbase = lax.axis_index("layer") * 8
    block_forces(layers, 7, zbase, material_scalars(par), u, lab, dt, modes, saved, saved_m, force, mass)


def first_contact(layers, own, near, far, opp, contact, lists):
    @pl.when(lax.axis_index("layer") == layers // 2)
    def _():
        fill_lists(own, near, far, opp, lists)
        sol_y, sol_x = one_hots(lists[0:1, :])
        land_y, land_x = one_hots(lists[6:7, :])
        far_y, far_x = one_hots(lists[1:2, :])
        own_pad = own[PAD : PAD + 48, :]
        pads = {
            NEAR: near[PAD : PAD + 48, :],
            FAR1: far[MATE_PAD : MATE_PAD + 48, :],
            OWN: own_pad,
            FAR2: far[OWN_PAD : OWN_PAD + 48, :],
            OPP2: opp[MATE_PAD : MATE_PAD + 48, :],
        }
        far_pad = []
        for role in range(5):
            part = slice(128 * role, 128 * role + 128)
            far_pad.append(gather(pads[role], far_y[:, part], far_x[:, part]))
        on_bump = lists[2:3, :] * (jnp.concatenate(far_pad, axis=1) - lists[3:6, :])
        on_pad = lists[7:8, :] * (lists[8:11, :] - gather(own_pad, land_y, land_x))
        contact[0] = scatter(on_pad, land_y, land_x)
        contact[1] = scatter(on_bump, sol_y, sol_x)


def first_step(
    blocks, layers,
    u, v, dt, lab, par, own, cols, zb, za, force, mass, contact, lists_in,
    u1, v1, dtm, out, lists,
    ul, uu, ll, dl, lu, du, fl, ml, fu, mu, col, col_lab, col_dt, col_f, col_m, modes, saved, saved_m,
):
    layer, here = lax.axis_index("layer"), lax.axis_index("plane")
    zeros = jnp.zeros((8, 256), F32)
    mats = material_scalars(par)
    for c in range(3):
        ul[c, 2], uu[c, 0] = u[c, 0], u[c, 7]
        for zz in (0, 1):
            row = 16 * (2 * c + zz)
            ul[c, zz] = zb[ZU_U + row : ZU_U + row + 16, :]
            uu[c, 1 + zz] = za[ZD_U + row : ZD_U + row + 16, :]
        for at, src, first, zu, zd in ((0, cols, 0, ZU_CL, ZD_CL), (3, cols, COL_BEYOND, ZU_CH, ZD_CH)):
            col[at, c, 8:16, :] = zeros
            col[at, c, 0:2, :] = zb[zu + 2 * c : zu + 2 * c + 2, :]
            col[at, c, 2:10, :] = src[first + 8 * c : first + 8 * c + 8, :]
            col[at, c, 10:12, :] = za[zd + 2 * c : zd + 2 * c + 2, :]
        for at, first, x in ((1, COL_LO, 0), (2, COL_HI, 15)):
            col[at, c, 8:16, :] = zeros
            col[at, c, 2:10, :] = own[first + 8 * c : first + 8 * c + 8, :]
            for zz in (0, 1):
                row = 16 * (2 * c + zz) + x
                col[at, c, zz : zz + 1, :] = zb[ZU_U + row : ZU_U + row + 1, :]
                col[at, c, 10 + zz : 11 + zz, :] = za[ZD_U + row : ZD_U + row + 1, :]
    for zz in (0, 1):
        ll[zz] = zb[ZU_LAB + 16 * zz : ZU_LAB + 16 * zz + 16, :]
        dl[zz] = zb[ZU_DT + 16 * zz : ZU_DT + 16 * zz + 16, :]
    lu[0], du[0] = lab[7].astype(F32), dt[7]
    lu[1], du[1] = za[ZD_LAB : ZD_LAB + 16, :], za[ZD_DT : ZD_DT + 16, :]
    for ref, first, zu, zd, zuf, zdf in (
        (col_lab, COL_LAB, ZU_CLAB, ZD_CLAB, ZU_LAB, ZD_LAB),
        (col_dt, COL_DT, ZU_CDT, ZD_CDT, ZU_DT, ZD_DT),
    ):
        for at in (0, 1):
            ref[at, 8:16, :] = zeros
        ref[0, 0:2, :] = zb[zu : zu + 2, :]
        ref[0, 2:10, :] = cols[first : first + 8, :]
        ref[0, 10:11, :] = za[zd : zd + 1, :]
        for zz in (0, 1):
            ref[1, zz : zz + 1, :] = zb[zuf + 16 * zz + 15 : zuf + 16 * zz + 16, :]
        ref[1, 2:10, :] = own[COL_HI + first : COL_HI + first + 8, :]
        ref[1, 10:11, :] = za[zdf + 15 : zdf + 16, :]

    zbase = layer * 8 - 2
    block_forces(layers, 2, zbase, mats, ul, ll, dl, modes, saved, saved_m, fl, ml)
    block_forces(layers, 2, zbase + 9, mats, uu, lu, du, modes, saved, saved_m, fu, mu)
    for at, inside, side in ((0, here > 0, 1), (1, here < blocks - 1, -1)):
        left = [col[2 * at, c] for c in range(3)]
        right = [col[2 * at + 1, c] for c in range(3)]
        forces, rho = column_forces(
            layers, zbase, mats, inside, side, left, right, col_lab[at], col_dt[at], True
        )
        for c in range(3):
            col_f[at, c] = forces[c]
        col_m[at] = rho

    for i in range(10):
        z, e = i - 1, i + 1
        total = mass[z] if 0 <= z < 8 else 0.0
        if z < 1:
            total = total + ml[e]
        if z > 6:
            total = total + mu[z - 7]
        total = LUMPED + with_columns(total, col_m[0, e : e + 1, :], col_m[1, e : e + 1, :])
        rate = DT / total
        dtm[i] = rate
        for c in range(3):
            pull = force[c, z] if 0 <= z < 8 else 0.0
            if z < 1:
                pull = pull + fl[c, e]
            if z > 6:
                pull = pull + fu[c, z - 7]
            pull = with_columns(pull, col_f[0, c, e : e + 1, :], col_f[1, c, e : e + 1, :])
            if z < 0:
                speed, place = zb[ZU_V + 16 * c : ZU_V + 16 * c + 16, :], ul[c, 1]
            elif z > 7:
                speed, place = za[ZD_V + 16 * c : ZD_V + 16 * c + 16, :], uu[c, 1]
            else:
                speed, place = v[c, z], u[c, z]
            speed = speed - rate * pull
            v1[c, i] = speed
            u1[c, i] = place + DT * speed

    @pl.when(layer == layers // 2)
    def _():
        for c in range(3):
            for face in (0, 1):
                at = 4 + face
                change = dtm[at] * contact[face, c]
                v1[c, at] = v1[c, at] + change
                u1[c, at] = u1[c, at] + DT * change
        lists[...] = lists_in[...]
        new_pad = jnp.concatenate([u1[c, 4] for c in range(3)], axis=0)
        new_bump = jnp.concatenate([u1[c, 5] for c in range(3)], axis=0)
        lists[3:6, :] = gather(new_bump, *one_hots(lists[0:1, :]))
        lists[8:11, :] = gather(new_pad, *one_hots(lists[6:7, :]))
        for role in range(5):
            part = slice(128 * role, 128 * role + 128)
            for i, row in enumerate((3, 4, 5, 8, 9, 10)):
                at, half = NEW_VALS + 4 * role + i // 2, i % 2
                out[at : at + 1, 128 * half : 128 * half + 128] = lists[row : row + 1, part]

    for x, row in ((15, NEW_HI), (0, NEW_LO)):
        for c in range(3):
            out[row + 10 * c : row + 10 * c + 8, :] = u1[c, 0:8, x, :]
            out[row + 10 * c + 8 : row + 10 * c + 10, :] = u1[c, 8:10, x, :]


def second_block(layers, u, dt, lab, par, zb, force, le, de, modes, saved):
    le[0] = zb[ZU_LAB + 16 : ZU_LAB + 32, :]
    de[0] = zb[ZU_DT + 16 : ZU_DT + 32, :]
    le[1:9] = lab[...].astype(F32)
    de[1:9] = dt[...]
    zbase = lax.axis_index("layer") * 8 - 1
    block_forces(layers, 9, zbase, material_scalars(par), u, le, de, modes, saved, None, force, None)


def second_step(
    blocks, layers,
    u, v, dtm, dt, lab, par, force, cols, zb, own, near, far,
    u2, v2,
    col, col_lab, col_dt, col_f,
):
    layer, here = lax.axis_index("layer"), lax.axis_index("plane")
    zeros = jnp.zeros((8, 256), F32)
    mats = material_scalars(par)
    even = on_even()
    for c in range(3):
        at, hi, lo = 10 * c, NEW_HI + 10 * c, NEW_LO + 10 * c
        for i in range(4):
            col[i, c, 8:16, :] = zeros
        col[0, c, 0:10, :] = jnp.where(even, far[at : at + 10, :], near[hi : hi + 10, :])
        col[1, c, 0:10, :] = own[lo : lo + 10, :]
        col[2, c, 0:10, :] = own[hi : hi + 10, :]
        col[3, c, 0:10, :] = jnp.where(even, near[lo : lo + 10, :], far[at : at + 10, :])
    for ref, src, first, zu, zuf in (
        (col_lab, lab, COL_LAB, ZU_CLAB, ZU_LAB),
        (col_dt, dt, COL_DT, ZU_CDT, ZU_DT),
    ):
        for at in (0, 1):
            ref[at, 8:16, :] = zeros
        ref[0, 0:1, :] = zb[zu + 1 : zu + 2, :]
        ref[0, 1:9, :] = cols[first : first + 8, :]
        ref[1, 0:1, :] = zb[zuf + 31 : zuf + 32, :]
        ref[1, 1:9, :] = src[:, 15, :].astype(F32)
    for at, inside, side in ((0, here > 0, 1), (1, here < blocks - 1, -1)):
        left = [col[2 * at, c] for c in range(3)]
        right = [col[2 * at + 1, c] for c in range(3)]
        forces, _ = column_forces(
            layers, layer * 8 - 1, mats, inside, side, left, right, col_lab[at], col_dt[at], False
        )
        for c in range(3):
            col_f[at, c] = forces[c]
    for z in range(8):
        e = z + 1
        rate = dtm[e]
        for c in range(3):
            pull = with_columns(force[c, e], col_f[0, c, e : e + 1, :], col_f[1, c, e : e + 1, :])
            speed = v[c, e] - rate * pull
            v2[c, z] = speed
            u2[c, z] = u[c, e] + DT * speed


def second_contact(layers, u, v, dtm, lists, near, far, opp, u2, v2, faces, sems):
    copies = []
    for i, (src, dst) in enumerate(((u, u2), (v, v2))):
        for first, last in ((0, 3), (5, 8)):
            copies.append(
                pltpu.make_async_copy(src.at[:, first:last], dst.at[:, first:last], sems.at[len(copies)])
            )
    for copy in copies:
        copy.start()
    for c in range(3):
        for face in (0, 1):
            faces[0, c, face] = u[c, 3 + face]
            faces[1, c, face] = v[c, 3 + face]

    @pl.when(lax.axis_index("layer") == layers // 2)
    def _():
        sol_y, sol_x = one_hots(lists[0:1, :])
        land_y, land_x = one_hots(lists[6:7, :])

        def values(i):
            half = slice(128 * (i % 2), 128 * (i % 2) + 128)
            own_row = (3, 4, 5, 8, 9, 10)[i]
            places = (
                (near, NEW_VALS + 4 * NEAR), (far, CROSS_MATE), None, (far, CROSS_OWN), (opp, CROSS_ON)
            )
            parts = [
                lists[own_row : own_row + 1, 256:384] if place is None
                else place[0][place[1] + i // 2 : place[1] + i // 2 + 1, half]
                for place in places
            ]
            return jnp.concatenate(parts, axis=1)

        far_bump = jnp.concatenate([values(i) for i in range(3)], axis=0)
        far_pad = jnp.concatenate([values(i) for i in range(3, 6)], axis=0)
        on_bump = lists[2:3, :] * (far_pad - lists[3:6, :])
        on_pad = lists[7:8, :] * (far_bump - lists[8:11, :])
        extra = (scatter(on_pad, land_y, land_x), scatter(on_bump, sol_y, sol_x))
        for c in range(3):
            for face in (0, 1):
                change = dtm[4 + face] * extra[face][c]
                faces[0, c, face] = faces[0, c, face] + DT * change
                faces[1, c, face] = faces[1, c, face] + change

    for i, dst in enumerate((u2, v2)):
        copy = pltpu.make_async_copy(faces.at[i], dst.at[:, 3:5], sems.at[4 + i])
        copy.start()
        copies.append(copy)
    for copy in copies:
        copy.wait()


VM = pl.BlockSpec(memory_space=pltpu.VMEM)
SM = pl.BlockSpec(memory_space=pltpu.SMEM)
HBM = pl.BlockSpec(memory_space=pltpu.HBM)


def call(kernel, in_specs, outs, scratch, name, flops, vmem=32, out_spec=VM):
    return pl.pallas_call(
        kernel,
        out_shape=[jax.ShapeDtypeStruct(shape, F32) for shape in outs],
        in_specs=in_specs,
        out_specs=[out_spec] * len(outs),
        scratch_shapes=[pltpu.VMEM(s, F32) if isinstance(s, tuple) else s for s in scratch],
        compiler_params=pltpu.CompilerParams(vmem_limit_bytes=vmem * 1024 * 1024),
        cost_estimate=pl.CostEstimate(flops=flops, bytes_accessed=2_000_000, transcendentals=0),
        name=name,
    )


def local(u, v, dt, lab, par, sol, land, stiff, tally):
    blocks, layers = lax.axis_size("plane"), lax.axis_size("layer")
    swaps = [(s, s ^ 1) for s in range(blocks)]
    crossings = [(s, s + 2 - 4 * (s % 2)) for s in range(blocks) if 0 <= s + 2 - 4 * (s % 2) < blocks]
    face_swaps = [(a * layers + layers // 2, b * layers + layers // 2) for a, b in swaps]

    def along_layer(value, steps):
        pairs = [(s, s + steps) for s in range(layers) if 0 <= s + steps < layers]
        return lax.ppermute(value, "layer", pairs)

    own = call(
        functools.partial(pack_export, blocks, layers),
        [HBM] * 7,
        [(EXPORT_ROWS, 256)],
        [u.shape, dt.shape, pltpu.VMEM(lab.shape, jnp.int32)]
        + [pltpu.VMEM((5, 1, 128), jnp.int32)] * 2
        + [(5, 1, 128), pltpu.SMEM((1, 5), jnp.int32), pltpu.VMEM((8, 640), jnp.int32)]
        + [pltpu.VMEM((256, 640), BF16), (16, 640), pltpu.SemaphoreType.DMA((7,))],
        "pack_export",
        100_000,
        63,
    )(u, dt, lab, sol.reshape(5, 1, 128), land.reshape(5, 1, 128), stiff.reshape(5, 1, 128), tally)[0]
    near = lax.ppermute(own, "plane", swaps)
    own = call(stage, [HBM], [own.shape], [pltpu.SemaphoreType.DMA], "stage", 100_000)(own)[0]
    cross = call(pack_cross, [VM] * 2, [(CROSS_ROWS, 256)], [], "pack_cross", 100_000)(own, near)[0]
    far = lax.ppermute(cross, "plane", crossings)
    modes = [(12, 16, 256), (12, 16, 256)]
    plane = (16, 256)
    force, mass = call(
        functools.partial(first_block, layers),
        [VM] * 3 + [SM],
        [(3, 8, 16, 256), (8, 16, 256)],
        modes + [plane],
        "first_block",
        50_000_000,
    )(u, dt, lab, par)
    far, force, mass = lax.optimization_barrier((far, force, mass))
    up, dn, cols = call(
        pack_layer, [VM] * 6, [(ZU_ROWS, 256), (ZD_ROWS, 256), (COLS_ROWS, 256)], [], "pack_layer", 100_000
    )(u, v, dt, lab, near, far)
    zb, za = along_layer(up, 1), along_layer(dn, -1)
    opp = lax.ppermute(far, ("plane", "layer"), face_swaps)
    contact, lists = call(
        functools.partial(first_contact, layers),
        [VM] * 4,
        [(2, 3, 16, 256), (16, 640)],
        [],
        "first_contact",
        10_000_000,
    )(own, near, far, opp)

    three, two = [(3, 3, 16, 256)] * 2 + [(2, 16, 256)] * 4, (2, 16, 256)
    u1, v1, dtm, own, lists = call(
        functools.partial(first_step, blocks, layers),
        [VM] * 4 + [SM] + [VM] * 8,
        [(3, 10, 16, 256), (3, 10, 16, 256), (10, 16, 256), (NEW_ROWS, 256), (16, 640)],
        three
        + [(3, 3, 16, 256), (3, 16, 256)] * 2
        + [(4, 3, 16, 256), two, two, (2, 3, 16, 256), two]
        + modes
        + [plane],
        "first_step",
        20_000_000,
    )(u, v, dt, lab, par, own, cols, zb, za, force, mass, contact, lists)
    near = lax.ppermute(own, "plane", swaps)
    cross = call(pack_new_cross, [VM] * 2, [(NEW_CROSS_ROWS, 256)], [], "pack_new_cross", 100_000)(own, near)[0]
    far = lax.ppermute(cross, "plane", crossings)
    force = call(
        functools.partial(second_block, layers),
        [VM] * 3 + [SM, VM],
        [(3, 10, 16, 256)],
        [(9, 16, 256), (9, 16, 256)] + modes,
        "second_block",
        50_000_000,
    )(u1, dt, lab, par, zb)[0]
    far, force = lax.optimization_barrier((far, force))
    opp = lax.ppermute(far, ("plane", "layer"), face_swaps)
    u2, v2 = call(
        functools.partial(second_step, blocks, layers),
        [VM] * 5 + [SM] + [VM] * 6,
        [(3, 8, 16, 256)] * 2,
        [(4, 3, 16, 256), two, two, (2, 3, 16, 256)],
        "second_step",
        20_000_000,
    )(u1, v1, dtm, dt, lab, par, force, cols, zb, own, near, far)
    return tuple(
        call(
            functools.partial(second_contact, layers),
            [VM] * 7,
            [(3, 8, 16, 256)] * 2,
            [(2, 3, 2, 16, 256), pltpu.SemaphoreType.DMA((6,))],
            "second_contact",
            10_000_000,
            out_spec=HBM,
        )(u2, v2, dtm, lists, near, far, opp)
    )


def solution(mesh):
    in_specs = (
        P(None, "layer", "plane", None),
        P(None, "layer", "plane", None),
        P("layer", "plane", None),
        P("layer", "plane", None),
        P(),
        P("plane", None, None),
        P("plane", None, None),
        P("plane", None, None),
        P("plane", None),
    )
    out_specs = (P(None, "layer", "plane", None), P(None, "layer", "plane", None))
    return jax.shard_map(local, mesh=mesh, in_specs=in_specs, out_specs=out_specs, check_vma=False)
```

```python
import functools

import jax
import jax.numpy as jnp
from jax import lax
from jax.experimental import pallas as pl
from jax.experimental.pallas import tpu as pltpu
from jax.sharding import PartitionSpec as P

DT = 0.05
LUMPED = 0.25
F32 = jnp.float32
BF16 = jnp.bfloat16
QUADS = ((0, 0), (0, 1), (1, 0), (1, 1))

COL_HI, COL_LO, LISTS, PAD, EXPORT_ROWS = 0, 40, 64, 88, 136
OWN_OPP2, MATE_FAR1, MATE_FAR2, OWN_PAD, MATE_PAD, CROSS_ROWS = 40, 44, 48, 56, 104, 152
COL_LAB, COL_DT, COL_BEYOND, COLS_ROWS = 24, 32, 40, 64
ZU_U, ZU_V, ZU_LAB, ZU_DT, ZU_CL, ZU_CH, ZU_CLAB, ZU_CDT, ZU_ROWS = 0, 96, 144, 176, 208, 214, 220, 222, 224
ZD_U, ZD_V, ZD_LAB, ZD_DT, ZD_CL, ZD_CH, ZD_CLAB, ZD_CDT, ZD_ROWS = 0, 96, 144, 160, 176, 182, 188, 189, 192
NEW_HI, NEW_LO, NEW_ROWS, VALUES_ROWS = 0, 32, 64, 24
CROSS_OWN, CROSS_MATE, CROSS_ON, NEW_CROSS_ROWS = 32, 36, 40, 48
NEAR, FAR1, OWN, FAR2, OPP2 = range(5)
OFFSETS = (1, -1, 0, -2, 2)


def iota(shape, dim):
    return lax.broadcasted_iota(jnp.int32, shape, dim)


def on_even():
    return lax.rem(lax.axis_index("plane"), 2) == 0


def role_offset(role):
    return jnp.where(on_even(), OFFSETS[role], -OFFSETS[role])


def pack_export(
    blocks, layers,
    u_hbm, dt_hbm, lab_hbm, sol_hbm, land_hbm, stiff_hbm, tally_hbm,
    out,
    u, dt, lab, sol, land, stiff, tally, pos, ohy, ohx, sems,
):
    copies = [
        pltpu.make_async_copy(src, dst, sems.at[i])
        for i, (src, dst) in enumerate(
            (
                (u_hbm, u), (dt_hbm, dt), (lab_hbm, lab), (sol_hbm, sol),
                (land_hbm, land), (stiff_hbm, stiff), (tally_hbm, tally),
            )
        )
    ]
    for copy in copies:
        copy.start()
    for copy in copies[3:]:
        copy.wait()
    pad_z = u.shape[1] // 2 - 1
    here = lax.axis_index("plane")
    on_face = lax.axis_index("layer") == layers // 2

    @pl.when(on_face)
    def _():
        out[LISTS : LISTS + 24, :] = jnp.zeros((24, 256), F32)
        for k in range(5):
            row = LISTS + 4 * k
            target = here + (k - 2)
            count = jnp.where((target >= 0) & (target < blocks), tally[0, k], 0)
            live = iota((1, 128), 1) < count
            out[row : row + 1, 0:128] = sol[k].astype(F32)
            out[row : row + 1, 128:256] = land[k].astype(F32)
            out[row + 1 : row + 2, 0:128] = jnp.where(live, stiff[k], 0.0)
            pos[0:1, 128 * k : 128 * k + 128] = sol[k]
        ohy[...], ohx[...] = one_hots(pos[0:1, :])

    for copy in copies[:3]:
        copy.wait()
    for x, row in ((15, COL_HI), (0, COL_LO)):
        for c in range(3):
            out[row + 8 * c : row + 8 * c + 8, :] = u[c, :, x, :]
    out[COL_HI + COL_LAB : COL_HI + COL_LAB + 8, :] = lab[:, 15, :].astype(F32)
    out[COL_HI + COL_DT : COL_HI + COL_DT + 8, :] = dt[:, 15, :]

    @pl.when(on_face)
    def _():
        bump = gather(jnp.concatenate([u[c, pad_z + 1] for c in range(3)], axis=0), ohy[...], ohx[...])
        for k in range(5):
            row, cols = LISTS + 4 * k, slice(128 * k, 128 * k + 128)
            out[row + 1 : row + 2, 128:256] = bump[0:1, cols]
            out[row + 2 : row + 3, 0:128] = bump[1:2, cols]
            out[row + 2 : row + 3, 128:256] = bump[2:3, cols]
        for c in range(3):
            out[PAD + 16 * c : PAD + 16 * c + 16, :] = u[c, pad_z]


def stage(src, dst, sem):
    copy = pltpu.make_async_copy(src, dst, sem)
    copy.start()
    copy.wait()


def pack_cross(own, mate, out):
    even = on_even()

    def bucket(ref, if_even, if_odd):
        a, b = LISTS + 4 * if_even, LISTS + 4 * if_odd
        return jnp.where(even, ref[a : a + 4, :], ref[b : b + 4, :])

    out[24:40, :] = mate[COL_HI + 24 : COL_HI + 40, :]
    out[0:24, :] = jnp.where(even, mate[COL_HI : COL_HI + 24, :], mate[COL_LO : COL_LO + 24, :])
    out[OWN_OPP2 : OWN_OPP2 + 4, :] = bucket(own, 4, 0)
    out[MATE_FAR1 : MATE_FAR1 + 4, :] = bucket(mate, 3, 1)
    out[MATE_FAR2 : MATE_FAR2 + 4, :] = bucket(mate, 4, 0)
    out[MATE_FAR2 + 4 : OWN_PAD, :] = jnp.zeros((OWN_PAD - MATE_FAR2 - 4, 256), F32)
    out[OWN_PAD : OWN_PAD + 48, :] = own[PAD : PAD + 48, :]
    out[MATE_PAD : MATE_PAD + 48, :] = mate[PAD : PAD + 48, :]


def pack_layer(u, v, dt, lab, near, far, up, dn, cols):
    even = on_even()
    cols[0:40, :] = jnp.where(even, far[0:40, :], near[COL_HI : COL_HI + 40, :])
    cols[COL_BEYOND : COL_BEYOND + 24, :] = jnp.where(even, near[COL_LO : COL_LO + 24, :], far[0:24, :])
    for c in range(3):
        for zz in (0, 1):
            row = 16 * (2 * c + zz)
            up[ZU_U + row : ZU_U + row + 16, :] = u[c, 6 + zz]
            dn[ZD_U + row : ZD_U + row + 16, :] = u[c, zz]
        up[ZU_V + 16 * c : ZU_V + 16 * c + 16, :] = v[c, 7]
        dn[ZD_V + 16 * c : ZD_V + 16 * c + 16, :] = v[c, 0]
        lo, hi = 8 * c, COL_BEYOND + 8 * c
        up[ZU_CL + 2 * c : ZU_CL + 2 * c + 2, :] = cols[lo + 6 : lo + 8, :]
        up[ZU_CH + 2 * c : ZU_CH + 2 * c + 2, :] = cols[hi + 6 : hi + 8, :]
        dn[ZD_CL + 2 * c : ZD_CL + 2 * c + 2, :] = cols[lo : lo + 2, :]
        dn[ZD_CH + 2 * c : ZD_CH + 2 * c + 2, :] = cols[hi : hi + 2, :]
    for zz in (0, 1):
        up[ZU_LAB + 16 * zz : ZU_LAB + 16 * zz + 16, :] = lab[6 + zz].astype(F32)
        up[ZU_DT + 16 * zz : ZU_DT + 16 * zz + 16, :] = dt[6 + zz]
    up[ZU_CLAB : ZU_CLAB + 2, :] = cols[COL_LAB + 6 : COL_LAB + 8, :]
    up[ZU_CDT : ZU_CDT + 2, :] = cols[COL_DT + 6 : COL_DT + 8, :]
    dn[ZD_LAB : ZD_LAB + 16, :] = lab[0].astype(F32)
    dn[ZD_DT : ZD_DT + 16, :] = dt[0]
    dn[ZD_CLAB : ZD_CLAB + 1, :] = cols[COL_LAB : COL_LAB + 1, :]
    dn[ZD_CDT : ZD_CDT + 1, :] = cols[COL_DT : COL_DT + 1, :]
    dn[ZD_CDT + 1 : ZD_ROWS, :] = jnp.zeros((ZD_ROWS - ZD_CDT - 1, 256), F32)


def material_scalars(par):
    out = []
    for m in range(4):
        lam, mu, alpha, rho = par[0, m], par[1, m], par[2, m], par[3, m]
        out.append(
            (
                lam * (1.0 / 16.0),
                mu * (1.0 / 16.0),
                (lam + 4.0 * mu) * (1.0 / 144.0),
                (3.0 * lam + 2.0 * mu) * alpha * 0.25,
                rho * 0.125,
            )
        )
    return out


def cell_fields(mats, lab, dt, mask, with_mass):
    is0, is1, is2 = lab == 0.0, lab == 1.0, lab == 2.0

    def pick(i):
        rest = jnp.where(is2, mats[2][i], mats[3][i])
        return jnp.where(is0, mats[0][i], jnp.where(is1, mats[1][i], rest)) * mask

    return pick(0), pick(1), pick(2), pick(3) * dt, pick(4) if with_mass else None


def plane_modes(u, ux):
    s, d = u + ux, ux - u
    sy, dy = pltpu.roll(s, 255, 1), pltpu.roll(d, 255, 1)
    return [s + sy, sy - s, d + dy, dy - d]


def cell_forces(lower, upper, l1, m1, k3, th):
    z, x, y = (
        {
            (i, j, k): (upper[c][q] - lower[c][q]) if i else (upper[c][q] + lower[c][q])
            for q, (j, k) in enumerate(QUADS)
            for i in (0, 1)
            if i + j + k
        }
        for c in range(3)
    )
    l2, m2 = l1 * (1.0 / 3.0), m1 * (1.0 / 3.0)
    p0 = l1 * (z[1, 0, 0] + x[0, 1, 0] + y[0, 0, 1]) - th
    m1x2 = m1 + m1
    zx = m1 * (x[1, 0, 0] + z[0, 1, 0])
    zy = m1 * (y[1, 0, 0] + z[0, 0, 1])
    xy = m1 * (y[0, 1, 0] + x[0, 0, 1])
    pz = l2 * (x[1, 1, 0] + y[1, 0, 1])
    px = l2 * (z[1, 1, 0] + y[0, 1, 1])
    py = l2 * (z[1, 0, 1] + x[0, 1, 1])
    tw = z[0, 1, 1] + x[1, 0, 1] + y[1, 1, 0]
    fz = {
        (1, 0, 0): p0 + m1x2 * z[1, 0, 0],
        (0, 1, 0): zx,
        (0, 0, 1): zy,
        (1, 1, 0): px + m1 * z[1, 1, 0],
        (1, 0, 1): py + m1 * z[1, 0, 1],
        (0, 1, 1): m2 * (tw + z[0, 1, 1]),
        (1, 1, 1): k3 * z[1, 1, 1],
    }
    fx = {
        (0, 1, 0): p0 + m1x2 * x[0, 1, 0],
        (1, 0, 0): zx,
        (0, 0, 1): xy,
        (1, 1, 0): pz + m1 * x[1, 1, 0],
        (0, 1, 1): py + m1 * x[0, 1, 1],
        (1, 0, 1): m2 * (tw + x[1, 0, 1]),
        (1, 1, 1): k3 * x[1, 1, 1],
    }
    fy = {
        (0, 0, 1): p0 + m1x2 * y[0, 0, 1],
        (1, 0, 0): zy,
        (0, 1, 0): xy,
        (1, 0, 1): pz + m1 * y[1, 0, 1],
        (0, 1, 1): px + m1 * y[0, 1, 1],
        (1, 1, 0): m2 * (tw + y[1, 1, 0]),
        (1, 1, 1): k3 * y[1, 1, 1],
    }
    low, high = [], []
    for f in (fz, fx, fy):
        low_c, high_c = [], []
        for j, k in QUADS:
            d = f[1, j, k]
            if j + k:
                s = f[0, j, k]
                low_c.append(s - d)
                high_c.append(s + d)
            else:
                low_c.append(-d)
                high_c.append(d)
        low.append(low_c)
        high.append(high_c)
    return low, high


def fold_y(a, b):
    return (a - b) + pltpu.roll(a + b, 1, 1)


def column_forces(layers, zg, valid, mats, inside, side, left, right, lab, dt, with_mass):
    rows = lab.shape[0]
    shape = (rows, 256)
    ok = (zg >= 0) & (zg <= layers * 8 - 2) & (zg != layers // 2 * 8 + 3) & (iota(shape, 1) < 255)
    mask = jnp.where(ok & valid & inside, 1.0, 0.0)
    l1, m1, k3, th, rho = cell_fields(mats, lab, dt, mask, with_mass)
    lower = [plane_modes(left[c], right[c]) for c in range(3)]
    upper = [[pltpu.roll(a, rows - 1, 0) for a in comp] for comp in lower]
    low, high = cell_forces(lower, upper, l1, m1, k3, th)
    forces = []
    for c in range(3):
        node = [low[c][q] + pltpu.roll(high[c][q], 1, 0) for q in range(4)]
        t0, t1 = fold_y(node[0], node[1]), fold_y(node[2], node[3])
        forces.append(t0 + t1 if side > 0 else t0 - t1)
    if with_mass:
        rho = rho + pltpu.roll(rho, 1, 1)
        rho = rho + pltpu.roll(rho, 1, 0)
    return forces, rho


def block_forces(layers, cells, zbase, mats, u, lab, dt, modes, saved, saved_m, force, mass):
    shape = (16, 256)
    row, lane = iota(shape, 0), iota(shape, 1)
    in_plane = jnp.where((lane < 255) & (row < 15), 1.0, 0.0)

    def forward(e, c):
        a = u[c, e]
        return plane_modes(a, pltpu.roll(a, 15, 0))

    for c in range(3):
        for q, value in enumerate(forward(0, c)):
            modes[4 * c + q] = value
            saved[4 * c + q] = jnp.zeros(shape, F32)
    if mass is not None:
        saved_m[...] = jnp.zeros(shape, F32)

    def fold(e, node):
        for c in range(3):
            t0, t1 = fold_y(node[c][0], node[c][1]), fold_y(node[c][2], node[c][3])
            force[c, e] = (t0 - t1) + pltpu.roll(t0 + t1, 1, 0)

    def body(e, carry):
        zg = zbase + e
        ok = (zg >= 0) & (zg <= layers * 8 - 2) & (zg != layers // 2 * 8 + 3)
        mask = in_plane * jnp.where(ok, 1.0, 0.0)
        l1, m1, k3, th, rho = cell_fields(mats, lab[e].astype(F32), dt[e], mask, mass is not None)
        lower = [[modes[4 * c + q] for q in range(4)] for c in range(3)]
        upper = [forward(e + 1, c) for c in range(3)]
        for c in range(3):
            for q in range(4):
                modes[4 * c + q] = upper[c][q]
        low, high = cell_forces(lower, upper, l1, m1, k3, th)
        fold(e, [[low[c][q] + saved[4 * c + q] for q in range(4)] for c in range(3)])
        for c in range(3):
            for q in range(4):
                saved[4 * c + q] = high[c][q]
        if mass is not None:
            rho = rho + pltpu.roll(rho, 1, 1)
            rho = rho + pltpu.roll(rho, 1, 0)
            mass[e] = rho + saved_m[...]
            saved_m[...] = rho
        return carry

    lax.fori_loop(0, cells, body, 0)
    fold(cells, [[saved[4 * c + q] for q in range(4)] for c in range(3)])
    if mass is not None:
        mass[cells] = saved_m[...]


def two_layers(layers, z, mats, nodes, lab, dt):
    shape = (16, 256)
    in_plane = jnp.where((iota(shape, 1) < 255) & (iota(shape, 0) < 15), 1.0, 0.0)
    modes = [[plane_modes(a, pltpu.roll(a, 15, 0)) for a in node] for node in nodes]
    parts, masses = [], []
    for i in (0, 1):
        zg = z + i
        ok = (zg >= 0) & (zg <= layers * 8 - 2) & (zg != layers // 2 * 8 + 3)
        mask = in_plane * jnp.where(ok, 1.0, 0.0)
        l1, m1, k3, th, rho = cell_fields(mats, lab[i], dt[i], mask, True)
        parts.append(cell_forces(modes[i], modes[i + 1], l1, m1, k3, th))
        rho = rho + pltpu.roll(rho, 1, 1)
        masses.append(rho + pltpu.roll(rho, 1, 0))
    (low0, high0), (low1, high1) = parts
    middle = [[high0[c][q] + low1[c][q] for q in range(4)] for c in range(3)]
    return (low0, middle, high1), (masses[0], masses[0] + masses[1], masses[1])


def fold_node(node):
    t0, t1 = fold_y(node[0], node[1]), fold_y(node[2], node[3])
    return (t0 - t1) + pltpu.roll(t0 + t1, 1, 0)


def with_columns(a, first, last):
    row = iota((8, 256), 0)
    top = a[0:8] + jnp.where(row == 0, jnp.broadcast_to(first, (8, 256)), 0.0)
    bottom = a[8:16] + jnp.where(row == 7, jnp.broadcast_to(last, (8, 256)), 0.0)
    return jnp.concatenate([top, bottom], axis=0)


def split3(a):
    hi = a.astype(BF16)
    rest = a - hi.astype(F32)
    mid = rest.astype(BF16)
    lo = (rest - mid.astype(F32)).astype(BF16)
    return jnp.concatenate([hi, mid, lo], axis=0)


def join3(a):
    n = a.shape[0] // 3
    return (a[:n] + a[n : 2 * n]) + a[2 * n :]


def one_hots(position):
    pos = position.astype(jnp.int32)
    n = pos.shape[1]
    y, x = pos & 255, pos >> 8
    ohy = jnp.where(iota((256, n), 0) == y, 1.0, 0.0).astype(BF16)
    ohx = jnp.where(iota((16, n), 0) == x, 1.0, 0.0)
    return ohy, ohx


def gather(face, ohy, ohx):
    n = ohx.shape[1]
    rows = join3(jnp.dot(split3(face), ohy, preferred_element_type=F32))
    return jnp.sum(rows.reshape(3, 16, n) * ohx[None], axis=1)


def scatter(values, ohy, ohx):
    n = ohx.shape[1]
    rows = (values[:, None, :] * ohx[None]).reshape(48, n)
    out = lax.dot_general(split3(rows), ohy, (((1,), (1,)), ((), ())), preferred_element_type=F32)
    return join3(out).reshape(3, 16, 256)


def fill_lists(own, near, far, opp, lists):
    sources = {
        NEAR: (near, LISTS + 4 * (2 - role_offset(NEAR))),
        FAR1: (far, MATE_FAR1),
        OWN: (own, LISTS + 8),
        FAR2: (far, OWN_OPP2),
        OPP2: (opp, MATE_FAR2),
    }
    for role, (ref, base) in sources.items():
        cols = slice(128 * role, 128 * role + 128)
        row = LISTS + 4 * (2 + role_offset(role))
        for i in range(3):
            mine, other = own[pl.ds(row + i, 1), :], ref[pl.ds(base + i, 1), :]
            for half in (0, 1):
                part = slice(128 * half, 128 * half + 128)
                lists[2 * i + half : 2 * i + half + 1, cols] = mine[:, part]
                if i + half:
                    lists[5 + 2 * i + half : 6 + 2 * i + half, cols] = other[:, part]


def first_block(layers, u, dt, lab, par, force, mass, modes, saved, saved_m):
    zbase = lax.axis_index("layer") * 8
    block_forces(layers, 7, zbase, material_scalars(par), u, lab, dt, modes, saved, saved_m, force, mass)


def first_inner(
    blocks, layers, u, v, par, own, cols, force, mass, u1, v1, dtm, col_f, col_m
):
    here = lax.axis_index("plane")
    mats = material_scalars(par)
    row = iota((8, 256), 0)
    for at, inside, side in ((0, here > 0, 1), (1, here < blocks - 1, -1)):
        first = COL_LO if at == 0 else COL_HI
        mine = [own[first + 8 * c : first + 8 * c + 8, :] for c in range(3)]
        beyond = COL_BEYOND if at else 0
        theirs = [cols[beyond + 8 * c : beyond + 8 * c + 8, :] for c in range(3)]
        left, right = (mine, theirs) if at else (theirs, mine)
        ref = own if at else cols
        forces, rho = column_forces(
            layers, row + lax.axis_index("layer") * 8, row < 7, mats, inside, side, left, right,
            ref[COL_LAB : COL_LAB + 8, :], ref[COL_DT : COL_DT + 8, :], True,
        )
        for c in range(3):
            col_f[at, c] = forces[c]
        col_m[at] = rho
    for i in range(6):
        z = i + 1
        rate = DT / (LUMPED + with_columns(mass[z], col_m[0, z : z + 1, :], col_m[1, z : z + 1, :]))
        dtm[i] = rate
        for c in range(3):
            pull = with_columns(force[c, z], col_f[0, c, z : z + 1, :], col_f[1, c, z : z + 1, :])
            speed = v[c, z] - rate * pull
            v1[c, i] = speed
            u1[c, i] = u[c, z] + DT * speed


def first_contact(layers, own, near, far, opp, u1, v1, dtm, u_face, v_face, out, lists):
    @pl.when(lax.axis_index("layer") == layers // 2)
    def _():
        fill_lists(own, near, far, opp, lists)
        sol_y, sol_x = one_hots(lists[0:1, :])
        land_y, land_x = one_hots(lists[6:7, :])
        far_y, far_x = one_hots(lists[1:2, :])
        own_pad = own[PAD : PAD + 48, :]
        pads = {
            NEAR: near[PAD : PAD + 48, :],
            FAR1: far[MATE_PAD : MATE_PAD + 48, :],
            OWN: own_pad,
            FAR2: far[OWN_PAD : OWN_PAD + 48, :],
            OPP2: opp[MATE_PAD : MATE_PAD + 48, :],
        }
        far_pad = []
        for role in range(5):
            part = slice(128 * role, 128 * role + 128)
            far_pad.append(gather(pads[role], far_y[:, part], far_x[:, part]))
        on_bump = lists[2:3, :] * (jnp.concatenate(far_pad, axis=1) - lists[3:6, :])
        on_pad = lists[7:8, :] * (lists[8:11, :] - gather(own_pad, land_y, land_x))
        extra = (scatter(on_pad, land_y, land_x), scatter(on_bump, sol_y, sol_x))
        faces = []
        for face in (0, 1):
            new = []
            for c in range(3):
                change = dtm[2 + face] * extra[face][c]
                v_face[face, c] = v1[c, 2 + face] + change
                new.append(u1[c, 2 + face] + DT * change)
                u_face[face, c] = new[c]
            faces.append(jnp.concatenate(new, axis=0))
        lists[3:6, :] = gather(faces[1], sol_y, sol_x)
        lists[8:11, :] = gather(faces[0], land_y, land_x)
        for role in range(5):
            part = slice(128 * role, 128 * role + 128)
            for i, row in enumerate((3, 4, 5, 8, 9, 10)):
                at, half = 4 * role + i // 2, i % 2
                out[at : at + 1, 128 * half : 128 * half + 128] = lists[row : row + 1, part]


def first_step(
    blocks, layers,
    u, v, dt, lab, par, own, cols, zb, za, force, mass, in_f, in_m, ui, vi, dtmi, u_face, v_face, values, mate,
    u1, v1, dtm, ends, cross, swap,
    col, col_lab, col_dt, col_f, col_m,
):
    layer, here = lax.axis_index("layer"), lax.axis_index("plane")
    even = on_even()
    mats = material_scalars(par)
    for c in range(3):
        for at, first, zu, zd in ((0, 0, ZU_CL, ZD_CL), (3, COL_BEYOND, ZU_CH, ZD_CH)):
            col[at, c, 0:2, :] = zb[zu + 2 * c : zu + 2 * c + 2, :]
            col[at, c, 2:3, :] = cols[first + 8 * c : first + 8 * c + 1, :]
            col[at, c, 3:4, :] = cols[first + 8 * c + 7 : first + 8 * c + 8, :]
            col[at, c, 4:6, :] = za[zd + 2 * c : zd + 2 * c + 2, :]
            col[at, c, 6:8, :] = jnp.zeros((2, 256), F32)
        for at, first, x in ((1, COL_LO, 0), (2, COL_HI, 15)):
            for zz in (0, 1):
                row = 16 * (2 * c + zz) + x
                col[at, c, zz : zz + 1, :] = zb[ZU_U + row : ZU_U + row + 1, :]
                col[at, c, 4 + zz : 5 + zz, :] = za[ZD_U + row : ZD_U + row + 1, :]
            col[at, c, 2:3, :] = own[first + 8 * c : first + 8 * c + 1, :]
            col[at, c, 3:4, :] = own[first + 8 * c + 7 : first + 8 * c + 8, :]
            col[at, c, 6:8, :] = jnp.zeros((2, 256), F32)
    for ref, first, zu, zd, zuf, zdf in (
        (col_lab, COL_LAB, ZU_CLAB, ZD_CLAB, ZU_LAB, ZD_LAB),
        (col_dt, COL_DT, ZU_CDT, ZD_CDT, ZU_DT, ZD_DT),
    ):
        for at in (0, 1):
            ref[at] = jnp.zeros((8, 256), F32)
        ref[0, 0:2, :] = zb[zu : zu + 2, :]
        ref[0, 3:4, :] = cols[first + 7 : first + 8, :]
        ref[0, 4:5, :] = za[zd : zd + 1, :]
        ref[1, 0:1, :] = zb[zuf + 15 : zuf + 16, :]
        ref[1, 1:2, :] = zb[zuf + 31 : zuf + 32, :]
        ref[1, 3:4, :] = own[COL_HI + first + 7 : COL_HI + first + 8, :]
        ref[1, 4:5, :] = za[zdf + 15 : zdf + 16, :]
    row = iota((8, 256), 0)
    zg = layer * 8 + jnp.where(row < 3, row - 2, row + 4)
    valid = (row < 5) & (row != 2)
    for at, inside, side in ((0, here > 0, 1), (1, here < blocks - 1, -1)):
        left = [col[2 * at, c] for c in range(3)]
        right = [col[2 * at + 1, c] for c in range(3)]
        forces, rho = column_forces(
            layers, zg, valid, mats, inside, side, left, right, col_lab[at], col_dt[at], True
        )
        for c in range(3):
            col_f[at, c] = forces[c]
        col_m[at] = rho

    def face(ref, row):
        return ref[row : row + 16, :]

    below = [[face(zb, ZU_U + 16 * (2 * c + zz)) for c in range(3)] for zz in (0, 1)]
    above = [[face(za, ZD_U + 16 * (2 * c + zz)) for c in range(3)] for zz in (0, 1)]
    first, last = [u[c, 0] for c in range(3)], [u[c, 7] for c in range(3)]
    low_f, low_m = two_layers(
        layers, layer * 8 - 2, mats, below + [first],
        (face(zb, ZU_LAB), face(zb, ZU_LAB + 16)), (face(zb, ZU_DT), face(zb, ZU_DT + 16)),
    )
    high_f, high_m = two_layers(
        layers, layer * 8 + 7, mats, [last] + above,
        (lab[7].astype(F32), face(za, ZD_LAB)), (dt[7], face(za, ZD_DT)),
    )
    v_below = [face(zb, ZU_V + 16 * c) for c in range(3)]
    v_above = [face(za, ZD_V + 16 * c) for c in range(3)]
    for i, z, at, pulls, weight, place, speeds in (
        (0, -1, 1, low_f[1], low_m[1], below[1], v_below),
        (1, 0, 2, low_f[2], low_m[2], first, [v[c, 0] for c in range(3)]),
        (8, 7, 3, high_f[0], high_m[0], last, [v[c, 7] for c in range(3)]),
        (9, 8, 4, high_f[1], high_m[1], above[0], v_above),
    ):
        inner = 0 <= z < 8
        edges = [col_m[side, at : at + 1, :] for side in (0, 1)]
        if inner:
            weight = weight + mass[z]
            edges = [edges[side] + in_m[side, z : z + 1, :] for side in (0, 1)]
        rate = DT / (LUMPED + with_columns(weight, *edges))
        dtm[i] = rate
        for c in range(3):
            pull = fold_node(pulls[c])
            edges = [col_f[side, c, at : at + 1, :] for side in (0, 1)]
            if inner:
                pull = pull + force[c, z]
                edges = [edges[side] + in_f[side, c, z : z + 1, :] for side in (0, 1)]
            speed = speeds[c] - rate * with_columns(pull, *edges)
            v1[c, i] = speed
            u1[c, i] = place[c] + DT * speed
    dtm[2:8] = dtmi[...]
    for c in range(3):
        u1[c, 2:8] = ui[c]
        v1[c, 2:8] = vi[c]

    @pl.when(layer == layers // 2)
    def _():
        for c in range(3):
            for i in (0, 1):
                u1[c, 4 + i] = u_face[i, c]
                v1[c, 4 + i] = v_face[i, c]
        for row, src, role in ((CROSS_OWN, mate, OPP2), (CROSS_MATE, values, FAR1), (CROSS_ON, values, FAR2)):
            cross[row : row + 4, :] = src[4 * role : 4 * role + 4, :]

    for x, row in ((15, NEW_HI), (0, NEW_LO)):
        for c in range(3):
            ends[row + 10 * c : row + 10 * c + 8, :] = u1[c, 0:8, x, :]
            ends[row + 10 * c + 8 : row + 10 * c + 10, :] = u1[c, 8:10, x, :]
        ends[row + 30 : row + 32, :] = jnp.zeros((2, 256), F32)
    upper, lower = ends[NEW_HI : NEW_HI + 32, :], ends[NEW_LO : NEW_LO + 32, :]
    cross[0:32, :] = jnp.where(even, lower, upper)
    swap[...] = jnp.where(even, upper, lower)


def second_block(layers, u, dt, lab, par, zb, force, le, de, modes, saved):
    le[0] = zb[ZU_LAB + 16 : ZU_LAB + 32, :]
    de[0] = zb[ZU_DT + 16 : ZU_DT + 32, :]
    le[1:9] = lab[...].astype(F32)
    de[1:9] = dt[...]
    zbase = lax.axis_index("layer") * 8 - 1
    block_forces(layers, 9, zbase, material_scalars(par), u, le, de, modes, saved, None, force, None)


def second_step(
    blocks, layers,
    u, v, dtm, dt, lab, par, force, cols, zb, own, near, far,
    u2, v2,
    col, col_lab, col_dt, col_f,
):
    layer, here = lax.axis_index("layer"), lax.axis_index("plane")
    zeros = jnp.zeros((8, 256), F32)
    mats = material_scalars(par)
    even = on_even()
    for c in range(3):
        at, hi, lo = 10 * c, NEW_HI + 10 * c, NEW_LO + 10 * c
        for i in range(4):
            col[i, c, 8:16, :] = zeros
        col[0, c, 0:10, :] = jnp.where(even, far[at : at + 10, :], near[at : at + 10, :])
        col[1, c, 0:10, :] = own[lo : lo + 10, :]
        col[2, c, 0:10, :] = own[hi : hi + 10, :]
        col[3, c, 0:10, :] = jnp.where(even, near[at : at + 10, :], far[at : at + 10, :])
    for ref, src, first, zu, zuf in (
        (col_lab, lab, COL_LAB, ZU_CLAB, ZU_LAB),
        (col_dt, dt, COL_DT, ZU_CDT, ZU_DT),
    ):
        for at in (0, 1):
            ref[at, 8:16, :] = zeros
        ref[0, 0:1, :] = zb[zu + 1 : zu + 2, :]
        ref[0, 1:9, :] = cols[first : first + 8, :]
        ref[1, 0:1, :] = zb[zuf + 31 : zuf + 32, :]
        ref[1, 1:9, :] = src[:, 15, :].astype(F32)
    zg = iota((16, 256), 0) + (layer * 8 - 1)
    for at, inside, side in ((0, here > 0, 1), (1, here < blocks - 1, -1)):
        left = [col[2 * at, c] for c in range(3)]
        right = [col[2 * at + 1, c] for c in range(3)]
        forces, _ = column_forces(
            layers, zg, zg < layer * 8 + 8, mats, inside, side, left, right, col_lab[at], col_dt[at], False
        )
        for c in range(3):
            col_f[at, c] = forces[c]
    for z in range(8):
        e = z + 1
        rate = dtm[e]
        for c in range(3):
            pull = with_columns(force[c, e], col_f[0, c, e : e + 1, :], col_f[1, c, e : e + 1, :])
            speed = v[c, e] - rate * pull
            v2[c, z] = speed
            u2[c, z] = u[c, e] + DT * speed


def second_contact(layers, u, v, dtm, lists, mate, far, opp, u2, v2, faces, sems):
    copies = []
    for i, (src, dst) in enumerate(((u, u2), (v, v2))):
        for first, last in ((0, 3), (5, 8)):
            copies.append(
                pltpu.make_async_copy(src.at[:, first:last], dst.at[:, first:last], sems.at[len(copies)])
            )
    for copy in copies:
        copy.start()
    for c in range(3):
        for face in (0, 1):
            faces[0, c, face] = u[c, 3 + face]
            faces[1, c, face] = v[c, 3 + face]

    @pl.when(lax.axis_index("layer") == layers // 2)
    def _():
        sol_y, sol_x = one_hots(lists[0:1, :])
        land_y, land_x = one_hots(lists[6:7, :])

        def values(i):
            half = slice(128 * (i % 2), 128 * (i % 2) + 128)
            own_row = (3, 4, 5, 8, 9, 10)[i]
            places = (
                (mate, 4 * NEAR), (far, CROSS_MATE), None, (far, CROSS_OWN), (opp, CROSS_ON)
            )
            parts = [
                lists[own_row : own_row + 1, 256:384] if place is None
                else place[0][place[1] + i // 2 : place[1] + i // 2 + 1, half]
                for place in places
            ]
            return jnp.concatenate(parts, axis=1)

        far_bump = jnp.concatenate([values(i) for i in range(3)], axis=0)
        far_pad = jnp.concatenate([values(i) for i in range(3, 6)], axis=0)
        on_bump = lists[2:3, :] * (far_pad - lists[3:6, :])
        on_pad = lists[7:8, :] * (far_bump - lists[8:11, :])
        extra = (scatter(on_pad, land_y, land_x), scatter(on_bump, sol_y, sol_x))
        for c in range(3):
            for face in (0, 1):
                change = dtm[4 + face] * extra[face][c]
                faces[0, c, face] = faces[0, c, face] + DT * change
                faces[1, c, face] = faces[1, c, face] + change

    for i, dst in enumerate((u2, v2)):
        copy = pltpu.make_async_copy(faces.at[i], dst.at[:, 3:5], sems.at[4 + i])
        copy.start()
        copies.append(copy)
    for copy in copies:
        copy.wait()


VM = pl.BlockSpec(memory_space=pltpu.VMEM)
SM = pl.BlockSpec(memory_space=pltpu.SMEM)
HBM = pl.BlockSpec(memory_space=pltpu.HBM)


def call(kernel, in_specs, outs, scratch, name, flops, vmem=32, out_spec=VM):
    return pl.pallas_call(
        kernel,
        out_shape=[jax.ShapeDtypeStruct(shape, F32) for shape in outs],
        in_specs=in_specs,
        out_specs=[out_spec] * len(outs),
        scratch_shapes=[pltpu.VMEM(s, F32) if isinstance(s, tuple) else s for s in scratch],
        compiler_params=pltpu.CompilerParams(vmem_limit_bytes=vmem * 1024 * 1024),
        cost_estimate=pl.CostEstimate(flops=flops, bytes_accessed=2_000_000, transcendentals=0),
        name=name,
    )


def local(u, v, dt, lab, par, sol, land, stiff, tally):
    blocks, layers = lax.axis_size("plane"), lax.axis_size("layer")
    swaps = [(s, s ^ 1) for s in range(blocks)]
    crossings = [(s, s + 2 - 4 * (s % 2)) for s in range(blocks) if 0 <= s + 2 - 4 * (s % 2) < blocks]
    face_swaps = [(a * layers + layers // 2, b * layers + layers // 2) for a, b in swaps]

    def along_layer(value, steps):
        pairs = [(s, s + steps) for s in range(layers) if 0 <= s + steps < layers]
        return lax.ppermute(value, "layer", pairs)

    own = call(
        functools.partial(pack_export, blocks, layers),
        [HBM] * 7,
        [(EXPORT_ROWS, 256)],
        [u.shape, dt.shape, pltpu.VMEM(lab.shape, jnp.int32)]
        + [pltpu.VMEM((5, 1, 128), jnp.int32)] * 2
        + [(5, 1, 128), pltpu.SMEM((1, 5), jnp.int32), pltpu.VMEM((8, 640), jnp.int32)]
        + [pltpu.VMEM((256, 640), BF16), (16, 640), pltpu.SemaphoreType.DMA((7,))],
        "pack_export",
        100_000,
        63,
    )(u, dt, lab, sol.reshape(5, 1, 128), land.reshape(5, 1, 128), stiff.reshape(5, 1, 128), tally)[0]
    near = lax.ppermute(own, "plane", swaps)
    own = call(stage, [HBM], [own.shape], [pltpu.SemaphoreType.DMA], "stage", 100_000)(own)[0]
    cross = call(pack_cross, [VM] * 2, [(CROSS_ROWS, 256)], [], "pack_cross", 100_000)(own, near)[0]
    far = lax.ppermute(cross, "plane", crossings)
    modes = [(12, 16, 256), (12, 16, 256)]
    plane = (16, 256)
    force, mass = call(
        functools.partial(first_block, layers),
        [VM] * 3 + [SM],
        [(3, 8, 16, 256), (8, 16, 256)],
        modes + [plane],
        "first_block",
        50_000_000,
    )(u, dt, lab, par)
    far, force, mass = lax.optimization_barrier((far, force, mass))
    up, dn, cols = call(
        pack_layer, [VM] * 6, [(ZU_ROWS, 256), (ZD_ROWS, 256), (COLS_ROWS, 256)], [], "pack_layer", 100_000
    )(u, v, dt, lab, near, far)
    zb, za = along_layer(up, 1), along_layer(dn, -1)
    opp = lax.ppermute(far, ("plane", "layer"), face_swaps)
    u1, v1, dtm, in_f, in_m = call(
        functools.partial(first_inner, blocks, layers),
        [VM] * 2 + [SM] + [VM] * 4,
        [(3, 6, 16, 256), (3, 6, 16, 256), (6, 16, 256), (2, 3, 8, 256), (2, 8, 256)],
        [],
        "first_inner",
        10_000_000,
    )(u, v, par, own, cols, force, mass)
    opp, u1, v1 = lax.optimization_barrier((opp, u1, v1))
    u_face, v_face, values, lists = call(
        functools.partial(first_contact, layers),
        [VM] * 7,
        [(2, 3, 16, 256), (2, 3, 16, 256), (VALUES_ROWS, 256), (16, 640)],
        [],
        "first_contact",
        10_000_000,
    )(own, near, far, opp, u1, v1, dtm)
    mate = lax.ppermute(values, ("plane", "layer"), face_swaps)

    two = (2, 8, 256)
    u1, v1, dtm, ends, cross, swap = call(
        functools.partial(first_step, blocks, layers),
        [VM] * 4 + [SM] + [VM] * 15,
        [(3, 10, 16, 256), (3, 10, 16, 256), (10, 16, 256), (NEW_ROWS, 256), (NEW_CROSS_ROWS, 256), (32, 256)],
        [(4, 3, 8, 256), two, two, (2, 3, 8, 256), two],
        "first_step",
        20_000_000,
    )(u, v, dt, lab, par, own, cols, zb, za, force, mass, in_f, in_m, u1, v1, dtm, u_face, v_face, values, mate)
    across = [(s, s + 1) for s in range(1, blocks - 1, 2)] + [(s, s - 1) for s in range(2, blocks, 2)]
    far = lax.ppermute(cross, "plane", across)
    near = lax.ppermute(swap, "plane", swaps)
    force = call(
        functools.partial(second_block, layers),
        [VM] * 3 + [SM, VM],
        [(3, 10, 16, 256)],
        [(9, 16, 256), (9, 16, 256)] + modes,
        "second_block",
        50_000_000,
    )(u1, dt, lab, par, zb)[0]
    far, near, force = lax.optimization_barrier((far, near, force))
    opp = lax.ppermute(far, ("plane", "layer"), face_swaps)
    two = (2, 16, 256)
    u2, v2 = call(
        functools.partial(second_step, blocks, layers),
        [VM] * 5 + [SM] + [VM] * 6,
        [(3, 8, 16, 256)] * 2,
        [(4, 3, 16, 256), two, two, (2, 3, 16, 256)],
        "second_step",
        20_000_000,
    )(u1, v1, dtm, dt, lab, par, force, cols, zb, ends, near, far)
    return tuple(
        call(
            functools.partial(second_contact, layers),
            [VM] * 7,
            [(3, 8, 16, 256)] * 2,
            [(2, 3, 2, 16, 256), pltpu.SemaphoreType.DMA((6,))],
            "second_contact",
            10_000_000,
            out_spec=HBM,
        )(u2, v2, dtm, lists, mate, far, opp)
    )


def solution(mesh):
    in_specs = (
        P(None, "layer", "plane", None),
        P(None, "layer", "plane", None),
        P("layer", "plane", None),
        P("layer", "plane", None),
        P(),
        P("plane", None, None),
        P("plane", None, None),
        P("plane", None, None),
        P("plane", None),
    )
    out_specs = (P(None, "layer", "plane", None), P(None, "layer", "plane", None))
    return jax.shard_map(local, mesh=mesh, in_specs=in_specs, out_specs=out_specs, check_vma=False)
```

```python
import functools

import jax
import jax.numpy as jnp
from jax import lax
from jax.experimental import pallas as pl
from jax.experimental.pallas import tpu as pltpu
from jax.sharding import PartitionSpec as P

DT = 0.05
LUMPED = 0.25
F32 = jnp.float32
BF16 = jnp.bfloat16
QUADS = ((0, 0), (0, 1), (1, 0), (1, 1))

COL_HI, COL_LO, LISTS, PAD, EXPORT_ROWS = 0, 40, 64, 88, 136
OWN_OPP2, MATE_FAR1, MATE_FAR2, OWN_PAD, MATE_PAD, CROSS_ROWS = 40, 44, 48, 56, 104, 152
COL_LAB, COL_DT, COL_BEYOND, COLS_ROWS = 24, 32, 40, 64
ZU_U, ZU_V, ZU_LAB, ZU_DT, ZU_CL, ZU_CH, ZU_CLAB, ZU_CDT, ZU_ROWS = 0, 96, 144, 176, 208, 214, 220, 222, 224
ZD_U, ZD_V, ZD_LAB, ZD_DT, ZD_CL, ZD_CH, ZD_CLAB, ZD_CDT, ZD_ROWS = 0, 96, 144, 160, 176, 182, 188, 189, 192
NEW_HI, NEW_LO, NEW_ROWS, VALUES_ROWS = 0, 32, 64, 24
CROSS_OWN, CROSS_MATE, CROSS_ON, NEW_CROSS_ROWS = 32, 36, 40, 48
NEAR, FAR1, OWN, FAR2, OPP2 = range(5)
OFFSETS = (1, -1, 0, -2, 2)


def iota(shape, dim):
    return lax.broadcasted_iota(jnp.int32, shape, dim)


def on_even():
    return lax.rem(lax.axis_index("plane"), 2) == 0


def role_offset(role):
    return jnp.where(on_even(), OFFSETS[role], -OFFSETS[role])


def pack_export(
    blocks, layers,
    u_hbm, dt_hbm, lab_hbm, sol_hbm, land_hbm, stiff_hbm, tally_hbm,
    out,
    u, dt, lab, sol, land, stiff, tally, pos, ohy, ohx, sems,
):
    copies = [
        pltpu.make_async_copy(src, dst, sems.at[i])
        for i, (src, dst) in enumerate(
            (
                (u_hbm, u), (dt_hbm, dt), (lab_hbm, lab), (sol_hbm, sol),
                (land_hbm, land), (stiff_hbm, stiff), (tally_hbm, tally),
            )
        )
    ]
    for copy in copies:
        copy.start()
    for copy in copies[3:]:
        copy.wait()
    pad_z = u.shape[1] // 2 - 1
    here = lax.axis_index("plane")
    on_face = lax.axis_index("layer") == layers // 2

    @pl.when(on_face)
    def _():
        out[LISTS : LISTS + 24, :] = jnp.zeros((24, 256), F32)
        for k in range(5):
            row = LISTS + 4 * k
            target = here + (k - 2)
            count = jnp.where((target >= 0) & (target < blocks), tally[0, k], 0)
            live = iota((1, 128), 1) < count
            out[row : row + 1, 0:128] = sol[k].astype(F32)
            out[row : row + 1, 128:256] = land[k].astype(F32)
            out[row + 1 : row + 2, 0:128] = jnp.where(live, stiff[k], 0.0)
            pos[0:1, 128 * k : 128 * k + 128] = sol[k]
        ohy[...], ohx[...] = one_hots(pos[0:1, :])

    for copy in copies[:3]:
        copy.wait()
    for x, row in ((15, COL_HI), (0, COL_LO)):
        for c in range(3):
            out[row + 8 * c : row + 8 * c + 8, :] = u[c, :, x, :]
    out[COL_HI + COL_LAB : COL_HI + COL_LAB + 8, :] = lab[:, 15, :].astype(F32)
    out[COL_HI + COL_DT : COL_HI + COL_DT + 8, :] = dt[:, 15, :]

    @pl.when(on_face)
    def _():
        bump = gather(jnp.concatenate([u[c, pad_z + 1] for c in range(3)], axis=0), ohy[...], ohx[...])
        for k in range(5):
            row, cols = LISTS + 4 * k, slice(128 * k, 128 * k + 128)
            out[row + 1 : row + 2, 128:256] = bump[0:1, cols]
            out[row + 2 : row + 3, 0:128] = bump[1:2, cols]
            out[row + 2 : row + 3, 128:256] = bump[2:3, cols]
        for c in range(3):
            out[PAD + 16 * c : PAD + 16 * c + 16, :] = u[c, pad_z]


def stage(src, dst, sem):
    copy = pltpu.make_async_copy(src, dst, sem)
    copy.start()
    copy.wait()


def pack_cross(own, mate, out):
    even = on_even()

    def bucket(ref, if_even, if_odd):
        a, b = LISTS + 4 * if_even, LISTS + 4 * if_odd
        return jnp.where(even, ref[a : a + 4, :], ref[b : b + 4, :])

    out[24:40, :] = mate[COL_HI + 24 : COL_HI + 40, :]
    out[0:24, :] = jnp.where(even, mate[COL_HI : COL_HI + 24, :], mate[COL_LO : COL_LO + 24, :])
    out[OWN_OPP2 : OWN_OPP2 + 4, :] = bucket(own, 4, 0)
    out[MATE_FAR1 : MATE_FAR1 + 4, :] = bucket(mate, 3, 1)
    out[MATE_FAR2 : MATE_FAR2 + 4, :] = bucket(mate, 4, 0)
    out[MATE_FAR2 + 4 : OWN_PAD, :] = jnp.zeros((OWN_PAD - MATE_FAR2 - 4, 256), F32)
    out[OWN_PAD : OWN_PAD + 48, :] = own[PAD : PAD + 48, :]
    out[MATE_PAD : MATE_PAD + 48, :] = mate[PAD : PAD + 48, :]


def pack_layer(u, v, dt, lab, near, far, up, dn, cols):
    even = on_even()
    cols[0:40, :] = jnp.where(even, far[0:40, :], near[COL_HI : COL_HI + 40, :])
    cols[COL_BEYOND : COL_BEYOND + 24, :] = jnp.where(even, near[COL_LO : COL_LO + 24, :], far[0:24, :])
    for c in range(3):
        for zz in (0, 1):
            row = 16 * (2 * c + zz)
            up[ZU_U + row : ZU_U + row + 16, :] = u[c, 6 + zz]
            dn[ZD_U + row : ZD_U + row + 16, :] = u[c, zz]
        up[ZU_V + 16 * c : ZU_V + 16 * c + 16, :] = v[c, 7]
        dn[ZD_V + 16 * c : ZD_V + 16 * c + 16, :] = v[c, 0]
        lo, hi = 8 * c, COL_BEYOND + 8 * c
        up[ZU_CL + 2 * c : ZU_CL + 2 * c + 2, :] = cols[lo + 6 : lo + 8, :]
        up[ZU_CH + 2 * c : ZU_CH + 2 * c + 2, :] = cols[hi + 6 : hi + 8, :]
        dn[ZD_CL + 2 * c : ZD_CL + 2 * c + 2, :] = cols[lo : lo + 2, :]
        dn[ZD_CH + 2 * c : ZD_CH + 2 * c + 2, :] = cols[hi : hi + 2, :]
    for zz in (0, 1):
        up[ZU_LAB + 16 * zz : ZU_LAB + 16 * zz + 16, :] = lab[6 + zz].astype(F32)
        up[ZU_DT + 16 * zz : ZU_DT + 16 * zz + 16, :] = dt[6 + zz]
    up[ZU_CLAB : ZU_CLAB + 2, :] = cols[COL_LAB + 6 : COL_LAB + 8, :]
    up[ZU_CDT : ZU_CDT + 2, :] = cols[COL_DT + 6 : COL_DT + 8, :]
    dn[ZD_LAB : ZD_LAB + 16, :] = lab[0].astype(F32)
    dn[ZD_DT : ZD_DT + 16, :] = dt[0]
    dn[ZD_CLAB : ZD_CLAB + 1, :] = cols[COL_LAB : COL_LAB + 1, :]
    dn[ZD_CDT : ZD_CDT + 1, :] = cols[COL_DT : COL_DT + 1, :]
    dn[ZD_CDT + 1 : ZD_ROWS, :] = jnp.zeros((ZD_ROWS - ZD_CDT - 1, 256), F32)


def material_scalars(par):
    out = []
    for m in range(4):
        lam, mu, alpha, rho = par[0, m], par[1, m], par[2, m], par[3, m]
        out.append(
            (
                lam * (1.0 / 16.0),
                mu * (1.0 / 16.0),
                (lam + 4.0 * mu) * (1.0 / 144.0),
                (3.0 * lam + 2.0 * mu) * alpha * 0.25,
                rho * 0.125,
            )
        )
    return out


def cell_fields(mats, lab, dt, mask, with_mass):
    is0, is1, is2 = lab == 0.0, lab == 1.0, lab == 2.0

    def pick(i):
        rest = jnp.where(is2, mats[2][i], mats[3][i])
        return jnp.where(is0, mats[0][i], jnp.where(is1, mats[1][i], rest)) * mask

    return pick(0), pick(1), pick(2), pick(3) * dt, pick(4) if with_mass else None


def plane_modes(u, ux):
    s, d = u + ux, ux - u
    sy, dy = pltpu.roll(s, 255, 1), pltpu.roll(d, 255, 1)
    return [s + sy, sy - s, d + dy, dy - d]


def cell_forces(lower, upper, l1, m1, k3, th):
    z, x, y = (
        {
            (i, j, k): (upper[c][q] - lower[c][q]) if i else (upper[c][q] + lower[c][q])
            for q, (j, k) in enumerate(QUADS)
            for i in (0, 1)
            if i + j + k
        }
        for c in range(3)
    )
    l2, m2 = l1 * (1.0 / 3.0), m1 * (1.0 / 3.0)
    p0 = l1 * (z[1, 0, 0] + x[0, 1, 0] + y[0, 0, 1]) - th
    m1x2 = m1 + m1
    zx = m1 * (x[1, 0, 0] + z[0, 1, 0])
    zy = m1 * (y[1, 0, 0] + z[0, 0, 1])
    xy = m1 * (y[0, 1, 0] + x[0, 0, 1])
    pz = l2 * (x[1, 1, 0] + y[1, 0, 1])
    px = l2 * (z[1, 1, 0] + y[0, 1, 1])
    py = l2 * (z[1, 0, 1] + x[0, 1, 1])
    tw = z[0, 1, 1] + x[1, 0, 1] + y[1, 1, 0]
    fz = {
        (1, 0, 0): p0 + m1x2 * z[1, 0, 0],
        (0, 1, 0): zx,
        (0, 0, 1): zy,
        (1, 1, 0): px + m1 * z[1, 1, 0],
        (1, 0, 1): py + m1 * z[1, 0, 1],
        (0, 1, 1): m2 * (tw + z[0, 1, 1]),
        (1, 1, 1): k3 * z[1, 1, 1],
    }
    fx = {
        (0, 1, 0): p0 + m1x2 * x[0, 1, 0],
        (1, 0, 0): zx,
        (0, 0, 1): xy,
        (1, 1, 0): pz + m1 * x[1, 1, 0],
        (0, 1, 1): py + m1 * x[0, 1, 1],
        (1, 0, 1): m2 * (tw + x[1, 0, 1]),
        (1, 1, 1): k3 * x[1, 1, 1],
    }
    fy = {
        (0, 0, 1): p0 + m1x2 * y[0, 0, 1],
        (1, 0, 0): zy,
        (0, 1, 0): xy,
        (1, 0, 1): pz + m1 * y[1, 0, 1],
        (0, 1, 1): px + m1 * y[0, 1, 1],
        (1, 1, 0): m2 * (tw + y[1, 1, 0]),
        (1, 1, 1): k3 * y[1, 1, 1],
    }
    low, high = [], []
    for f in (fz, fx, fy):
        low_c, high_c = [], []
        for j, k in QUADS:
            d = f[1, j, k]
            if j + k:
                s = f[0, j, k]
                low_c.append(s - d)
                high_c.append(s + d)
            else:
                low_c.append(-d)
                high_c.append(d)
        low.append(low_c)
        high.append(high_c)
    return low, high


def fold_y(a, b):
    return (a - b) + pltpu.roll(a + b, 1, 1)


def column_forces(layers, zg, valid, mats, inside, side, left, right, lab, dt, with_mass):
    rows = lab.shape[0]
    shape = (rows, 256)
    ok = (zg >= 0) & (zg <= layers * 8 - 2) & (zg != layers // 2 * 8 + 3) & (iota(shape, 1) < 255)
    mask = jnp.where(ok & valid & inside, 1.0, 0.0)
    l1, m1, k3, th, rho = cell_fields(mats, lab, dt, mask, with_mass)
    lower = [plane_modes(left[c], right[c]) for c in range(3)]
    upper = [[pltpu.roll(a, rows - 1, 0) for a in comp] for comp in lower]
    low, high = cell_forces(lower, upper, l1, m1, k3, th)
    forces = []
    for c in range(3):
        node = [low[c][q] + pltpu.roll(high[c][q], 1, 0) for q in range(4)]
        t0, t1 = fold_y(node[0], node[1]), fold_y(node[2], node[3])
        forces.append(t0 + t1 if side > 0 else t0 - t1)
    if with_mass:
        rho = rho + pltpu.roll(rho, 1, 1)
        rho = rho + pltpu.roll(rho, 1, 0)
    return forces, rho


def block_forces(layers, cells, group, zbase, mats, u, lab, dt, modes, saved, saved_m, force, mass):
    shape = (16, 256)
    row, lane = iota(shape, 0), iota(shape, 1)
    in_plane = jnp.where((lane < 255) & (row < 15), 1.0, 0.0)

    def forward(e, c):
        a = u[c, e]
        return plane_modes(a, pltpu.roll(a, 15, 0))

    for c in range(3):
        for q, value in enumerate(forward(0, c)):
            modes[4 * c + q] = value
            saved[4 * c + q] = jnp.zeros(shape, F32)
    if mass is not None:
        saved_m[...] = jnp.zeros(shape, F32)

    def fold(e, node):
        for c in range(3):
            t0, t1 = fold_y(node[c][0], node[c][1]), fold_y(node[c][2], node[c][3])
            force[c, e] = (t0 - t1) + pltpu.roll(t0 + t1, 1, 0)

    def body(i, carry):
        lower = [[modes[4 * c + q] for q in range(4)] for c in range(3)]
        held = [[saved[4 * c + q] for q in range(4)] for c in range(3)]
        held_m = None if mass is None else saved_m[...]
        for g in range(group):
            e = i * group + g
            zg = zbase + e
            ok = (zg >= 0) & (zg <= layers * 8 - 2) & (zg != layers // 2 * 8 + 3)
            mask = in_plane * jnp.where(ok, 1.0, 0.0)
            l1, m1, k3, th, rho = cell_fields(mats, lab[e].astype(F32), dt[e], mask, mass is not None)
            upper = [forward(e + 1, c) for c in range(3)]
            low, high = cell_forces(lower, upper, l1, m1, k3, th)
            fold(e, [[low[c][q] + held[c][q] for q in range(4)] for c in range(3)])
            lower, held = upper, high
            if mass is not None:
                rho = rho + pltpu.roll(rho, 1, 1)
                rho = rho + pltpu.roll(rho, 1, 0)
                mass[e] = rho + held_m
                held_m = rho
        for c in range(3):
            for q in range(4):
                modes[4 * c + q] = lower[c][q]
                saved[4 * c + q] = held[c][q]
        if mass is not None:
            saved_m[...] = held_m
        return carry

    lax.fori_loop(0, cells // group, body, 0)
    fold(cells, [[saved[4 * c + q] for q in range(4)] for c in range(3)])
    if mass is not None:
        mass[cells] = saved_m[...]


def two_layers(layers, z, mats, nodes, lab, dt):
    shape = (16, 256)
    in_plane = jnp.where((iota(shape, 1) < 255) & (iota(shape, 0) < 15), 1.0, 0.0)
    modes = [[plane_modes(a, pltpu.roll(a, 15, 0)) for a in node] for node in nodes]
    parts, masses = [], []
    for i in (0, 1):
        zg = z + i
        ok = (zg >= 0) & (zg <= layers * 8 - 2) & (zg != layers // 2 * 8 + 3)
        mask = in_plane * jnp.where(ok, 1.0, 0.0)
        l1, m1, k3, th, rho = cell_fields(mats, lab[i], dt[i], mask, True)
        parts.append(cell_forces(modes[i], modes[i + 1], l1, m1, k3, th))
        rho = rho + pltpu.roll(rho, 1, 1)
        masses.append(rho + pltpu.roll(rho, 1, 0))
    (low0, high0), (low1, high1) = parts
    middle = [[high0[c][q] + low1[c][q] for q in range(4)] for c in range(3)]
    return (low0, middle, high1), (masses[0], masses[0] + masses[1], masses[1])


def fold_node(node):
    t0, t1 = fold_y(node[0], node[1]), fold_y(node[2], node[3])
    return (t0 - t1) + pltpu.roll(t0 + t1, 1, 0)


def with_columns(a, first, last):
    row = iota((8, 256), 0)
    top = a[0:8] + jnp.where(row == 0, jnp.broadcast_to(first, (8, 256)), 0.0)
    bottom = a[8:16] + jnp.where(row == 7, jnp.broadcast_to(last, (8, 256)), 0.0)
    return jnp.concatenate([top, bottom], axis=0)


def split3(a):
    hi = a.astype(BF16)
    rest = a - hi.astype(F32)
    mid = rest.astype(BF16)
    lo = (rest - mid.astype(F32)).astype(BF16)
    return jnp.concatenate([hi, mid, lo], axis=0)


def join3(a):
    n = a.shape[0] // 3
    return (a[:n] + a[n : 2 * n]) + a[2 * n :]


def one_hots(position):
    pos = position.astype(jnp.int32)
    n = pos.shape[1]
    y, x = pos & 255, pos >> 8
    ohy = jnp.where(iota((256, n), 0) == y, 1.0, 0.0).astype(BF16)
    ohx = jnp.where(iota((16, n), 0) == x, 1.0, 0.0)
    return ohy, ohx


def gather(face, ohy, ohx):
    n = ohx.shape[1]
    rows = join3(jnp.dot(split3(face), ohy, preferred_element_type=F32))
    return jnp.sum(rows.reshape(3, 16, n) * ohx[None], axis=1)


def scatter(values, ohy, ohx):
    n = ohx.shape[1]
    rows = (values[:, None, :] * ohx[None]).reshape(48, n)
    out = lax.dot_general(split3(rows), ohy, (((1,), (1,)), ((), ())), preferred_element_type=F32)
    return join3(out).reshape(3, 16, 256)


def fill_lists(own, near, far, opp, lists):
    sources = {
        NEAR: (near, LISTS + 4 * (2 - role_offset(NEAR))),
        FAR1: (far, MATE_FAR1),
        OWN: (own, LISTS + 8),
        FAR2: (far, OWN_OPP2),
        OPP2: (opp, MATE_FAR2),
    }
    for role, (ref, base) in sources.items():
        cols = slice(128 * role, 128 * role + 128)
        row = LISTS + 4 * (2 + role_offset(role))
        for i in range(3):
            mine, other = own[pl.ds(row + i, 1), :], ref[pl.ds(base + i, 1), :]
            for half in (0, 1):
                part = slice(128 * half, 128 * half + 128)
                lists[2 * i + half : 2 * i + half + 1, cols] = mine[:, part]
                if i + half:
                    lists[5 + 2 * i + half : 6 + 2 * i + half, cols] = other[:, part]


def first_block(layers, u, dt, lab, par, force, mass, modes, saved, saved_m):
    zbase = lax.axis_index("layer") * 8
    block_forces(layers, 7, 1, zbase, material_scalars(par), u, lab, dt, modes, saved, saved_m, force, mass)


def first_inner(
    blocks, layers, u, v, par, own, cols, force, mass, u1, v1, dtm, col_f, col_m
):
    here = lax.axis_index("plane")
    mats = material_scalars(par)
    row = iota((8, 256), 0)
    for at, inside, side in ((0, here > 0, 1), (1, here < blocks - 1, -1)):
        first = COL_LO if at == 0 else COL_HI
        mine = [own[first + 8 * c : first + 8 * c + 8, :] for c in range(3)]
        beyond = COL_BEYOND if at else 0
        theirs = [cols[beyond + 8 * c : beyond + 8 * c + 8, :] for c in range(3)]
        left, right = (mine, theirs) if at else (theirs, mine)
        ref = own if at else cols
        forces, rho = column_forces(
            layers, row + lax.axis_index("layer") * 8, row < 7, mats, inside, side, left, right,
            ref[COL_LAB : COL_LAB + 8, :], ref[COL_DT : COL_DT + 8, :], True,
        )
        for c in range(3):
            col_f[at, c] = forces[c]
        col_m[at] = rho
    for i in range(6):
        z = i + 1
        rate = DT / (LUMPED + with_columns(mass[z], col_m[0, z : z + 1, :], col_m[1, z : z + 1, :]))
        dtm[i] = rate
        for c in range(3):
            pull = with_columns(force[c, z], col_f[0, c, z : z + 1, :], col_f[1, c, z : z + 1, :])
            speed = v[c, z] - rate * pull
            v1[c, i] = speed
            u1[c, i] = u[c, z] + DT * speed


def first_contact(layers, own, near, far, opp, u1, v1, dtm, u_face, v_face, out, lists):
    @pl.when(lax.axis_index("layer") == layers // 2)
    def _():
        fill_lists(own, near, far, opp, lists)
        sol_y, sol_x = one_hots(lists[0:1, :])
        land_y, land_x = one_hots(lists[6:7, :])
        far_y, far_x = one_hots(lists[1:2, :])
        own_pad = own[PAD : PAD + 48, :]
        pads = {
            NEAR: near[PAD : PAD + 48, :],
            FAR1: far[MATE_PAD : MATE_PAD + 48, :],
            OWN: own_pad,
            FAR2: far[OWN_PAD : OWN_PAD + 48, :],
            OPP2: opp[MATE_PAD : MATE_PAD + 48, :],
        }
        far_pad = []
        for role in range(5):
            part = slice(128 * role, 128 * role + 128)
            far_pad.append(gather(pads[role], far_y[:, part], far_x[:, part]))
        on_bump = lists[2:3, :] * (jnp.concatenate(far_pad, axis=1) - lists[3:6, :])
        on_pad = lists[7:8, :] * (lists[8:11, :] - gather(own_pad, land_y, land_x))
        extra = (scatter(on_pad, land_y, land_x), scatter(on_bump, sol_y, sol_x))
        faces = []
        for face in (0, 1):
            new = []
            for c in range(3):
                change = dtm[2 + face] * extra[face][c]
                v_face[face, c] = v1[c, 2 + face] + change
                new.append(u1[c, 2 + face] + DT * change)
                u_face[face, c] = new[c]
            faces.append(jnp.concatenate(new, axis=0))
        lists[3:6, :] = gather(faces[1], sol_y, sol_x)
        lists[8:11, :] = gather(faces[0], land_y, land_x)
        for role in range(5):
            part = slice(128 * role, 128 * role + 128)
            for i, row in enumerate((3, 4, 5, 8, 9, 10)):
                at, half = 4 * role + i // 2, i % 2
                out[at : at + 1, 128 * half : 128 * half + 128] = lists[row : row + 1, part]


def first_step(
    blocks, layers,
    u, v, dt, lab, par, own, cols, zb, za, force, mass, in_f, in_m, ui, vi, dtmi, u_face, v_face,
    u1, v1, dtm, ends,
    col, col_lab, col_dt, col_f, col_m,
):
    layer, here = lax.axis_index("layer"), lax.axis_index("plane")
    mats = material_scalars(par)
    for c in range(3):
        for at, first, zu, zd in ((0, 0, ZU_CL, ZD_CL), (3, COL_BEYOND, ZU_CH, ZD_CH)):
            col[at, c, 0:2, :] = zb[zu + 2 * c : zu + 2 * c + 2, :]
            col[at, c, 2:3, :] = cols[first + 8 * c : first + 8 * c + 1, :]
            col[at, c, 3:4, :] = cols[first + 8 * c + 7 : first + 8 * c + 8, :]
            col[at, c, 4:6, :] = za[zd + 2 * c : zd + 2 * c + 2, :]
            col[at, c, 6:8, :] = jnp.zeros((2, 256), F32)
        for at, first, x in ((1, COL_LO, 0), (2, COL_HI, 15)):
            for zz in (0, 1):
                row = 16 * (2 * c + zz) + x
                col[at, c, zz : zz + 1, :] = zb[ZU_U + row : ZU_U + row + 1, :]
                col[at, c, 4 + zz : 5 + zz, :] = za[ZD_U + row : ZD_U + row + 1, :]
            col[at, c, 2:3, :] = own[first + 8 * c : first + 8 * c + 1, :]
            col[at, c, 3:4, :] = own[first + 8 * c + 7 : first + 8 * c + 8, :]
            col[at, c, 6:8, :] = jnp.zeros((2, 256), F32)
    for ref, first, zu, zd, zuf, zdf in (
        (col_lab, COL_LAB, ZU_CLAB, ZD_CLAB, ZU_LAB, ZD_LAB),
        (col_dt, COL_DT, ZU_CDT, ZD_CDT, ZU_DT, ZD_DT),
    ):
        for at in (0, 1):
            ref[at] = jnp.zeros((8, 256), F32)
        ref[0, 0:2, :] = zb[zu : zu + 2, :]
        ref[0, 3:4, :] = cols[first + 7 : first + 8, :]
        ref[0, 4:5, :] = za[zd : zd + 1, :]
        ref[1, 0:1, :] = zb[zuf + 15 : zuf + 16, :]
        ref[1, 1:2, :] = zb[zuf + 31 : zuf + 32, :]
        ref[1, 3:4, :] = own[COL_HI + first + 7 : COL_HI + first + 8, :]
        ref[1, 4:5, :] = za[zdf + 15 : zdf + 16, :]
    row = iota((8, 256), 0)
    zg = layer * 8 + jnp.where(row < 3, row - 2, row + 4)
    valid = (row < 5) & (row != 2)
    for at, inside, side in ((0, here > 0, 1), (1, here < blocks - 1, -1)):
        left = [col[2 * at, c] for c in range(3)]
        right = [col[2 * at + 1, c] for c in range(3)]
        forces, rho = column_forces(
            layers, zg, valid, mats, inside, side, left, right, col_lab[at], col_dt[at], True
        )
        for c in range(3):
            col_f[at, c] = forces[c]
        col_m[at] = rho

    def face(ref, row):
        return ref[row : row + 16, :]

    below = [[face(zb, ZU_U + 16 * (2 * c + zz)) for c in range(3)] for zz in (0, 1)]
    above = [[face(za, ZD_U + 16 * (2 * c + zz)) for c in range(3)] for zz in (0, 1)]
    first, last = [u[c, 0] for c in range(3)], [u[c, 7] for c in range(3)]
    low_f, low_m = two_layers(
        layers, layer * 8 - 2, mats, below + [first],
        (face(zb, ZU_LAB), face(zb, ZU_LAB + 16)), (face(zb, ZU_DT), face(zb, ZU_DT + 16)),
    )
    high_f, high_m = two_layers(
        layers, layer * 8 + 7, mats, [last] + above,
        (lab[7].astype(F32), face(za, ZD_LAB)), (dt[7], face(za, ZD_DT)),
    )
    v_below = [face(zb, ZU_V + 16 * c) for c in range(3)]
    v_above = [face(za, ZD_V + 16 * c) for c in range(3)]
    for i, z, at, pulls, weight, place, speeds in (
        (0, -1, 1, low_f[1], low_m[1], below[1], v_below),
        (1, 0, 2, low_f[2], low_m[2], first, [v[c, 0] for c in range(3)]),
        (8, 7, 3, high_f[0], high_m[0], last, [v[c, 7] for c in range(3)]),
        (9, 8, 4, high_f[1], high_m[1], above[0], v_above),
    ):
        inner = 0 <= z < 8
        edges = [col_m[side, at : at + 1, :] for side in (0, 1)]
        if inner:
            weight = weight + mass[z]
            edges = [edges[side] + in_m[side, z : z + 1, :] for side in (0, 1)]
        rate = DT / (LUMPED + with_columns(weight, *edges))
        dtm[i] = rate
        for c in range(3):
            pull = fold_node(pulls[c])
            edges = [col_f[side, c, at : at + 1, :] for side in (0, 1)]
            if inner:
                pull = pull + force[c, z]
                edges = [edges[side] + in_f[side, c, z : z + 1, :] for side in (0, 1)]
            speed = speeds[c] - rate * with_columns(pull, *edges)
            v1[c, i] = speed
            u1[c, i] = place[c] + DT * speed
    dtm[2:8] = dtmi[...]
    for c in range(3):
        u1[c, 2:8] = ui[c]
        v1[c, 2:8] = vi[c]

    @pl.when(layer == layers // 2)
    def _():
        for c in range(3):
            for i in (0, 1):
                u1[c, 4 + i] = u_face[i, c]
                v1[c, 4 + i] = v_face[i, c]

    for x, row in ((15, NEW_HI), (0, NEW_LO)):
        for c in range(3):
            ends[row + 10 * c : row + 10 * c + 8, :] = u1[c, 0:8, x, :]
            ends[row + 10 * c + 8 : row + 10 * c + 10, :] = u1[c, 8:10, x, :]
        ends[row + 30 : row + 32, :] = jnp.zeros((2, 256), F32)


def pack_new_cross(ends, values, mate, out):
    out[0:32, :] = jnp.where(on_even(), ends[NEW_LO : NEW_LO + 32, :], ends[NEW_HI : NEW_HI + 32, :])
    for row, src, role in ((CROSS_OWN, mate, OPP2), (CROSS_MATE, values, FAR1), (CROSS_ON, values, FAR2)):
        out[row : row + 4, :] = src[4 * role : 4 * role + 4, :]
    out[44:48, :] = jnp.zeros((4, 256), F32)


def pack_last(ends, far, out):
    out[0:32, :] = jnp.where(on_even(), ends[NEW_HI : NEW_HI + 32, :], ends[NEW_LO : NEW_LO + 32, :])
    out[32:48, :] = far[32:48, :]


def second_block(layers, u, dt, lab, par, zb, force, le, de, modes, saved):
    le[0] = zb[ZU_LAB + 16 : ZU_LAB + 32, :]
    de[0] = zb[ZU_DT + 16 : ZU_DT + 32, :]
    le[1:9] = lab[...].astype(F32)
    de[1:9] = dt[...]
    zbase = lax.axis_index("layer") * 8 - 1
    block_forces(layers, 9, 3, zbase, material_scalars(par), u, le, de, modes, saved, None, force, None)


def second_column(blocks, layers, at, src, own_row, dt, lab, par, cols, zb, ends, col, col_lab, col_dt):
    layer, here = lax.axis_index("layer"), lax.axis_index("plane")
    zeros = jnp.zeros((8, 256), F32)
    for c in range(3):
        col[0, c, 8:16, :] = zeros
        col[1, c, 8:16, :] = zeros
        col[0, c, 0:10, :] = src[10 * c : 10 * c + 10, :]
        col[1, c, 0:10, :] = ends[own_row + 10 * c : own_row + 10 * c + 10, :]
    for ref, field, first, zu, zuf in (
        (col_lab, lab, COL_LAB, ZU_CLAB, ZU_LAB),
        (col_dt, dt, COL_DT, ZU_CDT, ZU_DT),
    ):
        ref[8:16, :] = zeros
        if at:
            ref[0:1, :] = zb[zuf + 31 : zuf + 32, :]
            ref[1:9, :] = field[:, 15, :].astype(F32)
        else:
            ref[0:1, :] = zb[zu + 1 : zu + 2, :]
            ref[1:9, :] = cols[first : first + 8, :]
    zg = iota((16, 256), 0) + (layer * 8 - 1)
    inside = here < blocks - 1 if at else here > 0
    theirs, mine = [col[0, c] for c in range(3)], [col[1, c] for c in range(3)]
    left, right = (mine, theirs) if at else (theirs, mine)
    return column_forces(
        layers, zg, zg < layer * 8 + 8, material_scalars(par), inside, -1 if at else 1, left, right,
        col_lab[...], col_dt[...], False,
    )[0]


def second_step(
    blocks, layers,
    u, v, dtm, dt, lab, par, force, cols, zb, ends, far,
    u2, v2,
    col, col_lab, col_dt, col_f,
):
    for at in (0, 1):
        @pl.when(on_even() == (at == 0))
        def _():
            forces = second_column(
                blocks, layers, at, far, NEW_HI if at else NEW_LO, dt, lab, par, cols, zb, ends, col, col_lab, col_dt
            )
            for c in range(3):
                col_f[at, c] = forces[c]
                col_f[1 - at, c] = jnp.zeros((16, 256), F32)

    for z in range(8):
        e = z + 1
        rate = dtm[e]
        for c in range(3):
            pull = with_columns(force[c, e], col_f[0, c, e : e + 1, :], col_f[1, c, e : e + 1, :])
            speed = v[c, e] - rate * pull
            v2[c, z] = speed
            u2[c, z] = u[c, e] + DT * speed


def second_contact(
    blocks, layers,
    u_in, v_in, dtm, lists, mate, far, opp, dt, lab, par, cols, zb, ends,
    u2, v2,
    u, v, col, col_lab, col_dt, sems,
):
    u[...] = u_in[...]
    v[...] = v_in[...]
    for at in (0, 1):
        @pl.when(on_even() == (at == 1))
        def _():
            forces = second_column(
                blocks, layers, at, opp, NEW_HI if at else NEW_LO, dt, lab, par, cols, zb, ends, col, col_lab, col_dt
            )
            x = 15 if at else 0
            rate = dtm[1:9, x, :]
            for c in range(3):
                change = rate * forces[c][1:9]
                v[c, :, x, :] = v[c, :, x, :] - change
                u[c, :, x, :] = u[c, :, x, :] - DT * change

    copies = []
    for src, dst in ((u, u2), (v, v2)):
        for first, last in ((0, 3), (5, 8)):
            copies.append(
                pltpu.make_async_copy(src.at[:, first:last], dst.at[:, first:last], sems.at[len(copies)])
            )
    for copy in copies:
        copy.start()

    @pl.when(lax.axis_index("layer") == layers // 2)
    def _():
        sol_y, sol_x = one_hots(lists[0:1, :])
        land_y, land_x = one_hots(lists[6:7, :])

        def values(i):
            half = slice(128 * (i % 2), 128 * (i % 2) + 128)
            own_row = (3, 4, 5, 8, 9, 10)[i]
            places = (
                (mate, 4 * NEAR), (far, CROSS_MATE), None, (far, CROSS_OWN), (opp, CROSS_ON)
            )
            parts = [
                lists[own_row : own_row + 1, 256:384] if place is None
                else place[0][place[1] + i // 2 : place[1] + i // 2 + 1, half]
                for place in places
            ]
            return jnp.concatenate(parts, axis=1)

        far_bump = jnp.concatenate([values(i) for i in range(3)], axis=0)
        far_pad = jnp.concatenate([values(i) for i in range(3, 6)], axis=0)
        on_bump = lists[2:3, :] * (far_pad - lists[3:6, :])
        on_pad = lists[7:8, :] * (far_bump - lists[8:11, :])
        extra = (scatter(on_pad, land_y, land_x), scatter(on_bump, sol_y, sol_x))
        for c in range(3):
            for face in (0, 1):
                change = dtm[4 + face] * extra[face][c]
                u[c, 3 + face] = u[c, 3 + face] + DT * change
                v[c, 3 + face] = v[c, 3 + face] + change

    for i, (src, dst) in enumerate(((u, u2), (v, v2))):
        copy = pltpu.make_async_copy(src.at[:, 3:5], dst.at[:, 3:5], sems.at[4 + i])
        copy.start()
        copies.append(copy)
    for copy in copies:
        copy.wait()


VM = pl.BlockSpec(memory_space=pltpu.VMEM)
SM = pl.BlockSpec(memory_space=pltpu.SMEM)
HBM = pl.BlockSpec(memory_space=pltpu.HBM)


def call(kernel, in_specs, outs, scratch, name, flops, vmem=32, out_spec=VM):
    return pl.pallas_call(
        kernel,
        out_shape=[jax.ShapeDtypeStruct(shape, F32) for shape in outs],
        in_specs=in_specs,
        out_specs=[out_spec] * len(outs),
        scratch_shapes=[pltpu.VMEM(s, F32) if isinstance(s, tuple) else s for s in scratch],
        compiler_params=pltpu.CompilerParams(vmem_limit_bytes=vmem * 1024 * 1024),
        cost_estimate=pl.CostEstimate(flops=flops, bytes_accessed=2_000_000, transcendentals=0),
        name=name,
    )


def local(u, v, dt, lab, par, sol, land, stiff, tally):
    blocks, layers = lax.axis_size("plane"), lax.axis_size("layer")
    swaps = [(s, s ^ 1) for s in range(blocks)]
    crossings = [(s, s + 2 - 4 * (s % 2)) for s in range(blocks) if 0 <= s + 2 - 4 * (s % 2) < blocks]
    face_swaps = [(a * layers + layers // 2, b * layers + layers // 2) for a, b in swaps]

    def along_layer(value, steps):
        pairs = [(s, s + steps) for s in range(layers) if 0 <= s + steps < layers]
        return lax.ppermute(value, "layer", pairs)

    own = call(
        functools.partial(pack_export, blocks, layers),
        [HBM] * 7,
        [(EXPORT_ROWS, 256)],
        [u.shape, dt.shape, pltpu.VMEM(lab.shape, jnp.int32)]
        + [pltpu.VMEM((5, 1, 128), jnp.int32)] * 2
        + [(5, 1, 128), pltpu.SMEM((1, 5), jnp.int32), pltpu.VMEM((8, 640), jnp.int32)]
        + [pltpu.VMEM((256, 640), BF16), (16, 640), pltpu.SemaphoreType.DMA((7,))],
        "pack_export",
        100_000,
        63,
    )(u, dt, lab, sol.reshape(5, 1, 128), land.reshape(5, 1, 128), stiff.reshape(5, 1, 128), tally)[0]
    near = lax.ppermute(own, "plane", swaps)
    own = call(stage, [HBM], [own.shape], [pltpu.SemaphoreType.DMA], "stage", 100_000)(own)[0]
    cross = call(pack_cross, [VM] * 2, [(CROSS_ROWS, 256)], [], "pack_cross", 100_000)(own, near)[0]
    far = lax.ppermute(cross, "plane", crossings)
    modes = [(12, 16, 256), (12, 16, 256)]
    plane = (16, 256)
    force, mass = call(
        functools.partial(first_block, layers),
        [VM] * 3 + [SM],
        [(3, 8, 16, 256), (8, 16, 256)],
        modes + [plane],
        "first_block",
        50_000_000,
    )(u, dt, lab, par)
    far, force, mass = lax.optimization_barrier((far, force, mass))
    up, dn, cols = call(
        pack_layer, [VM] * 6, [(ZU_ROWS, 256), (ZD_ROWS, 256), (COLS_ROWS, 256)], [], "pack_layer", 100_000
    )(u, v, dt, lab, near, far)
    zb, za = along_layer(up, 1), along_layer(dn, -1)
    opp = lax.ppermute(far, ("plane", "layer"), face_swaps)
    u1, v1, dtm, in_f, in_m = call(
        functools.partial(first_inner, blocks, layers),
        [VM] * 2 + [SM] + [VM] * 4,
        [(3, 6, 16, 256), (3, 6, 16, 256), (6, 16, 256), (2, 3, 8, 256), (2, 8, 256)],
        [],
        "first_inner",
        10_000_000,
    )(u, v, par, own, cols, force, mass)
    opp, u1, v1 = lax.optimization_barrier((opp, u1, v1))
    u_face, v_face, values, lists = call(
        functools.partial(first_contact, layers),
        [VM] * 7,
        [(2, 3, 16, 256), (2, 3, 16, 256), (VALUES_ROWS, 256), (16, 640)],
        [],
        "first_contact",
        10_000_000,
    )(own, near, far, opp, u1, v1, dtm)
    mate = lax.ppermute(values, ("plane", "layer"), face_swaps)

    two = (2, 8, 256)
    u1, v1, dtm, ends = call(
        functools.partial(first_step, blocks, layers),
        [VM] * 4 + [SM] + [VM] * 13,
        [(3, 10, 16, 256), (3, 10, 16, 256), (10, 16, 256), (NEW_ROWS, 256)],
        [(4, 3, 8, 256), two, two, (2, 3, 8, 256), two],
        "first_step",
        20_000_000,
    )(u, v, dt, lab, par, own, cols, zb, za, force, mass, in_f, in_m, u1, v1, dtm, u_face, v_face)
    across = [(s, s + 1) for s in range(1, blocks - 1, 2)] + [(s, s - 1) for s in range(2, blocks, 2)]
    cross = call(pack_new_cross, [VM] * 3, [(NEW_CROSS_ROWS, 256)], [], "pack_new_cross", 100_000)(ends, values, mate)[0]
    far = lax.ppermute(cross, "plane", across)
    force = call(
        functools.partial(second_block, layers),
        [VM] * 3 + [SM, VM],
        [(3, 10, 16, 256)],
        [(9, 16, 256), (9, 16, 256)] + modes,
        "second_block",
        50_000_000,
    )(u1, dt, lab, par, zb)[0]
    far, force = lax.optimization_barrier((far, force))
    last = call(pack_last, [VM] * 2, [(NEW_CROSS_ROWS, 256)], [], "pack_last", 100_000)(ends, far)[0]
    opp = lax.ppermute(last, "plane", swaps)
    column = [(2, 3, 16, 256), (16, 256), (16, 256)]
    u2, v2 = call(
        functools.partial(second_step, blocks, layers),
        [VM] * 5 + [SM] + [VM] * 5,
        [(3, 8, 16, 256)] * 2,
        column + [(2, 3, 16, 256)],
        "second_step",
        20_000_000,
    )(u1, v1, dtm, dt, lab, par, force, cols, zb, ends, far)
    return tuple(
        call(
            functools.partial(second_contact, blocks, layers),
            [VM] * 9 + [SM] + [VM] * 3,
            [(3, 8, 16, 256)] * 2,
            [(3, 8, 16, 256)] * 2 + column + [pltpu.SemaphoreType.DMA((6,))],
            "second_contact",
            10_000_000,
            out_spec=HBM,
        )(u2, v2, dtm, lists, mate, far, opp, dt, lab, par, cols, zb, ends)
    )


def solution(mesh):
    in_specs = (
        P(None, "layer", "plane", None),
        P(None, "layer", "plane", None),
        P("layer", "plane", None),
        P("layer", "plane", None),
        P(),
        P("plane", None, None),
        P("plane", None, None),
        P("plane", None, None),
        P("plane", None),
    )
    out_specs = (P(None, "layer", "plane", None), P(None, "layer", "plane", None))
    return jax.shard_map(local, mesh=mesh, in_specs=in_specs, out_specs=out_specs, check_vma=False)
```

```python
import functools

import jax
import jax.numpy as jnp
from jax import lax
from jax.experimental import pallas as pl
from jax.experimental.pallas import tpu as pltpu
from jax.sharding import PartitionSpec as P

DT = 0.05
LUMPED = 0.25
F32 = jnp.float32
BF16 = jnp.bfloat16
QUADS = ((0, 0), (0, 1), (1, 0), (1, 1))

COL_HI, COL_LO, LISTS, PAD, EXPORT_ROWS = 0, 40, 64, 88, 136
OWN_OPP2, MATE_FAR1, OWN_PAD, MATE_PAD, CROSS_ROWS = 40, 44, 48, 96, 144
SKIP_LIST, SKIP_PAD, SKIP_ROWS = 0, 8, 232
COL_LAB, COL_DT, COL_BEYOND, COLS_ROWS = 24, 32, 40, 64
ZU_U, ZU_V, ZU_LAB, ZU_DT, ZU_CL, ZU_CH, ZU_CLAB, ZU_CDT, ZU_ROWS = 0, 96, 144, 176, 208, 214, 220, 222, 224
ZD_U, ZD_V, ZD_LAB, ZD_DT, ZD_CL, ZD_CH, ZD_CLAB, ZD_CDT, ZD_ROWS = 0, 96, 144, 160, 176, 182, 188, 189, 192
NEW_HI, NEW_LO, NEW_ROWS, VALUES_ROWS = 0, 32, 64, 24
CROSS_OWN, CROSS_MATE, CROSS_ON, NEW_CROSS_ROWS = 32, 36, 40, 48
NEAR, FAR1, OWN, FAR2, OPP2 = range(5)
OFFSETS = (1, -1, 0, -2, 2)


def iota(shape, dim):
    return lax.broadcasted_iota(jnp.int32, shape, dim)


def on_even():
    return lax.rem(lax.axis_index("plane"), 2) == 0


def role_offset(role):
    return jnp.where(on_even(), OFFSETS[role], -OFFSETS[role])


def pack_export(
    blocks, layers,
    u_hbm, dt_hbm, lab_hbm, sol_hbm, land_hbm, stiff_hbm, tally_hbm,
    out,
    u, dt, lab, sol, land, stiff, tally, pos, ohy, ohx, sems,
):
    copies = [
        pltpu.make_async_copy(src, dst, sems.at[i])
        for i, (src, dst) in enumerate(
            (
                (u_hbm, u), (dt_hbm, dt), (lab_hbm, lab), (sol_hbm, sol),
                (land_hbm, land), (stiff_hbm, stiff), (tally_hbm, tally),
            )
        )
    ]
    for copy in copies:
        copy.start()
    for copy in copies[3:]:
        copy.wait()
    pad_z = u.shape[1] // 2 - 1
    here = lax.axis_index("plane")
    on_face = lax.axis_index("layer") == layers // 2

    @pl.when(on_face)
    def _():
        out[LISTS : LISTS + 24, :] = jnp.zeros((24, 256), F32)
        for k in range(5):
            row = LISTS + 4 * k
            target = here + (k - 2)
            count = jnp.where((target >= 0) & (target < blocks), tally[0, k], 0)
            live = iota((1, 128), 1) < count
            out[row : row + 1, 0:128] = sol[k].astype(F32)
            out[row : row + 1, 128:256] = land[k].astype(F32)
            out[row + 1 : row + 2, 0:128] = jnp.where(live, stiff[k], 0.0)
            pos[0:1, 128 * k : 128 * k + 128] = sol[k]
        ohy[...], ohx[...] = one_hots(pos[0:1, :])

    for copy in copies[:3]:
        copy.wait()
    for x, row in ((15, COL_HI), (0, COL_LO)):
        for c in range(3):
            out[row + 8 * c : row + 8 * c + 8, :] = u[c, :, x, :]
    out[COL_HI + COL_LAB : COL_HI + COL_LAB + 8, :] = lab[:, 15, :].astype(F32)
    out[COL_HI + COL_DT : COL_HI + COL_DT + 8, :] = dt[:, 15, :]

    @pl.when(on_face)
    def _():
        bump = gather(jnp.concatenate([u[c, pad_z + 1] for c in range(3)], axis=0), ohy[...], ohx[...])
        for k in range(5):
            row, cols = LISTS + 4 * k, slice(128 * k, 128 * k + 128)
            out[row + 1 : row + 2, 128:256] = bump[0:1, cols]
            out[row + 2 : row + 3, 0:128] = bump[1:2, cols]
            out[row + 2 : row + 3, 128:256] = bump[2:3, cols]
        for c in range(3):
            out[PAD + 16 * c : PAD + 16 * c + 16, :] = u[c, pad_z]


def stage(src, dst, sem):
    copy = pltpu.make_async_copy(src, dst, sem)
    copy.start()
    copy.wait()


def pack_cross(own, mate, out, skip):
    even = on_even()

    def bucket(ref, if_even, if_odd):
        a, b = LISTS + 4 * if_even, LISTS + 4 * if_odd
        return jnp.where(even, ref[a : a + 4, :], ref[b : b + 4, :])

    out[24:40, :] = mate[COL_HI + 24 : COL_HI + 40, :]
    out[0:24, :] = jnp.where(even, mate[COL_HI : COL_HI + 24, :], mate[COL_LO : COL_LO + 24, :])
    out[OWN_OPP2 : OWN_OPP2 + 4, :] = bucket(own, 4, 0)
    out[MATE_FAR1 : MATE_FAR1 + 4, :] = bucket(mate, 3, 1)
    out[OWN_PAD : OWN_PAD + 48, :] = own[PAD : PAD + 48, :]
    out[MATE_PAD : MATE_PAD + 48, :] = mate[PAD : PAD + 48, :]
    skip[SKIP_LIST : SKIP_LIST + 4, :] = bucket(own, 0, 4)
    skip[SKIP_LIST + 4 : SKIP_PAD, :] = jnp.zeros((4, 256), F32)
    skip[SKIP_PAD : SKIP_PAD + 48, :] = own[PAD : PAD + 48, :]


def pack_layer(u, v, dt, lab, near, far, up, dn, cols):
    even = on_even()
    cols[0:40, :] = jnp.where(even, far[0:40, :], near[COL_HI : COL_HI + 40, :])
    cols[COL_BEYOND : COL_BEYOND + 24, :] = jnp.where(even, near[COL_LO : COL_LO + 24, :], far[0:24, :])
    for c in range(3):
        for zz in (0, 1):
            row = 16 * (2 * c + zz)
            up[ZU_U + row : ZU_U + row + 16, :] = u[c, 6 + zz]
            dn[ZD_U + row : ZD_U + row + 16, :] = u[c, zz]
        up[ZU_V + 16 * c : ZU_V + 16 * c + 16, :] = v[c, 7]
        dn[ZD_V + 16 * c : ZD_V + 16 * c + 16, :] = v[c, 0]
        lo, hi = 8 * c, COL_BEYOND + 8 * c
        up[ZU_CL + 2 * c : ZU_CL + 2 * c + 2, :] = cols[lo + 6 : lo + 8, :]
        up[ZU_CH + 2 * c : ZU_CH + 2 * c + 2, :] = cols[hi + 6 : hi + 8, :]
        dn[ZD_CL + 2 * c : ZD_CL + 2 * c + 2, :] = cols[lo : lo + 2, :]
        dn[ZD_CH + 2 * c : ZD_CH + 2 * c + 2, :] = cols[hi : hi + 2, :]
    for zz in (0, 1):
        up[ZU_LAB + 16 * zz : ZU_LAB + 16 * zz + 16, :] = lab[6 + zz].astype(F32)
        up[ZU_DT + 16 * zz : ZU_DT + 16 * zz + 16, :] = dt[6 + zz]
    up[ZU_CLAB : ZU_CLAB + 2, :] = cols[COL_LAB + 6 : COL_LAB + 8, :]
    up[ZU_CDT : ZU_CDT + 2, :] = cols[COL_DT + 6 : COL_DT + 8, :]
    dn[ZD_LAB : ZD_LAB + 16, :] = lab[0].astype(F32)
    dn[ZD_DT : ZD_DT + 16, :] = dt[0]
    dn[ZD_CLAB : ZD_CLAB + 1, :] = cols[COL_LAB : COL_LAB + 1, :]
    dn[ZD_CDT : ZD_CDT + 1, :] = cols[COL_DT : COL_DT + 1, :]
    dn[ZD_CDT + 1 : ZD_ROWS, :] = jnp.zeros((ZD_ROWS - ZD_CDT - 1, 256), F32)


def material_scalars(par):
    out = []
    for m in range(4):
        lam, mu, alpha, rho = par[0, m], par[1, m], par[2, m], par[3, m]
        out.append(
            (
                lam * (1.0 / 16.0),
                mu * (1.0 / 16.0),
                (lam + 4.0 * mu) * (1.0 / 144.0),
                (3.0 * lam + 2.0 * mu) * alpha * 0.25,
                rho * 0.125,
            )
        )
    return out


def cell_fields(mats, lab, dt, mask, with_mass):
    is0, is1, is2 = lab == 0.0, lab == 1.0, lab == 2.0

    def pick(i):
        rest = jnp.where(is2, mats[2][i], mats[3][i])
        return jnp.where(is0, mats[0][i], jnp.where(is1, mats[1][i], rest)) * mask

    return pick(0), pick(1), pick(2), pick(3) * dt, pick(4) if with_mass else None


def plane_modes(u, ux):
    s, d = u + ux, ux - u
    sy, dy = pltpu.roll(s, 255, 1), pltpu.roll(d, 255, 1)
    return [s + sy, sy - s, d + dy, dy - d]


def cell_forces(lower, upper, l1, m1, k3, th):
    z, x, y = (
        {
            (i, j, k): (upper[c][q] - lower[c][q]) if i else (upper[c][q] + lower[c][q])
            for q, (j, k) in enumerate(QUADS)
            for i in (0, 1)
            if i + j + k
        }
        for c in range(3)
    )
    l2, m2 = l1 * (1.0 / 3.0), m1 * (1.0 / 3.0)
    p0 = l1 * (z[1, 0, 0] + x[0, 1, 0] + y[0, 0, 1]) - th
    m1x2 = m1 + m1
    zx = m1 * (x[1, 0, 0] + z[0, 1, 0])
    zy = m1 * (y[1, 0, 0] + z[0, 0, 1])
    xy = m1 * (y[0, 1, 0] + x[0, 0, 1])
    pz = l2 * (x[1, 1, 0] + y[1, 0, 1])
    px = l2 * (z[1, 1, 0] + y[0, 1, 1])
    py = l2 * (z[1, 0, 1] + x[0, 1, 1])
    tw = z[0, 1, 1] + x[1, 0, 1] + y[1, 1, 0]
    fz = {
        (1, 0, 0): p0 + m1x2 * z[1, 0, 0],
        (0, 1, 0): zx,
        (0, 0, 1): zy,
        (1, 1, 0): px + m1 * z[1, 1, 0],
        (1, 0, 1): py + m1 * z[1, 0, 1],
        (0, 1, 1): m2 * (tw + z[0, 1, 1]),
        (1, 1, 1): k3 * z[1, 1, 1],
    }
    fx = {
        (0, 1, 0): p0 + m1x2 * x[0, 1, 0],
        (1, 0, 0): zx,
        (0, 0, 1): xy,
        (1, 1, 0): pz + m1 * x[1, 1, 0],
        (0, 1, 1): py + m1 * x[0, 1, 1],
        (1, 0, 1): m2 * (tw + x[1, 0, 1]),
        (1, 1, 1): k3 * x[1, 1, 1],
    }
    fy = {
        (0, 0, 1): p0 + m1x2 * y[0, 0, 1],
        (1, 0, 0): zy,
        (0, 1, 0): xy,
        (1, 0, 1): pz + m1 * y[1, 0, 1],
        (0, 1, 1): px + m1 * y[0, 1, 1],
        (1, 1, 0): m2 * (tw + y[1, 1, 0]),
        (1, 1, 1): k3 * y[1, 1, 1],
    }
    low, high = [], []
    for f in (fz, fx, fy):
        low_c, high_c = [], []
        for j, k in QUADS:
            d = f[1, j, k]
            if j + k:
                s = f[0, j, k]
                low_c.append(s - d)
                high_c.append(s + d)
            else:
                low_c.append(-d)
                high_c.append(d)
        low.append(low_c)
        high.append(high_c)
    return low, high


def fold_y(a, b):
    return (a - b) + pltpu.roll(a + b, 1, 1)


def column_forces(layers, zg, valid, mats, inside, side, left, right, lab, dt, with_mass):
    rows = lab.shape[0]
    shape = (rows, 256)
    ok = (zg >= 0) & (zg <= layers * 8 - 2) & (zg != layers // 2 * 8 + 3) & (iota(shape, 1) < 255)
    mask = jnp.where(ok & valid & inside, 1.0, 0.0)
    l1, m1, k3, th, rho = cell_fields(mats, lab, dt, mask, with_mass)
    lower = [plane_modes(left[c], right[c]) for c in range(3)]
    upper = [[pltpu.roll(a, rows - 1, 0) for a in comp] for comp in lower]
    low, high = cell_forces(lower, upper, l1, m1, k3, th)
    forces = []
    for c in range(3):
        node = [low[c][q] + pltpu.roll(high[c][q], 1, 0) for q in range(4)]
        t0, t1 = fold_y(node[0], node[1]), fold_y(node[2], node[3])
        forces.append(t0 + side * t1)
    if with_mass:
        rho = rho + pltpu.roll(rho, 1, 1)
        rho = rho + pltpu.roll(rho, 1, 0)
    return forces, rho


def block_forces(layers, cells, group, zbase, mats, u, lab, dt, modes, saved, saved_m, force, mass):
    shape = (16, 256)
    row, lane = iota(shape, 0), iota(shape, 1)
    in_plane = jnp.where((lane < 255) & (row < 15), 1.0, 0.0)

    def forward(e, c):
        a = u[c, e]
        return plane_modes(a, pltpu.roll(a, 15, 0))

    for c in range(3):
        for q, value in enumerate(forward(0, c)):
            modes[4 * c + q] = value
            saved[4 * c + q] = jnp.zeros(shape, F32)
    if mass is not None:
        saved_m[...] = jnp.zeros(shape, F32)

    def fold(e, node):
        for c in range(3):
            t0, t1 = fold_y(node[c][0], node[c][1]), fold_y(node[c][2], node[c][3])
            force[c, e] = (t0 - t1) + pltpu.roll(t0 + t1, 1, 0)

    def body(i, carry):
        lower = [[modes[4 * c + q] for q in range(4)] for c in range(3)]
        held = [[saved[4 * c + q] for q in range(4)] for c in range(3)]
        held_m = None if mass is None else saved_m[...]
        for g in range(group):
            e = i * group + g
            zg = zbase + e
            ok = (zg >= 0) & (zg <= layers * 8 - 2) & (zg != layers // 2 * 8 + 3)
            mask = in_plane * jnp.where(ok, 1.0, 0.0)
            l1, m1, k3, th, rho = cell_fields(mats, lab[e].astype(F32), dt[e], mask, mass is not None)
            upper = [forward(e + 1, c) for c in range(3)]
            low, high = cell_forces(lower, upper, l1, m1, k3, th)
            fold(e, [[low[c][q] + held[c][q] for q in range(4)] for c in range(3)])
            lower, held = upper, high
            if mass is not None:
                rho = rho + pltpu.roll(rho, 1, 1)
                rho = rho + pltpu.roll(rho, 1, 0)
                mass[e] = rho + held_m
                held_m = rho
        for c in range(3):
            for q in range(4):
                modes[4 * c + q] = lower[c][q]
                saved[4 * c + q] = held[c][q]
        if mass is not None:
            saved_m[...] = held_m
        return carry

    lax.fori_loop(0, cells // group, body, 0)
    fold(cells, [[saved[4 * c + q] for q in range(4)] for c in range(3)])
    if mass is not None:
        mass[cells] = saved_m[...]


def two_layers(layers, z, mats, nodes, lab, dt):
    shape = (16, 256)
    in_plane = jnp.where((iota(shape, 1) < 255) & (iota(shape, 0) < 15), 1.0, 0.0)
    modes = [[plane_modes(a, pltpu.roll(a, 15, 0)) for a in node] for node in nodes]
    parts, masses = [], []
    for i in (0, 1):
        zg = z + i
        ok = (zg >= 0) & (zg <= layers * 8 - 2) & (zg != layers // 2 * 8 + 3)
        mask = in_plane * jnp.where(ok, 1.0, 0.0)
        l1, m1, k3, th, rho = cell_fields(mats, lab[i], dt[i], mask, True)
        parts.append(cell_forces(modes[i], modes[i + 1], l1, m1, k3, th))
        rho = rho + pltpu.roll(rho, 1, 1)
        masses.append(rho + pltpu.roll(rho, 1, 0))
    (low0, high0), (low1, high1) = parts
    middle = [[high0[c][q] + low1[c][q] for q in range(4)] for c in range(3)]
    return (low0, middle, high1), (masses[0], masses[0] + masses[1], masses[1])


def fold_node(node):
    t0, t1 = fold_y(node[0], node[1]), fold_y(node[2], node[3])
    return (t0 - t1) + pltpu.roll(t0 + t1, 1, 0)


def with_columns(a, first, last):
    row = iota((8, 256), 0)
    top = a[0:8] + jnp.where(row == 0, jnp.broadcast_to(first, (8, 256)), 0.0)
    bottom = a[8:16] + jnp.where(row == 7, jnp.broadcast_to(last, (8, 256)), 0.0)
    return jnp.concatenate([top, bottom], axis=0)


def split3(a):
    hi = a.astype(BF16)
    rest = a - hi.astype(F32)
    mid = rest.astype(BF16)
    lo = (rest - mid.astype(F32)).astype(BF16)
    return jnp.concatenate([hi, mid, lo], axis=0)


def join3(a):
    n = a.shape[0] // 3
    return (a[:n] + a[n : 2 * n]) + a[2 * n :]


def one_hots(position):
    pos = position.astype(jnp.int32)
    n = pos.shape[1]
    y, x = pos & 255, pos >> 8
    ohy = jnp.where(iota((256, n), 0) == y, 1.0, 0.0).astype(BF16)
    ohx = jnp.where(iota((16, n), 0) == x, 1.0, 0.0)
    return ohy, ohx


def gather(face, ohy, ohx):
    n = ohx.shape[1]
    rows = join3(jnp.dot(split3(face), ohy, preferred_element_type=F32))
    return jnp.sum(rows.reshape(3, 16, n) * ohx[None], axis=1)


def scatter(values, ohy, ohx):
    n = ohx.shape[1]
    rows = (values[:, None, :] * ohx[None]).reshape(48, n)
    out = lax.dot_general(split3(rows), ohy, (((1,), (1,)), ((), ())), preferred_element_type=F32)
    return join3(out).reshape(3, 16, 256)


def fill_lists(own, near, far, opp, lists):
    sources = {
        NEAR: (near, LISTS + 4 * (2 - role_offset(NEAR))),
        FAR1: (far, MATE_FAR1),
        OWN: (own, LISTS + 8),
        FAR2: (far, OWN_OPP2),
        OPP2: (opp, SKIP_LIST),
    }
    for role, (ref, base) in sources.items():
        cols = slice(128 * role, 128 * role + 128)
        row = LISTS + 4 * (2 + role_offset(role))
        for i in range(3):
            mine, other = own[pl.ds(row + i, 1), :], ref[pl.ds(base + i, 1), :]
            for half in (0, 1):
                part = slice(128 * half, 128 * half + 128)
                lists[2 * i + half : 2 * i + half + 1, cols] = mine[:, part]
                if i + half:
                    lists[5 + 2 * i + half : 6 + 2 * i + half, cols] = other[:, part]


def first_block(layers, u, dt, lab, par, force, mass, modes, saved, saved_m):
    zbase = lax.axis_index("layer") * 8
    block_forces(layers, 7, 7, zbase, material_scalars(par), u, lab, dt, modes, saved, saved_m, force, mass)


def first_inner(
    blocks, layers, u, v, par, own, cols, force, mass, u1, v1, dtm, col_f, col_m
):
    here = lax.axis_index("plane")
    mats = material_scalars(par)
    row = iota((8, 256), 0)
    for at, inside, side in ((0, here > 0, 1), (1, here < blocks - 1, -1)):
        first = COL_LO if at == 0 else COL_HI
        mine = [own[first + 8 * c : first + 8 * c + 8, :] for c in range(3)]
        beyond = COL_BEYOND if at else 0
        theirs = [cols[beyond + 8 * c : beyond + 8 * c + 8, :] for c in range(3)]
        left, right = (mine, theirs) if at else (theirs, mine)
        ref = own if at else cols
        forces, rho = column_forces(
            layers, row + lax.axis_index("layer") * 8, row < 7, mats, inside, side, left, right,
            ref[COL_LAB : COL_LAB + 8, :], ref[COL_DT : COL_DT + 8, :], True,
        )
        for c in range(3):
            col_f[at, c] = forces[c]
        col_m[at] = rho
    for i in range(6):
        z = i + 1
        rate = DT / (LUMPED + with_columns(mass[z], col_m[0, z : z + 1, :], col_m[1, z : z + 1, :]))
        dtm[i] = rate
        for c in range(3):
            pull = with_columns(force[c, z], col_f[0, c, z : z + 1, :], col_f[1, c, z : z + 1, :])
            speed = v[c, z] - rate * pull
            v1[c, i] = speed
            u1[c, i] = u[c, z] + DT * speed


def first_contact(layers, own, near, far, opp, u1, v1, dtm, u_face, v_face, out, lists):
    @pl.when(lax.axis_index("layer") == layers // 2)
    def _():
        fill_lists(own, near, far, opp, lists)
        sol_y, sol_x = one_hots(lists[0:1, :])
        land_y, land_x = one_hots(lists[6:7, :])
        far_y, far_x = one_hots(lists[1:2, :])
        own_pad = own[PAD : PAD + 48, :]
        pads = {
            NEAR: near[PAD : PAD + 48, :],
            FAR1: far[MATE_PAD : MATE_PAD + 48, :],
            OWN: own_pad,
            FAR2: far[OWN_PAD : OWN_PAD + 48, :],
            OPP2: opp[SKIP_PAD : SKIP_PAD + 48, :],
        }
        far_pad = []
        for role in range(5):
            part = slice(128 * role, 128 * role + 128)
            far_pad.append(gather(pads[role], far_y[:, part], far_x[:, part]))
        on_bump = lists[2:3, :] * (jnp.concatenate(far_pad, axis=1) - lists[3:6, :])
        on_pad = lists[7:8, :] * (lists[8:11, :] - gather(own_pad, land_y, land_x))
        extra = (scatter(on_pad, land_y, land_x), scatter(on_bump, sol_y, sol_x))
        faces = []
        for face in (0, 1):
            new = []
            for c in range(3):
                change = dtm[2 + face] * extra[face][c]
                v_face[face, c] = v1[c, 2 + face] + change
                new.append(u1[c, 2 + face] + DT * change)
                u_face[face, c] = new[c]
            faces.append(jnp.concatenate(new, axis=0))
        lists[3:6, :] = gather(faces[1], sol_y, sol_x)
        lists[8:11, :] = gather(faces[0], land_y, land_x)
        for role in range(5):
            part = slice(128 * role, 128 * role + 128)
            for i, row in enumerate((3, 4, 5, 8, 9, 10)):
                at, half = 4 * role + i // 2, i % 2
                out[at : at + 1, 128 * half : 128 * half + 128] = lists[row : row + 1, part]


def first_step(
    blocks, layers,
    u, v, dt, lab, par, own, cols, zb, za, force, mass, in_f, in_m, ui, vi, dtmi, u_face, v_face,
    u1, v1, dtm, ends,
    col, col_lab, col_dt, col_f, col_m,
):
    layer, here = lax.axis_index("layer"), lax.axis_index("plane")
    mats = material_scalars(par)
    for c in range(3):
        for at, first, zu, zd in ((0, 0, ZU_CL, ZD_CL), (3, COL_BEYOND, ZU_CH, ZD_CH)):
            col[at, c, 0:2, :] = zb[zu + 2 * c : zu + 2 * c + 2, :]
            col[at, c, 2:3, :] = cols[first + 8 * c : first + 8 * c + 1, :]
            col[at, c, 3:4, :] = cols[first + 8 * c + 7 : first + 8 * c + 8, :]
            col[at, c, 4:6, :] = za[zd + 2 * c : zd + 2 * c + 2, :]
            col[at, c, 6:8, :] = jnp.zeros((2, 256), F32)
        for at, first, x in ((1, COL_LO, 0), (2, COL_HI, 15)):
            for zz in (0, 1):
                row = 16 * (2 * c + zz) + x
                col[at, c, zz : zz + 1, :] = zb[ZU_U + row : ZU_U + row + 1, :]
                col[at, c, 4 + zz : 5 + zz, :] = za[ZD_U + row : ZD_U + row + 1, :]
            col[at, c, 2:3, :] = own[first + 8 * c : first + 8 * c + 1, :]
            col[at, c, 3:4, :] = own[first + 8 * c + 7 : first + 8 * c + 8, :]
            col[at, c, 6:8, :] = jnp.zeros((2, 256), F32)
    for ref, first, zu, zd, zuf, zdf in (
        (col_lab, COL_LAB, ZU_CLAB, ZD_CLAB, ZU_LAB, ZD_LAB),
        (col_dt, COL_DT, ZU_CDT, ZD_CDT, ZU_DT, ZD_DT),
    ):
        for at in (0, 1):
            ref[at] = jnp.zeros((8, 256), F32)
        ref[0, 0:2, :] = zb[zu : zu + 2, :]
        ref[0, 3:4, :] = cols[first + 7 : first + 8, :]
        ref[0, 4:5, :] = za[zd : zd + 1, :]
        ref[1, 0:1, :] = zb[zuf + 15 : zuf + 16, :]
        ref[1, 1:2, :] = zb[zuf + 31 : zuf + 32, :]
        ref[1, 3:4, :] = own[COL_HI + first + 7 : COL_HI + first + 8, :]
        ref[1, 4:5, :] = za[zdf + 15 : zdf + 16, :]
    row = iota((8, 256), 0)
    zg = layer * 8 + jnp.where(row < 3, row - 2, row + 4)
    valid = (row < 5) & (row != 2)
    for at, inside, side in ((0, here > 0, 1), (1, here < blocks - 1, -1)):
        left = [col[2 * at, c] for c in range(3)]
        right = [col[2 * at + 1, c] for c in range(3)]
        forces, rho = column_forces(
            layers, zg, valid, mats, inside, side, left, right, col_lab[at], col_dt[at], True
        )
        for c in range(3):
            col_f[at, c] = forces[c]
        col_m[at] = rho

    def face(ref, row):
        return ref[row : row + 16, :]

    below = [[face(zb, ZU_U + 16 * (2 * c + zz)) for c in range(3)] for zz in (0, 1)]
    above = [[face(za, ZD_U + 16 * (2 * c + zz)) for c in range(3)] for zz in (0, 1)]
    first, last = [u[c, 0] for c in range(3)], [u[c, 7] for c in range(3)]
    low_f, low_m = two_layers(
        layers, layer * 8 - 2, mats, below + [first],
        (face(zb, ZU_LAB), face(zb, ZU_LAB + 16)), (face(zb, ZU_DT), face(zb, ZU_DT + 16)),
    )
    high_f, high_m = two_layers(
        layers, layer * 8 + 7, mats, [last] + above,
        (lab[7].astype(F32), face(za, ZD_LAB)), (dt[7], face(za, ZD_DT)),
    )
    v_below = [face(zb, ZU_V + 16 * c) for c in range(3)]
    v_above = [face(za, ZD_V + 16 * c) for c in range(3)]
    for i, z, at, pulls, weight, place, speeds in (
        (0, -1, 1, low_f[1], low_m[1], below[1], v_below),
        (1, 0, 2, low_f[2], low_m[2], first, [v[c, 0] for c in range(3)]),
        (8, 7, 3, high_f[0], high_m[0], last, [v[c, 7] for c in range(3)]),
        (9, 8, 4, high_f[1], high_m[1], above[0], v_above),
    ):
        inner = 0 <= z < 8
        edges = [col_m[side, at : at + 1, :] for side in (0, 1)]
        if inner:
            weight = weight + mass[z]
            edges = [edges[side] + in_m[side, z : z + 1, :] for side in (0, 1)]
        rate = DT / (LUMPED + with_columns(weight, *edges))
        dtm[i] = rate
        for c in range(3):
            pull = fold_node(pulls[c])
            edges = [col_f[side, c, at : at + 1, :] for side in (0, 1)]
            if inner:
                pull = pull + force[c, z]
                edges = [edges[side] + in_f[side, c, z : z + 1, :] for side in (0, 1)]
            speed = speeds[c] - rate * with_columns(pull, *edges)
            v1[c, i] = speed
            u1[c, i] = place[c] + DT * speed
    dtm[2:8] = dtmi[...]
    for c in range(3):
        u1[c, 2:8] = ui[c]
        v1[c, 2:8] = vi[c]

    @pl.when(layer == layers // 2)
    def _():
        for c in range(3):
            for i in (0, 1):
                u1[c, 4 + i] = u_face[i, c]
                v1[c, 4 + i] = v_face[i, c]

    for x, row in ((15, NEW_HI), (0, NEW_LO)):
        for c in range(3):
            ends[row + 10 * c : row + 10 * c + 8, :] = u1[c, 0:8, x, :]
            ends[row + 10 * c + 8 : row + 10 * c + 10, :] = u1[c, 8:10, x, :]
        ends[row + 30 : row + 32, :] = jnp.zeros((2, 256), F32)


def pack_new_cross(ends, values, mate, out):
    out[0:32, :] = jnp.where(on_even(), ends[NEW_LO : NEW_LO + 32, :], ends[NEW_HI : NEW_HI + 32, :])
    for row, src, role in ((CROSS_OWN, mate, OPP2), (CROSS_MATE, values, FAR1), (CROSS_ON, values, FAR2)):
        out[row : row + 4, :] = src[4 * role : 4 * role + 4, :]
    out[44:48, :] = jnp.zeros((4, 256), F32)


def pack_last(ends, far, out):
    out[0:32, :] = jnp.where(on_even(), ends[NEW_HI : NEW_HI + 32, :], ends[NEW_LO : NEW_LO + 32, :])
    out[32:48, :] = far[32:48, :]


def second_block(layers, u, dt, lab, par, zb, force, le, de, modes, saved):
    le[0] = zb[ZU_LAB + 16 : ZU_LAB + 32, :]
    de[0] = zb[ZU_DT + 16 : ZU_DT + 32, :]
    le[1:9] = lab[...].astype(F32)
    de[1:9] = dt[...]
    zbase = lax.axis_index("layer") * 8 - 1
    block_forces(layers, 9, 3, zbase, material_scalars(par), u, le, de, modes, saved, None, force, None)


def second_column(blocks, layers, right_side, theirs, dt, lab, par, cols, zb, ends, col, col_lab, col_dt):
    layer, here = lax.axis_index("layer"), lax.axis_index("plane")
    zeros = jnp.zeros((8, 256), F32)
    mine = jnp.where(right_side, ends[NEW_HI : NEW_HI + 32, :], ends[NEW_LO : NEW_LO + 32, :])
    left, right = jnp.where(right_side, mine, theirs), jnp.where(right_side, theirs, mine)
    for c in range(3):
        for i, value in enumerate((left, right)):
            col[i, c, 8:16, :] = zeros
            col[i, c, 0:10, :] = value[10 * c : 10 * c + 10, :]
    for ref, field, first, zu, zuf in (
        (col_lab, lab, COL_LAB, ZU_CLAB, ZU_LAB),
        (col_dt, dt, COL_DT, ZU_CDT, ZU_DT),
    ):
        ref[8:16, :] = zeros
        ref[0:1, :] = jnp.where(right_side, zb[zuf + 31 : zuf + 32, :], zb[zu + 1 : zu + 2, :])
        ref[1:9, :] = jnp.where(right_side, field[:, 15, :].astype(F32), cols[first : first + 8, :])
    zg = iota((16, 256), 0) + (layer * 8 - 1)
    inside = jnp.where(right_side, here < blocks - 1, here > 0)
    return column_forces(
        layers, zg, zg < layer * 8 + 8, material_scalars(par), inside, jnp.where(right_side, -1.0, 1.0),
        [col[0, c] for c in range(3)], [col[1, c] for c in range(3)], col_lab[...], col_dt[...], False,
    )[0]


def second_step(
    blocks, layers,
    u, v, dtm, dt, lab, par, force, cols, zb, ends, far,
    u2, v2,
    col, col_lab, col_dt, col_f,
):
    even = on_even()
    forces = second_column(
        blocks, layers, jnp.logical_not(even), far[0:32, :], dt, lab, par, cols, zb, ends, col, col_lab, col_dt
    )
    for c in range(3):
        col_f[0, c] = jnp.where(even, forces[c], 0.0)
        col_f[1, c] = jnp.where(even, 0.0, forces[c])
    for z in range(8):
        e = z + 1
        rate = dtm[e]
        for c in range(3):
            pull = with_columns(force[c, e], col_f[0, c, e : e + 1, :], col_f[1, c, e : e + 1, :])
            speed = v[c, e] - rate * pull
            v2[c, z] = speed
            u2[c, z] = u[c, e] + DT * speed


def second_contact(
    blocks, layers,
    u_in, v_in, dtm, lists, mate, far, opp, dt, lab, par, cols, zb, ends,
    u2, v2,
    u, v, col, col_lab, col_dt, col_f, sems,
):
    even = on_even()
    on_face = lax.axis_index("layer") == layers // 2
    forces = second_column(
        blocks, layers, even, opp[0:32, :], dt, lab, par, cols, zb, ends, col, col_lab, col_dt
    )
    for c in range(3):
        col_f[0, c] = jnp.where(even, 0.0, forces[c])
        col_f[1, c] = jnp.where(even, forces[c], 0.0)
    sol_y, sol_x = one_hots(lists[0:1, :])
    land_y, land_x = one_hots(lists[6:7, :])

    def values(i):
        half = slice(128 * (i % 2), 128 * (i % 2) + 128)
        own_row = (3, 4, 5, 8, 9, 10)[i]
        places = (
            (mate, 4 * NEAR), (far, CROSS_MATE), None, (far, CROSS_OWN), (opp, CROSS_ON)
        )
        parts = [
            lists[own_row : own_row + 1, 256:384] if place is None
            else place[0][place[1] + i // 2 : place[1] + i // 2 + 1, half]
            for place in places
        ]
        return jnp.concatenate(parts, axis=1)

    far_bump = jnp.concatenate([values(i) for i in range(3)], axis=0)
    far_pad = jnp.concatenate([values(i) for i in range(3, 6)], axis=0)
    on_bump = lists[2:3, :] * (far_pad - lists[3:6, :])
    on_pad = lists[7:8, :] * (far_bump - lists[8:11, :])
    extra = (scatter(on_pad, land_y, land_x), scatter(on_bump, sol_y, sol_x))
    for z in (0, 1, 2, 5, 6, 7, 3, 4):
        e = z + 1
        rate = dtm[e]
        for c in range(3):
            pull = with_columns(jnp.zeros((16, 256), F32), col_f[0, c, e : e + 1, :], col_f[1, c, e : e + 1, :])
            if z in (3, 4):
                pull = pull - jnp.where(on_face, extra[z - 3][c], 0.0)
            change = rate * pull
            v[c, z] = v_in[c, z] - change
            u[c, z] = u_in[c, z] - DT * change
    copies = [pltpu.make_async_copy(src, dst, sems.at[i]) for i, (src, dst) in enumerate(((u, u2), (v, v2)))]
    for copy in copies:
        copy.start()
    for copy in copies:
        copy.wait()


VM = pl.BlockSpec(memory_space=pltpu.VMEM)
SM = pl.BlockSpec(memory_space=pltpu.SMEM)
HBM = pl.BlockSpec(memory_space=pltpu.HBM)


def call(kernel, in_specs, outs, scratch, name, flops, vmem=32, out_spec=VM):
    return pl.pallas_call(
        kernel,
        out_shape=[jax.ShapeDtypeStruct(shape, F32) for shape in outs],
        in_specs=in_specs,
        out_specs=[out_spec] * len(outs),
        scratch_shapes=[pltpu.VMEM(s, F32) if isinstance(s, tuple) else s for s in scratch],
        compiler_params=pltpu.CompilerParams(vmem_limit_bytes=vmem * 1024 * 1024),
        cost_estimate=pl.CostEstimate(flops=flops, bytes_accessed=flops // 25, transcendentals=0),
        name=name,
    )


def local(u, v, dt, lab, par, sol, land, stiff, tally):
    blocks, layers = lax.axis_size("plane"), lax.axis_size("layer")
    swaps = [(s, s ^ 1) for s in range(blocks)]
    crossings = [(s, s + 2 - 4 * (s % 2)) for s in range(blocks) if 0 <= s + 2 - 4 * (s % 2) < blocks]
    face_swaps = [(a * layers + layers // 2, b * layers + layers // 2) for a, b in swaps]

    def along_layer(value, steps):
        pairs = [(s, s + steps) for s in range(layers) if 0 <= s + steps < layers]
        return lax.ppermute(value, "layer", pairs)

    own = call(
        functools.partial(pack_export, blocks, layers),
        [HBM] * 7,
        [(EXPORT_ROWS, 256)],
        [u.shape, dt.shape, pltpu.VMEM(lab.shape, jnp.int32)]
        + [pltpu.VMEM((5, 1, 128), jnp.int32)] * 2
        + [(5, 1, 128), pltpu.SMEM((1, 5), jnp.int32), pltpu.VMEM((8, 640), jnp.int32)]
        + [pltpu.VMEM((256, 640), BF16), (16, 640), pltpu.SemaphoreType.DMA((7,))],
        "pack_export",
        100_000,
        63,
    )(u, dt, lab, sol.reshape(5, 1, 128), land.reshape(5, 1, 128), stiff.reshape(5, 1, 128), tally)[0]
    near = lax.ppermute(own, "plane", swaps)
    own = call(stage, [HBM], [own.shape], [pltpu.SemaphoreType.DMA], "stage", 100_000)(own)[0]
    cross, skip = call(pack_cross, [VM] * 2, [(CROSS_ROWS, 256), (SKIP_ROWS, 256)], [], "pack_cross", 1_000)(own, near)
    far = lax.ppermute(cross, "plane", crossings)
    skips = [(s * layers + layers // 2, t * layers + layers // 2) for t, s in crossings]
    opp = lax.ppermute(skip, ("plane", "layer"), skips)
    modes = [(12, 16, 256), (12, 16, 256)]
    plane = (16, 256)
    force, mass = call(
        functools.partial(first_block, layers),
        [VM] * 3 + [SM],
        [(3, 8, 16, 256), (8, 16, 256)],
        modes + [plane],
        "first_block",
        50_000_000,
    )(u, dt, lab, par)
    far, force, mass = lax.optimization_barrier((far, force, mass))
    up, dn, cols = call(
        pack_layer, [VM] * 6, [(ZU_ROWS, 256), (ZD_ROWS, 256), (COLS_ROWS, 256)], [], "pack_layer", 1_000
    )(u, v, dt, lab, near, far)
    zb, za = along_layer(up, 1), along_layer(dn, -1)
    u1, v1, dtm, in_f, in_m = call(
        functools.partial(first_inner, blocks, layers),
        [VM] * 2 + [SM] + [VM] * 4,
        [(3, 6, 16, 256), (3, 6, 16, 256), (6, 16, 256), (2, 3, 8, 256), (2, 8, 256)],
        [],
        "first_inner",
        1_000,
    )(u, v, par, own, cols, force, mass)
    opp, u1, v1 = lax.optimization_barrier((opp, u1, v1))
    u_face, v_face, values, lists = call(
        functools.partial(first_contact, layers),
        [VM] * 7,
        [(2, 3, 16, 256), (2, 3, 16, 256), (VALUES_ROWS, 256), (16, 640)],
        [],
        "first_contact",
        10_000_000,
    )(own, near, far, opp, u1, v1, dtm)
    mate = lax.ppermute(values, ("plane", "layer"), face_swaps)

    two = (2, 8, 256)
    u1, v1, dtm, ends = call(
        functools.partial(first_step, blocks, layers),
        [VM] * 4 + [SM] + [VM] * 13,
        [(3, 10, 16, 256), (3, 10, 16, 256), (10, 16, 256), (NEW_ROWS, 256)],
        [(4, 3, 8, 256), two, two, (2, 3, 8, 256), two],
        "first_step",
        20_000_000,
    )(u, v, dt, lab, par, own, cols, zb, za, force, mass, in_f, in_m, u1, v1, dtm, u_face, v_face)
    across = [(s, s + 1) for s in range(1, blocks - 1, 2)] + [(s, s - 1) for s in range(2, blocks, 2)]
    cross = call(pack_new_cross, [VM] * 3, [(NEW_CROSS_ROWS, 256)], [], "pack_new_cross", 100_000)(ends, values, mate)[0]
    far = lax.ppermute(cross, "plane", across)
    force = call(
        functools.partial(second_block, layers),
        [VM] * 3 + [SM, VM],
        [(3, 10, 16, 256)],
        [(9, 16, 256), (9, 16, 256)] + modes,
        "second_block",
        50_000_000,
    )(u1, dt, lab, par, zb)[0]
    far, force = lax.optimization_barrier((far, force))
    last = call(pack_last, [VM] * 2, [(NEW_CROSS_ROWS, 256)], [], "pack_last", 100_000)(ends, far)[0]
    opp = lax.ppermute(last, "plane", swaps)
    column = [(2, 3, 16, 256), (16, 256), (16, 256)]
    u2, v2 = call(
        functools.partial(second_step, blocks, layers),
        [VM] * 5 + [SM] + [VM] * 5,
        [(3, 8, 16, 256)] * 2,
        column + [(2, 3, 16, 256)],
        "second_step",
        20_000_000,
    )(u1, v1, dtm, dt, lab, par, force, cols, zb, ends, far)
    return tuple(
        call(
            functools.partial(second_contact, blocks, layers),
            [VM] * 9 + [SM] + [VM] * 3,
            [(3, 8, 16, 256)] * 2,
            [(3, 8, 16, 256)] * 2 + column + [(2, 3, 16, 256), pltpu.SemaphoreType.DMA((2,))],
            "second_contact",
            10_000_000,
            out_spec=HBM,
        )(u2, v2, dtm, lists, mate, far, opp, dt, lab, par, cols, zb, ends)
    )


def solution(mesh):
    in_specs = (
        P(None, "layer", "plane", None),
        P(None, "layer", "plane", None),
        P("layer", "plane", None),
        P("layer", "plane", None),
        P(),
        P("plane", None, None),
        P("plane", None, None),
        P("plane", None, None),
        P("plane", None),
    )
    out_specs = (P(None, "layer", "plane", None), P(None, "layer", "plane", None))
    return jax.shard_map(local, mesh=mesh, in_specs=in_specs, out_specs=out_specs, check_vma=False)
```

```python
import functools

import jax
import jax.numpy as jnp
from jax import lax
from jax.experimental import pallas as pl
from jax.experimental.pallas import tpu as pltpu
from jax.sharding import PartitionSpec as P

DT = 0.05
LUMPED = 0.25
F32 = jnp.float32
BF16 = jnp.bfloat16
QUADS = ((0, 0), (0, 1), (1, 0), (1, 1))

COL_HI, COL_LO, LISTS, PAD, EXPORT_ROWS = 0, 40, 64, 88, 136
OWN_OPP2, MATE_FAR1, OWN_PAD, MATE_PAD, CROSS_ROWS = 40, 44, 48, 96, 144
SKIP_LIST, SKIP_PAD, SKIP_ROWS = 0, 8, 232
COL_LAB, COL_DT, COL_BEYOND, COLS_ROWS = 24, 32, 40, 64
ZU_U, ZU_V, ZU_LAB, ZU_DT, ZU_CL, ZU_CH, ZU_CLAB, ZU_CDT, ZU_ROWS = 0, 96, 144, 176, 208, 214, 220, 222, 224
ZD_U, ZD_V, ZD_LAB, ZD_DT, ZD_CL, ZD_CH, ZD_CLAB, ZD_CDT, ZD_ROWS = 0, 96, 144, 160, 176, 182, 188, 189, 192
NEW_HI, NEW_LO, NEW_ROWS, VALUES_ROWS = 0, 48, 96, 24
CROSS_OWN, CROSS_MATE, CROSS_ON, NEW_CROSS_ROWS = 48, 52, 56, 64
NEAR, FAR1, OWN, FAR2, OPP2 = range(5)
OFFSETS = (1, -1, 0, -2, 2)


def iota(shape, dim):
    return lax.broadcasted_iota(jnp.int32, shape, dim)


def on_even():
    return lax.rem(lax.axis_index("plane"), 2) == 0


def role_offset(role):
    return jnp.where(on_even(), OFFSETS[role], -OFFSETS[role])


def pack_export(
    blocks, layers,
    u_hbm, dt_hbm, lab_hbm, sol_hbm, land_hbm, stiff_hbm, tally_hbm,
    out,
    u, dt, lab, sol, land, stiff, tally, pos, ohy, ohx, sems,
):
    copies = [
        pltpu.make_async_copy(src, dst, sems.at[i])
        for i, (src, dst) in enumerate(
            (
                (u_hbm, u), (dt_hbm, dt), (lab_hbm, lab), (sol_hbm, sol),
                (land_hbm, land), (stiff_hbm, stiff), (tally_hbm, tally),
            )
        )
    ]
    for copy in copies:
        copy.start()
    for copy in copies[3:]:
        copy.wait()
    pad_z = u.shape[1] // 2 - 1
    here = lax.axis_index("plane")
    on_face = lax.axis_index("layer") == layers // 2

    @pl.when(on_face)
    def _():
        out[LISTS : LISTS + 24, :] = jnp.zeros((24, 256), F32)
        for k in range(5):
            row = LISTS + 4 * k
            target = here + (k - 2)
            count = jnp.where((target >= 0) & (target < blocks), tally[0, k], 0)
            live = iota((1, 128), 1) < count
            out[row : row + 1, 0:128] = sol[k].astype(F32)
            out[row : row + 1, 128:256] = land[k].astype(F32)
            out[row + 1 : row + 2, 0:128] = jnp.where(live, stiff[k], 0.0)
            pos[0:1, 128 * k : 128 * k + 128] = sol[k]
        ohy[...], ohx[...] = one_hots(pos[0:1, :])

    for copy in copies[:3]:
        copy.wait()
    for x, row in ((15, COL_HI), (0, COL_LO)):
        for c in range(3):
            out[row + 8 * c : row + 8 * c + 8, :] = u[c, :, x, :]
    out[COL_HI + COL_LAB : COL_HI + COL_LAB + 8, :] = lab[:, 15, :].astype(F32)
    out[COL_HI + COL_DT : COL_HI + COL_DT + 8, :] = dt[:, 15, :]

    @pl.when(on_face)
    def _():
        bump = gather(jnp.concatenate([u[c, pad_z + 1] for c in range(3)], axis=0), ohy[...], ohx[...])
        for k in range(5):
            row, cols = LISTS + 4 * k, slice(128 * k, 128 * k + 128)
            out[row + 1 : row + 2, 128:256] = bump[0:1, cols]
            out[row + 2 : row + 3, 0:128] = bump[1:2, cols]
            out[row + 2 : row + 3, 128:256] = bump[2:3, cols]
        for c in range(3):
            out[PAD + 16 * c : PAD + 16 * c + 16, :] = u[c, pad_z]


def stage(src, dst, sem):
    copy = pltpu.make_async_copy(src, dst, sem)
    copy.start()
    copy.wait()


def pack_cross(own, mate, out, skip):
    even = on_even()

    def bucket(ref, if_even, if_odd):
        a, b = LISTS + 4 * if_even, LISTS + 4 * if_odd
        return jnp.where(even, ref[a : a + 4, :], ref[b : b + 4, :])

    out[24:40, :] = mate[COL_HI + 24 : COL_HI + 40, :]
    out[0:24, :] = jnp.where(even, mate[COL_HI : COL_HI + 24, :], mate[COL_LO : COL_LO + 24, :])
    out[OWN_OPP2 : OWN_OPP2 + 4, :] = bucket(own, 4, 0)
    out[MATE_FAR1 : MATE_FAR1 + 4, :] = bucket(mate, 3, 1)
    out[OWN_PAD : OWN_PAD + 48, :] = own[PAD : PAD + 48, :]
    out[MATE_PAD : MATE_PAD + 48, :] = mate[PAD : PAD + 48, :]
    skip[SKIP_LIST : SKIP_LIST + 4, :] = bucket(own, 0, 4)
    skip[SKIP_LIST + 4 : SKIP_PAD, :] = jnp.zeros((4, 256), F32)
    skip[SKIP_PAD : SKIP_PAD + 48, :] = own[PAD : PAD + 48, :]


def pack_layer(u, v, dt, lab, near, far, up, dn, cols):
    even = on_even()
    cols[0:40, :] = jnp.where(even, far[0:40, :], near[COL_HI : COL_HI + 40, :])
    cols[COL_BEYOND : COL_BEYOND + 24, :] = jnp.where(even, near[COL_LO : COL_LO + 24, :], far[0:24, :])
    for c in range(3):
        for zz in (0, 1):
            row = 16 * (2 * c + zz)
            up[ZU_U + row : ZU_U + row + 16, :] = u[c, 6 + zz]
            dn[ZD_U + row : ZD_U + row + 16, :] = u[c, zz]
        up[ZU_V + 16 * c : ZU_V + 16 * c + 16, :] = v[c, 7]
        dn[ZD_V + 16 * c : ZD_V + 16 * c + 16, :] = v[c, 0]
        lo, hi = 8 * c, COL_BEYOND + 8 * c
        up[ZU_CL + 2 * c : ZU_CL + 2 * c + 2, :] = cols[lo + 6 : lo + 8, :]
        up[ZU_CH + 2 * c : ZU_CH + 2 * c + 2, :] = cols[hi + 6 : hi + 8, :]
        dn[ZD_CL + 2 * c : ZD_CL + 2 * c + 2, :] = cols[lo : lo + 2, :]
        dn[ZD_CH + 2 * c : ZD_CH + 2 * c + 2, :] = cols[hi : hi + 2, :]
    for zz in (0, 1):
        up[ZU_LAB + 16 * zz : ZU_LAB + 16 * zz + 16, :] = lab[6 + zz].astype(F32)
        up[ZU_DT + 16 * zz : ZU_DT + 16 * zz + 16, :] = dt[6 + zz]
    up[ZU_CLAB : ZU_CLAB + 2, :] = cols[COL_LAB + 6 : COL_LAB + 8, :]
    up[ZU_CDT : ZU_CDT + 2, :] = cols[COL_DT + 6 : COL_DT + 8, :]
    dn[ZD_LAB : ZD_LAB + 16, :] = lab[0].astype(F32)
    dn[ZD_DT : ZD_DT + 16, :] = dt[0]
    dn[ZD_CLAB : ZD_CLAB + 1, :] = cols[COL_LAB : COL_LAB + 1, :]
    dn[ZD_CDT : ZD_CDT + 1, :] = cols[COL_DT : COL_DT + 1, :]
    dn[ZD_CDT + 1 : ZD_ROWS, :] = jnp.zeros((ZD_ROWS - ZD_CDT - 1, 256), F32)


def material_scalars(par):
    out = []
    for m in range(4):
        lam, mu, alpha, rho = par[0, m], par[1, m], par[2, m], par[3, m]
        out.append(
            (
                lam * (1.0 / 16.0),
                mu * (1.0 / 16.0),
                (lam + 4.0 * mu) * (1.0 / 144.0),
                (3.0 * lam + 2.0 * mu) * alpha * 0.25,
                rho * 0.125,
            )
        )
    return out


def cell_fields(mats, lab, dt, mask, with_mass):
    is0, is1, is2 = lab == 0.0, lab == 1.0, lab == 2.0

    def pick(i):
        rest = jnp.where(is2, mats[2][i], mats[3][i])
        return jnp.where(is0, mats[0][i], jnp.where(is1, mats[1][i], rest)) * mask

    return pick(0), pick(1), pick(2), pick(3) * dt, pick(4) if with_mass else None


def plane_modes(u, ux):
    s, d = u + ux, ux - u
    sy, dy = pltpu.roll(s, 255, 1), pltpu.roll(d, 255, 1)
    return [s + sy, sy - s, d + dy, dy - d]


def cell_forces(lower, upper, l1, m1, k3, th):
    z, x, y = (
        {
            (i, j, k): (upper[c][q] - lower[c][q]) if i else (upper[c][q] + lower[c][q])
            for q, (j, k) in enumerate(QUADS)
            for i in (0, 1)
            if i + j + k
        }
        for c in range(3)
    )
    l2, m2 = l1 * (1.0 / 3.0), m1 * (1.0 / 3.0)
    p0 = l1 * (z[1, 0, 0] + x[0, 1, 0] + y[0, 0, 1]) - th
    m1x2 = m1 + m1
    zx = m1 * (x[1, 0, 0] + z[0, 1, 0])
    zy = m1 * (y[1, 0, 0] + z[0, 0, 1])
    xy = m1 * (y[0, 1, 0] + x[0, 0, 1])
    pz = l2 * (x[1, 1, 0] + y[1, 0, 1])
    px = l2 * (z[1, 1, 0] + y[0, 1, 1])
    py = l2 * (z[1, 0, 1] + x[0, 1, 1])
    tw = z[0, 1, 1] + x[1, 0, 1] + y[1, 1, 0]
    fz = {
        (1, 0, 0): p0 + m1x2 * z[1, 0, 0],
        (0, 1, 0): zx,
        (0, 0, 1): zy,
        (1, 1, 0): px + m1 * z[1, 1, 0],
        (1, 0, 1): py + m1 * z[1, 0, 1],
        (0, 1, 1): m2 * (tw + z[0, 1, 1]),
        (1, 1, 1): k3 * z[1, 1, 1],
    }
    fx = {
        (0, 1, 0): p0 + m1x2 * x[0, 1, 0],
        (1, 0, 0): zx,
        (0, 0, 1): xy,
        (1, 1, 0): pz + m1 * x[1, 1, 0],
        (0, 1, 1): py + m1 * x[0, 1, 1],
        (1, 0, 1): m2 * (tw + x[1, 0, 1]),
        (1, 1, 1): k3 * x[1, 1, 1],
    }
    fy = {
        (0, 0, 1): p0 + m1x2 * y[0, 0, 1],
        (1, 0, 0): zy,
        (0, 1, 0): xy,
        (1, 0, 1): pz + m1 * y[1, 0, 1],
        (0, 1, 1): px + m1 * y[0, 1, 1],
        (1, 1, 0): m2 * (tw + y[1, 1, 0]),
        (1, 1, 1): k3 * y[1, 1, 1],
    }
    low, high = [], []
    for f in (fz, fx, fy):
        low_c, high_c = [], []
        for j, k in QUADS:
            d = f[1, j, k]
            if j + k:
                s = f[0, j, k]
                low_c.append(s - d)
                high_c.append(s + d)
            else:
                low_c.append(-d)
                high_c.append(d)
        low.append(low_c)
        high.append(high_c)
    return low, high


def fold_y(a, b):
    return (a - b) + pltpu.roll(a + b, 1, 1)


def column_forces(layers, zg, valid, mats, inside, side, left, right, lab, dt, with_mass):
    rows = lab.shape[0]
    shape = (rows, 256)
    ok = (zg >= 0) & (zg <= layers * 8 - 2) & (zg != layers // 2 * 8 + 3) & (iota(shape, 1) < 255)
    mask = jnp.where(ok & valid & inside, 1.0, 0.0)
    *fields, rho = cell_fields(mats, lab, dt, mask, with_mass)
    if with_mass:
        rho = rho + pltpu.roll(rho, 1, 1)
        rho = rho + pltpu.roll(rho, 1, 0)
    return column_part(fields, side, left, right), rho


def column_part(fields, side, left, right):
    rows = left[0].shape[0]
    lower = [plane_modes(left[c], right[c]) for c in range(3)]
    upper = [[pltpu.roll(a, rows - 1, 0) for a in comp] for comp in lower]
    low, high = cell_forces(lower, upper, *fields)
    forces = []
    for c in range(3):
        node = [low[c][q] + pltpu.roll(high[c][q], 1, 0) for q in range(4)]
        t0, t1 = fold_y(node[0], node[1]), fold_y(node[2], node[3])
        forces.append(t0 + side * t1)
    return forces


def block_forces(layers, cells, group, zbase, mats, u, lab, dt, modes, saved, saved_m, force, mass):
    shape = (16, 256)
    row, lane = iota(shape, 0), iota(shape, 1)
    in_plane = jnp.where((lane < 255) & (row < 15), 1.0, 0.0)

    def forward(e, c):
        a = u[c, e]
        return plane_modes(a, pltpu.roll(a, 15, 0))

    for c in range(3):
        for q, value in enumerate(forward(0, c)):
            modes[4 * c + q] = value
            saved[4 * c + q] = jnp.zeros(shape, F32)
    if mass is not None:
        saved_m[...] = jnp.zeros(shape, F32)

    def fold(e, node):
        for c in range(3):
            t0, t1 = fold_y(node[c][0], node[c][1]), fold_y(node[c][2], node[c][3])
            force[c, e] = (t0 - t1) + pltpu.roll(t0 + t1, 1, 0)

    def body(i, carry):
        lower = [[modes[4 * c + q] for q in range(4)] for c in range(3)]
        held = [[saved[4 * c + q] for q in range(4)] for c in range(3)]
        held_m = None if mass is None else saved_m[...]
        for g in range(group):
            e = i * group + g
            zg = zbase + e
            ok = (zg >= 0) & (zg <= layers * 8 - 2) & (zg != layers // 2 * 8 + 3)
            mask = in_plane * jnp.where(ok, 1.0, 0.0)
            l1, m1, k3, th, rho = cell_fields(mats, lab[e].astype(F32), dt[e], mask, mass is not None)
            upper = [forward(e + 1, c) for c in range(3)]
            low, high = cell_forces(lower, upper, l1, m1, k3, th)
            fold(e, [[low[c][q] + held[c][q] for q in range(4)] for c in range(3)])
            lower, held = upper, high
            if mass is not None:
                rho = rho + pltpu.roll(rho, 1, 1)
                rho = rho + pltpu.roll(rho, 1, 0)
                mass[e] = rho + held_m
                held_m = rho
        for c in range(3):
            for q in range(4):
                modes[4 * c + q] = lower[c][q]
                saved[4 * c + q] = held[c][q]
        if mass is not None:
            saved_m[...] = held_m
        return carry

    lax.fori_loop(0, cells // group, body, 0)
    fold(cells, [[saved[4 * c + q] for q in range(4)] for c in range(3)])
    if mass is not None:
        mass[cells] = saved_m[...]


def two_layers(layers, z, mats, nodes, lab, dt):
    shape = (16, 256)
    in_plane = jnp.where((iota(shape, 1) < 255) & (iota(shape, 0) < 15), 1.0, 0.0)
    modes = [[plane_modes(a, pltpu.roll(a, 15, 0)) for a in node] for node in nodes]
    parts, masses = [], []
    for i in (0, 1):
        zg = z + i
        ok = (zg >= 0) & (zg <= layers * 8 - 2) & (zg != layers // 2 * 8 + 3)
        mask = in_plane * jnp.where(ok, 1.0, 0.0)
        l1, m1, k3, th, rho = cell_fields(mats, lab[i], dt[i], mask, True)
        parts.append(cell_forces(modes[i], modes[i + 1], l1, m1, k3, th))
        rho = rho + pltpu.roll(rho, 1, 1)
        masses.append(rho + pltpu.roll(rho, 1, 0))
    (low0, high0), (low1, high1) = parts
    middle = [[high0[c][q] + low1[c][q] for q in range(4)] for c in range(3)]
    return (low0, middle, high1), (masses[0], masses[0] + masses[1], masses[1])


def fold_node(node):
    t0, t1 = fold_y(node[0], node[1]), fold_y(node[2], node[3])
    return (t0 - t1) + pltpu.roll(t0 + t1, 1, 0)


def with_columns(a, first, last):
    row = iota((8, 256), 0)
    top = a[0:8] + jnp.where(row == 0, jnp.broadcast_to(first, (8, 256)), 0.0)
    bottom = a[8:16] + jnp.where(row == 7, jnp.broadcast_to(last, (8, 256)), 0.0)
    return jnp.concatenate([top, bottom], axis=0)


def split3(a):
    hi = a.astype(BF16)
    rest = a - hi.astype(F32)
    mid = rest.astype(BF16)
    lo = (rest - mid.astype(F32)).astype(BF16)
    return jnp.concatenate([hi, mid, lo], axis=0)


def join3(a):
    n = a.shape[0] // 3
    return (a[:n] + a[n : 2 * n]) + a[2 * n :]


def one_hots(position):
    pos = position.astype(jnp.int32)
    n = pos.shape[1]
    y, x = pos & 255, pos >> 8
    ohy = jnp.where(iota((256, n), 0) == y, 1.0, 0.0).astype(BF16)
    ohx = jnp.where(iota((16, n), 0) == x, 1.0, 0.0)
    return ohy, ohx


def gather(face, ohy, ohx):
    n = ohx.shape[1]
    rows = join3(jnp.dot(split3(face), ohy, preferred_element_type=F32))
    return jnp.sum(rows.reshape(3, 16, n) * ohx[None], axis=1)


def scatter(values, ohy, ohx):
    n = ohx.shape[1]
    rows = (values[:, None, :] * ohx[None]).reshape(48, n)
    out = lax.dot_general(split3(rows), ohy, (((1,), (1,)), ((), ())), preferred_element_type=F32)
    return join3(out).reshape(3, 16, 256)


def fill_lists(own, near, far, opp, lists):
    sources = {
        NEAR: (near, LISTS + 4 * (2 - role_offset(NEAR))),
        FAR1: (far, MATE_FAR1),
        OWN: (own, LISTS + 8),
        FAR2: (far, OWN_OPP2),
        OPP2: (opp, SKIP_LIST),
    }
    for role, (ref, base) in sources.items():
        cols = slice(128 * role, 128 * role + 128)
        row = LISTS + 4 * (2 + role_offset(role))
        for i in range(3):
            mine, other = own[pl.ds(row + i, 1), :], ref[pl.ds(base + i, 1), :]
            for half in (0, 1):
                part = slice(128 * half, 128 * half + 128)
                lists[2 * i + half : 2 * i + half + 1, cols] = mine[:, part]
                if i + half:
                    lists[5 + 2 * i + half : 6 + 2 * i + half, cols] = other[:, part]


def first_block(layers, u, dt, lab, par, force, mass, modes, saved, saved_m):
    zbase = lax.axis_index("layer") * 8
    block_forces(layers, 7, 7, zbase, material_scalars(par), u, lab, dt, modes, saved, saved_m, force, mass)


def first_inner(
    blocks, layers, u, v, par, own, cols, force, mass, u1, v1, dtm, col_f, col_m
):
    here = lax.axis_index("plane")
    mats = material_scalars(par)
    row = iota((8, 256), 0)
    for at, inside, side in ((0, here > 0, 1), (1, here < blocks - 1, -1)):
        first = COL_LO if at == 0 else COL_HI
        mine = [own[first + 8 * c : first + 8 * c + 8, :] for c in range(3)]
        beyond = COL_BEYOND if at else 0
        theirs = [cols[beyond + 8 * c : beyond + 8 * c + 8, :] for c in range(3)]
        left, right = (mine, theirs) if at else (theirs, mine)
        ref = own if at else cols
        forces, rho = column_forces(
            layers, row + lax.axis_index("layer") * 8, row < 7, mats, inside, side, left, right,
            ref[COL_LAB : COL_LAB + 8, :], ref[COL_DT : COL_DT + 8, :], True,
        )
        for c in range(3):
            col_f[at, c] = forces[c]
        col_m[at] = rho
    for i in range(6):
        z = i + 1
        rate = DT / (LUMPED + with_columns(mass[z], col_m[0, z : z + 1, :], col_m[1, z : z + 1, :]))
        dtm[i] = rate
        for c in range(3):
            pull = with_columns(force[c, z], col_f[0, c, z : z + 1, :], col_f[1, c, z : z + 1, :])
            speed = v[c, z] - rate * pull
            v1[c, i] = speed
            u1[c, i] = u[c, z] + DT * speed


def first_contact(layers, own, near, far, opp, u1, v1, dtm, u_face, v_face, out, lists):
    @pl.when(lax.axis_index("layer") == layers // 2)
    def _():
        fill_lists(own, near, far, opp, lists)
        sol_y, sol_x = one_hots(lists[0:1, :])
        land_y, land_x = one_hots(lists[6:7, :])
        far_y, far_x = one_hots(lists[1:2, :])
        own_pad = own[PAD : PAD + 48, :]
        pads = {
            NEAR: near[PAD : PAD + 48, :],
            FAR1: far[MATE_PAD : MATE_PAD + 48, :],
            OWN: own_pad,
            FAR2: far[OWN_PAD : OWN_PAD + 48, :],
            OPP2: opp[SKIP_PAD : SKIP_PAD + 48, :],
        }
        far_pad = []
        for role in range(5):
            part = slice(128 * role, 128 * role + 128)
            far_pad.append(gather(pads[role], far_y[:, part], far_x[:, part]))
        on_bump = lists[2:3, :] * (jnp.concatenate(far_pad, axis=1) - lists[3:6, :])
        on_pad = lists[7:8, :] * (lists[8:11, :] - gather(own_pad, land_y, land_x))
        extra = (scatter(on_pad, land_y, land_x), scatter(on_bump, sol_y, sol_x))
        faces = []
        for face in (0, 1):
            new = []
            for c in range(3):
                change = dtm[2 + face] * extra[face][c]
                v_face[face, c] = v1[c, 2 + face] + change
                new.append(u1[c, 2 + face] + DT * change)
                u_face[face, c] = new[c]
            faces.append(jnp.concatenate(new, axis=0))
        lists[3:6, :] = gather(faces[1], sol_y, sol_x)
        lists[8:11, :] = gather(faces[0], land_y, land_x)
        for role in range(5):
            part = slice(128 * role, 128 * role + 128)
            for i, row in enumerate((3, 4, 5, 8, 9, 10)):
                at, half = 4 * role + i // 2, i % 2
                out[at : at + 1, 128 * half : 128 * half + 128] = lists[row : row + 1, part]


def first_step(
    blocks, layers,
    u, v, dt, lab, par, own, cols, zb, za, force, mass, in_f, in_m, ui, vi, dtmi, u_face, v_face,
    u1, v1, dtm, ends,
    col, col_lab, col_dt, col_f, col_m,
):
    layer, here = lax.axis_index("layer"), lax.axis_index("plane")
    mats = material_scalars(par)
    for c in range(3):
        for at, first, zu, zd in ((0, 0, ZU_CL, ZD_CL), (3, COL_BEYOND, ZU_CH, ZD_CH)):
            col[at, c, 0:2, :] = zb[zu + 2 * c : zu + 2 * c + 2, :]
            col[at, c, 2:3, :] = cols[first + 8 * c : first + 8 * c + 1, :]
            col[at, c, 3:4, :] = cols[first + 8 * c + 7 : first + 8 * c + 8, :]
            col[at, c, 4:6, :] = za[zd + 2 * c : zd + 2 * c + 2, :]
            col[at, c, 6:8, :] = jnp.zeros((2, 256), F32)
        for at, first, x in ((1, COL_LO, 0), (2, COL_HI, 15)):
            for zz in (0, 1):
                row = 16 * (2 * c + zz) + x
                col[at, c, zz : zz + 1, :] = zb[ZU_U + row : ZU_U + row + 1, :]
                col[at, c, 4 + zz : 5 + zz, :] = za[ZD_U + row : ZD_U + row + 1, :]
            col[at, c, 2:3, :] = own[first + 8 * c : first + 8 * c + 1, :]
            col[at, c, 3:4, :] = own[first + 8 * c + 7 : first + 8 * c + 8, :]
            col[at, c, 6:8, :] = jnp.zeros((2, 256), F32)
    for ref, first, zu, zd, zuf, zdf in (
        (col_lab, COL_LAB, ZU_CLAB, ZD_CLAB, ZU_LAB, ZD_LAB),
        (col_dt, COL_DT, ZU_CDT, ZD_CDT, ZU_DT, ZD_DT),
    ):
        for at in (0, 1):
            ref[at] = jnp.zeros((8, 256), F32)
        ref[0, 0:2, :] = zb[zu : zu + 2, :]
        ref[0, 3:4, :] = cols[first + 7 : first + 8, :]
        ref[0, 4:5, :] = za[zd : zd + 1, :]
        ref[1, 0:1, :] = zb[zuf + 15 : zuf + 16, :]
        ref[1, 1:2, :] = zb[zuf + 31 : zuf + 32, :]
        ref[1, 3:4, :] = own[COL_HI + first + 7 : COL_HI + first + 8, :]
        ref[1, 4:5, :] = za[zdf + 15 : zdf + 16, :]
    row = iota((8, 256), 0)
    zg = layer * 8 + jnp.where(row < 3, row - 2, row + 4)
    valid = (row < 5) & (row != 2)
    for at, inside, side in ((0, here > 0, 1), (1, here < blocks - 1, -1)):
        left = [col[2 * at, c] for c in range(3)]
        right = [col[2 * at + 1, c] for c in range(3)]
        forces, rho = column_forces(
            layers, zg, valid, mats, inside, side, left, right, col_lab[at], col_dt[at], True
        )
        for c in range(3):
            col_f[at, c] = forces[c]
        col_m[at] = rho

    def face(ref, row):
        return ref[row : row + 16, :]

    below = [[face(zb, ZU_U + 16 * (2 * c + zz)) for c in range(3)] for zz in (0, 1)]
    above = [[face(za, ZD_U + 16 * (2 * c + zz)) for c in range(3)] for zz in (0, 1)]
    first, last = [u[c, 0] for c in range(3)], [u[c, 7] for c in range(3)]
    low_f, low_m = two_layers(
        layers, layer * 8 - 2, mats, below + [first],
        (face(zb, ZU_LAB), face(zb, ZU_LAB + 16)), (face(zb, ZU_DT), face(zb, ZU_DT + 16)),
    )
    high_f, high_m = two_layers(
        layers, layer * 8 + 7, mats, [last] + above,
        (lab[7].astype(F32), face(za, ZD_LAB)), (dt[7], face(za, ZD_DT)),
    )
    v_below = [face(zb, ZU_V + 16 * c) for c in range(3)]
    v_above = [face(za, ZD_V + 16 * c) for c in range(3)]
    for i, z, at, pulls, weight, place, speeds in (
        (0, -1, 1, low_f[1], low_m[1], below[1], v_below),
        (1, 0, 2, low_f[2], low_m[2], first, [v[c, 0] for c in range(3)]),
        (8, 7, 3, high_f[0], high_m[0], last, [v[c, 7] for c in range(3)]),
        (9, 8, 4, high_f[1], high_m[1], above[0], v_above),
    ):
        inner = 0 <= z < 8
        edges = [col_m[side, at : at + 1, :] for side in (0, 1)]
        if inner:
            weight = weight + mass[z]
            edges = [edges[side] + in_m[side, z : z + 1, :] for side in (0, 1)]
        rate = DT / (LUMPED + with_columns(weight, *edges))
        dtm[i] = rate
        for c in range(3):
            pull = fold_node(pulls[c])
            edges = [col_f[side, c, at : at + 1, :] for side in (0, 1)]
            if inner:
                pull = pull + force[c, z]
                edges = [edges[side] + in_f[side, c, z : z + 1, :] for side in (0, 1)]
            speed = speeds[c] - rate * with_columns(pull, *edges)
            v1[c, i] = speed
            u1[c, i] = place[c] + DT * speed
    dtm[2:8] = dtmi[...]
    for c in range(3):
        u1[c, 2:8] = ui[c]
        v1[c, 2:8] = vi[c]

    @pl.when(layer == layers // 2)
    def _():
        for c in range(3):
            for i in (0, 1):
                u1[c, 4 + i] = u_face[i, c]
                v1[c, 4 + i] = v_face[i, c]

    for x, row in ((15, NEW_HI), (0, NEW_LO)):
        for c in range(3):
            ends[row + 16 * c : row + 16 * c + 8, :] = u1[c, 0:8, x, :]
            ends[row + 16 * c + 8 : row + 16 * c + 16, :] = jnp.zeros((8, 256), F32)
            ends[row + 16 * c + 8 : row + 16 * c + 10, :] = u1[c, 8:10, x, :]


def pack_new_cross(ends, values, mate, out):
    out[0:48, :] = jnp.where(on_even(), ends[NEW_LO : NEW_LO + 48, :], ends[NEW_HI : NEW_HI + 48, :])
    for row, src, role in ((CROSS_OWN, mate, OPP2), (CROSS_MATE, values, FAR1), (CROSS_ON, values, FAR2)):
        out[row : row + 4, :] = src[4 * role : 4 * role + 4, :]
    out[60:64, :] = jnp.zeros((4, 256), F32)


def pack_last(ends, far, out):
    out[0:48, :] = jnp.where(on_even(), ends[NEW_HI : NEW_HI + 48, :], ends[NEW_LO : NEW_LO + 48, :])
    out[48:64, :] = far[48:64, :]


def second_block(blocks, layers, u, dt, lab, par, zb, cols, force, fields, le, de, col, modes, saved):
    layer, here = lax.axis_index("layer"), lax.axis_index("plane")
    mats = material_scalars(par)
    le[0] = zb[ZU_LAB + 16 : ZU_LAB + 32, :]
    de[0] = zb[ZU_DT + 16 : ZU_DT + 32, :]
    le[1:9] = lab[...].astype(F32)
    de[1:9] = dt[...]
    row = iota((16, 256), 0)
    zg = row + (layer * 8 - 1)
    ok = (zg >= 0) & (zg <= layers * 8 - 2) & (zg != layers // 2 * 8 + 3) & (row < 9) & (iota((16, 256), 1) < 255)
    for at in (0, 1):
        right_side = on_even() if at else jnp.logical_not(on_even())
        for i, (field, first, zu, zuf) in enumerate(
            ((lab, COL_LAB, ZU_CLAB, ZU_LAB), (dt, COL_DT, ZU_CDT, ZU_DT))
        ):
            col[i, 8:16, :] = jnp.zeros((8, 256), F32)
            col[i, 0:1, :] = jnp.where(right_side, zb[zuf + 31 : zuf + 32, :], zb[zu + 1 : zu + 2, :])
            col[i, 1:9, :] = jnp.where(right_side, field[:, 15, :].astype(F32), cols[first : first + 8, :])
        inside = jnp.where(right_side, here < blocks - 1, here > 0)
        mask = jnp.where(ok & inside, 1.0, 0.0)
        for i, value in enumerate(cell_fields(mats, col[0], col[1], mask, False)[:4]):
            fields[at, i] = value
    block_forces(layers, 9, 3, layer * 8 - 1, mats, u, le, de, modes, saved, None, force, None)


def second_column(at, fields, ends, theirs):
    right_side = on_even() if at else jnp.logical_not(on_even())
    left, right = [], []
    for c in range(3):
        hi, lo, other = NEW_HI + 16 * c, NEW_LO + 16 * c, theirs[16 * c : 16 * c + 16, :]
        left.append(jnp.where(right_side, ends[hi : hi + 16, :], other))
        right.append(jnp.where(right_side, other, ends[lo : lo + 16, :]))
    side = jnp.where(right_side, -1.0, 1.0)
    return column_part([fields[at, i] for i in range(4)], side, left, right)


def second_step(u, v, dtm, force, fields, ends, far, u2, v2, col_f):
    even = on_even()
    forces = second_column(0, fields, ends, far)
    for c in range(3):
        col_f[0, c] = jnp.where(even, forces[c], 0.0)
        col_f[1, c] = jnp.where(even, 0.0, forces[c])
    for z in range(8):
        e = z + 1
        rate = dtm[e]
        for c in range(3):
            pull = with_columns(force[c, e], col_f[0, c, e : e + 1, :], col_f[1, c, e : e + 1, :])
            speed = v[c, e] - rate * pull
            v2[c, z] = speed
            u2[c, z] = u[c, e] + DT * speed


def second_contact(
    layers, u_in, v_in, dtm, lists, mate, far, opp, fields, ends, u2, v2, u, v, col_f, sems
):
    even = on_even()
    on_face = lax.axis_index("layer") == layers // 2
    forces = second_column(1, fields, ends, opp)
    for c in range(3):
        col_f[0, c] = jnp.where(even, 0.0, forces[c])
        col_f[1, c] = jnp.where(even, forces[c], 0.0)

    def update(z, extra):
        e = z + 1
        rate = dtm[e]
        for c in range(3):
            pull = with_columns(jnp.zeros((16, 256), F32), col_f[0, c, e : e + 1, :], col_f[1, c, e : e + 1, :])
            if extra is not None:
                pull = pull - jnp.where(on_face, extra[c], 0.0)
            change = rate * pull
            v[c, z] = v_in[c, z] - change
            u[c, z] = u_in[c, z] - DT * change

    def copy_out(first, last):
        for src, dst in ((u, u2), (v, v2)):
            copy = pltpu.make_async_copy(src.at[:, first:last], dst.at[:, first:last], sems.at[len(copies)])
            copy.start()
            copies.append(copy)

    copies = []
    for first in (0, 5):
        for z in range(first, first + 3):
            update(z, None)
        copy_out(first, first + 3)
    sol_y, sol_x = one_hots(lists[0:1, :])
    land_y, land_x = one_hots(lists[6:7, :])

    def values(i):
        half = slice(128 * (i % 2), 128 * (i % 2) + 128)
        own_row = (3, 4, 5, 8, 9, 10)[i]
        places = (
            (mate, 4 * NEAR), (far, CROSS_MATE), None, (far, CROSS_OWN), (opp, CROSS_ON)
        )
        parts = [
            lists[own_row : own_row + 1, 256:384] if place is None
            else place[0][place[1] + i // 2 : place[1] + i // 2 + 1, half]
            for place in places
        ]
        return jnp.concatenate(parts, axis=1)

    far_bump = jnp.concatenate([values(i) for i in range(3)], axis=0)
    far_pad = jnp.concatenate([values(i) for i in range(3, 6)], axis=0)
    on_bump = lists[2:3, :] * (far_pad - lists[3:6, :])
    on_pad = lists[7:8, :] * (far_bump - lists[8:11, :])
    extra = (scatter(on_pad, land_y, land_x), scatter(on_bump, sol_y, sol_x))
    for z in (3, 4):
        update(z, extra[z - 3])
    copy_out(3, 5)
    for copy in copies:
        copy.wait()


VM = pl.BlockSpec(memory_space=pltpu.VMEM)
SM = pl.BlockSpec(memory_space=pltpu.SMEM)
HBM = pl.BlockSpec(memory_space=pltpu.HBM)


def call(kernel, in_specs, outs, scratch, name, flops, vmem=32, out_spec=VM):
    return pl.pallas_call(
        kernel,
        out_shape=[jax.ShapeDtypeStruct(shape, F32) for shape in outs],
        in_specs=in_specs,
        out_specs=[out_spec] * len(outs),
        scratch_shapes=[pltpu.VMEM(s, F32) if isinstance(s, tuple) else s for s in scratch],
        compiler_params=pltpu.CompilerParams(vmem_limit_bytes=vmem * 1024 * 1024),
        cost_estimate=pl.CostEstimate(flops=flops, bytes_accessed=flops // 25, transcendentals=0),
        name=name,
    )


def local(u, v, dt, lab, par, sol, land, stiff, tally):
    blocks, layers = lax.axis_size("plane"), lax.axis_size("layer")
    swaps = [(s, s ^ 1) for s in range(blocks)]
    crossings = [(s, s + 2 - 4 * (s % 2)) for s in range(blocks) if 0 <= s + 2 - 4 * (s % 2) < blocks]
    face_swaps = [(a * layers + layers // 2, b * layers + layers // 2) for a, b in swaps]

    def along_layer(value, steps):
        pairs = [(s, s + steps) for s in range(layers) if 0 <= s + steps < layers]
        return lax.ppermute(value, "layer", pairs)

    own = call(
        functools.partial(pack_export, blocks, layers),
        [HBM] * 7,
        [(EXPORT_ROWS, 256)],
        [u.shape, dt.shape, pltpu.VMEM(lab.shape, jnp.int32)]
        + [pltpu.VMEM((5, 1, 128), jnp.int32)] * 2
        + [(5, 1, 128), pltpu.SMEM((1, 5), jnp.int32), pltpu.VMEM((8, 640), jnp.int32)]
        + [pltpu.VMEM((256, 640), BF16), (16, 640), pltpu.SemaphoreType.DMA((7,))],
        "pack_export",
        100_000,
        63,
    )(u, dt, lab, sol.reshape(5, 1, 128), land.reshape(5, 1, 128), stiff.reshape(5, 1, 128), tally)[0]
    near = lax.ppermute(own, "plane", swaps)
    own = call(stage, [HBM], [own.shape], [pltpu.SemaphoreType.DMA], "stage", 100_000)(own)[0]
    cross, skip = call(pack_cross, [VM] * 2, [(CROSS_ROWS, 256), (SKIP_ROWS, 256)], [], "pack_cross", 1_000)(own, near)
    far = lax.ppermute(cross, "plane", crossings)
    skips = [(s * layers + layers // 2, t * layers + layers // 2) for t, s in crossings]
    opp = lax.ppermute(skip, ("plane", "layer"), skips)
    modes = [(12, 16, 256), (12, 16, 256)]
    plane = (16, 256)
    force, mass = call(
        functools.partial(first_block, layers),
        [VM] * 3 + [SM],
        [(3, 8, 16, 256), (8, 16, 256)],
        modes + [plane],
        "first_block",
        50_000_000,
    )(u, dt, lab, par)
    far, force, mass = lax.optimization_barrier((far, force, mass))
    up, dn, cols = call(
        pack_layer, [VM] * 6, [(ZU_ROWS, 256), (ZD_ROWS, 256), (COLS_ROWS, 256)], [], "pack_layer", 1_000
    )(u, v, dt, lab, near, far)
    zb, za = along_layer(up, 1), along_layer(dn, -1)
    u1, v1, dtm, in_f, in_m = call(
        functools.partial(first_inner, blocks, layers),
        [VM] * 2 + [SM] + [VM] * 4,
        [(3, 6, 16, 256), (3, 6, 16, 256), (6, 16, 256), (2, 3, 8, 256), (2, 8, 256)],
        [],
        "first_inner",
        1_000,
    )(u, v, par, own, cols, force, mass)
    opp, u1, v1 = lax.optimization_barrier((opp, u1, v1))
    u_face, v_face, values, lists = call(
        functools.partial(first_contact, layers),
        [VM] * 7,
        [(2, 3, 16, 256), (2, 3, 16, 256), (VALUES_ROWS, 256), (16, 640)],
        [],
        "first_contact",
        10_000_000,
    )(own, near, far, opp, u1, v1, dtm)
    mate = lax.ppermute(values, ("plane", "layer"), face_swaps)

    two = (2, 8, 256)
    u1, v1, dtm, ends = call(
        functools.partial(first_step, blocks, layers),
        [VM] * 4 + [SM] + [VM] * 13,
        [(3, 10, 16, 256), (3, 10, 16, 256), (10, 16, 256), (NEW_ROWS, 256)],
        [(4, 3, 8, 256), two, two, (2, 3, 8, 256), two],
        "first_step",
        20_000_000,
    )(u, v, dt, lab, par, own, cols, zb, za, force, mass, in_f, in_m, u1, v1, dtm, u_face, v_face)
    across = [(s, s + 1) for s in range(1, blocks - 1, 2)] + [(s, s - 1) for s in range(2, blocks, 2)]
    cross = call(pack_new_cross, [VM] * 3, [(NEW_CROSS_ROWS, 256)], [], "pack_new_cross", 100_000)(ends, values, mate)[0]
    far = lax.ppermute(cross, "plane", across)
    force, fields = call(
        functools.partial(second_block, blocks, layers),
        [VM] * 3 + [SM] + [VM] * 2,
        [(3, 10, 16, 256), (2, 4, 16, 256)],
        [(9, 16, 256), (9, 16, 256), (2, 16, 256)] + modes,
        "second_block",
        50_000_000,
    )(u1, dt, lab, par, zb, cols)
    far, force = lax.optimization_barrier((far, force))
    last = call(pack_last, [VM] * 2, [(NEW_CROSS_ROWS, 256)], [], "pack_last", 100_000)(ends, far)[0]
    opp = lax.ppermute(last, "plane", swaps)
    u2, v2 = call(
        second_step, [VM] * 7, [(3, 8, 16, 256)] * 2, [(2, 3, 16, 256)], "second_step", 20_000_000
    )(u1, v1, dtm, force, fields, ends, far)
    return tuple(
        call(
            functools.partial(second_contact, layers),
            [VM] * 9,
            [(3, 8, 16, 256)] * 2,
            [(3, 8, 16, 256)] * 2 + [(2, 3, 16, 256), pltpu.SemaphoreType.DMA((6,))],
            "second_contact",
            10_000_000,
            out_spec=HBM,
        )(u2, v2, dtm, lists, mate, far, opp, fields, ends)
    )


def solution(mesh):
    in_specs = (
        P(None, "layer", "plane", None),
        P(None, "layer", "plane", None),
        P("layer", "plane", None),
        P("layer", "plane", None),
        P(),
        P("plane", None, None),
        P("plane", None, None),
        P("plane", None, None),
        P("plane", None),
    )
    out_specs = (P(None, "layer", "plane", None), P(None, "layer", "plane", None))
    return jax.shard_map(local, mesh=mesh, in_specs=in_specs, out_specs=out_specs, check_vma=False)
```

```python
import functools

import jax
import jax.numpy as jnp
from jax import lax
from jax.experimental import pallas as pl
from jax.experimental.pallas import tpu as pltpu
from jax.sharding import PartitionSpec as P

DT = 0.05
LUMPED = 0.25
F32 = jnp.float32
BF16 = jnp.bfloat16
QUADS = ((0, 0), (0, 1), (1, 0), (1, 1))

COL_HI, COL_LO, LISTS, PAD, EXPORT_ROWS = 0, 40, 64, 88, 136
OWN_OPP2, MATE_FAR1, OWN_PAD, MATE_PAD, CROSS_ROWS = 40, 44, 48, 96, 144
SKIP_LIST, SKIP_PAD, SKIP_ROWS = 0, 8, 232
COL_LAB, COL_DT, COL_BEYOND, COLS_ROWS = 24, 32, 40, 64
ZU_U, ZU_V, ZU_LAB, ZU_DT, ZU_CL, ZU_CH, ZU_CLAB, ZU_CDT, ZU_ROWS = 0, 96, 144, 176, 208, 214, 220, 222, 224
ZD_U, ZD_V, ZD_LAB, ZD_DT, ZD_CL, ZD_CH, ZD_CLAB, ZD_CDT, ZD_ROWS = 0, 96, 144, 160, 176, 182, 188, 189, 192
NEW_HI, NEW_LO, NEW_ROWS, VALUES_ROWS = 0, 48, 96, 24
CROSS_OWN, CROSS_MATE, CROSS_ON, NEW_CROSS_ROWS = 48, 52, 56, 64
NEAR, FAR1, OWN, FAR2, OPP2 = range(5)
OFFSETS = (1, -1, 0, -2, 2)


def iota(shape, dim):
    return lax.broadcasted_iota(jnp.int32, shape, dim)


def on_even():
    return lax.rem(lax.axis_index("plane"), 2) == 0


def role_offset(role):
    return jnp.where(on_even(), OFFSETS[role], -OFFSETS[role])


def pack_export(
    blocks, layers,
    u_hbm, dt_hbm, lab_hbm, sol_hbm, land_hbm, stiff_hbm, tally_hbm,
    out,
    u, dt, lab, sol, land, stiff, tally, pos, ohy, ohx, sems,
):
    copies = [
        pltpu.make_async_copy(src, dst, sems.at[i])
        for i, (src, dst) in enumerate(
            (
                (u_hbm, u), (dt_hbm, dt), (lab_hbm, lab), (sol_hbm, sol),
                (land_hbm, land), (stiff_hbm, stiff), (tally_hbm, tally),
            )
        )
    ]
    for copy in copies:
        copy.start()
    for copy in copies[3:]:
        copy.wait()
    pad_z = u.shape[1] // 2 - 1
    here = lax.axis_index("plane")
    on_face = lax.axis_index("layer") == layers // 2

    @pl.when(on_face)
    def _():
        out[LISTS : LISTS + 24, :] = jnp.zeros((24, 256), F32)
        for k in range(5):
            row = LISTS + 4 * k
            target = here + (k - 2)
            count = jnp.where((target >= 0) & (target < blocks), tally[0, k], 0)
            live = iota((1, 128), 1) < count
            out[row : row + 1, 0:128] = sol[k].astype(F32)
            out[row : row + 1, 128:256] = land[k].astype(F32)
            out[row + 1 : row + 2, 0:128] = jnp.where(live, stiff[k], 0.0)
            pos[0:1, 128 * k : 128 * k + 128] = sol[k]
        ohy[...], ohx[...] = one_hots(pos[0:1, :])

    for copy in copies[:3]:
        copy.wait()
    for x, row in ((15, COL_HI), (0, COL_LO)):
        for c in range(3):
            out[row + 8 * c : row + 8 * c + 8, :] = u[c, :, x, :]
    out[COL_HI + COL_LAB : COL_HI + COL_LAB + 8, :] = lab[:, 15, :].astype(F32)
    out[COL_HI + COL_DT : COL_HI + COL_DT + 8, :] = dt[:, 15, :]

    @pl.when(on_face)
    def _():
        bump = gather(jnp.concatenate([u[c, pad_z + 1] for c in range(3)], axis=0), ohy[...], ohx[...])
        for k in range(5):
            row, cols = LISTS + 4 * k, slice(128 * k, 128 * k + 128)
            out[row + 1 : row + 2, 128:256] = bump[0:1, cols]
            out[row + 2 : row + 3, 0:128] = bump[1:2, cols]
            out[row + 2 : row + 3, 128:256] = bump[2:3, cols]
        for c in range(3):
            out[PAD + 16 * c : PAD + 16 * c + 16, :] = u[c, pad_z]


def stage(src, dst, sem):
    copy = pltpu.make_async_copy(src, dst, sem)
    copy.start()
    copy.wait()


def pack_cross(own, mate, out, skip):
    even = on_even()

    def bucket(ref, if_even, if_odd):
        a, b = LISTS + 4 * if_even, LISTS + 4 * if_odd
        return jnp.where(even, ref[a : a + 4, :], ref[b : b + 4, :])

    out[24:40, :] = mate[COL_HI + 24 : COL_HI + 40, :]
    out[0:24, :] = jnp.where(even, mate[COL_HI : COL_HI + 24, :], mate[COL_LO : COL_LO + 24, :])
    out[OWN_OPP2 : OWN_OPP2 + 4, :] = bucket(own, 4, 0)
    out[MATE_FAR1 : MATE_FAR1 + 4, :] = bucket(mate, 3, 1)
    out[OWN_PAD : OWN_PAD + 48, :] = own[PAD : PAD + 48, :]
    out[MATE_PAD : MATE_PAD + 48, :] = mate[PAD : PAD + 48, :]
    skip[SKIP_LIST : SKIP_LIST + 4, :] = bucket(own, 0, 4)
    skip[SKIP_LIST + 4 : SKIP_PAD, :] = jnp.zeros((4, 256), F32)
    skip[SKIP_PAD : SKIP_PAD + 48, :] = own[PAD : PAD + 48, :]


def pack_layer(u, v, dt, lab, near, far, up, dn, cols):
    even = on_even()
    cols[0:40, :] = jnp.where(even, far[0:40, :], near[COL_HI : COL_HI + 40, :])
    cols[COL_BEYOND : COL_BEYOND + 24, :] = jnp.where(even, near[COL_LO : COL_LO + 24, :], far[0:24, :])
    for c in range(3):
        for zz in (0, 1):
            row = 16 * (2 * c + zz)
            up[ZU_U + row : ZU_U + row + 16, :] = u[c, 6 + zz]
            dn[ZD_U + row : ZD_U + row + 16, :] = u[c, zz]
        up[ZU_V + 16 * c : ZU_V + 16 * c + 16, :] = v[c, 7]
        dn[ZD_V + 16 * c : ZD_V + 16 * c + 16, :] = v[c, 0]
        lo, hi = 8 * c, COL_BEYOND + 8 * c
        up[ZU_CL + 2 * c : ZU_CL + 2 * c + 2, :] = cols[lo + 6 : lo + 8, :]
        up[ZU_CH + 2 * c : ZU_CH + 2 * c + 2, :] = cols[hi + 6 : hi + 8, :]
        dn[ZD_CL + 2 * c : ZD_CL + 2 * c + 2, :] = cols[lo : lo + 2, :]
        dn[ZD_CH + 2 * c : ZD_CH + 2 * c + 2, :] = cols[hi : hi + 2, :]
    for zz in (0, 1):
        up[ZU_LAB + 16 * zz : ZU_LAB + 16 * zz + 16, :] = lab[6 + zz].astype(F32)
        up[ZU_DT + 16 * zz : ZU_DT + 16 * zz + 16, :] = dt[6 + zz]
    up[ZU_CLAB : ZU_CLAB + 2, :] = cols[COL_LAB + 6 : COL_LAB + 8, :]
    up[ZU_CDT : ZU_CDT + 2, :] = cols[COL_DT + 6 : COL_DT + 8, :]
    dn[ZD_LAB : ZD_LAB + 16, :] = lab[0].astype(F32)
    dn[ZD_DT : ZD_DT + 16, :] = dt[0]
    dn[ZD_CLAB : ZD_CLAB + 1, :] = cols[COL_LAB : COL_LAB + 1, :]
    dn[ZD_CDT : ZD_CDT + 1, :] = cols[COL_DT : COL_DT + 1, :]
    dn[ZD_CDT + 1 : ZD_ROWS, :] = jnp.zeros((ZD_ROWS - ZD_CDT - 1, 256), F32)


def material_scalars(par):
    out = []
    for m in range(4):
        lam, mu, alpha, rho = par[0, m], par[1, m], par[2, m], par[3, m]
        out.append(
            (
                lam * (1.0 / 16.0),
                mu * (1.0 / 16.0),
                (lam + 4.0 * mu) * (1.0 / 144.0),
                (3.0 * lam + 2.0 * mu) * alpha * 0.25,
                rho * 0.125,
            )
        )
    return out


def cell_fields(mats, lab, dt, mask, with_mass):
    is0, is1, is2 = lab == 0.0, lab == 1.0, lab == 2.0

    def pick(i):
        rest = jnp.where(is2, mats[2][i], mats[3][i])
        return jnp.where(is0, mats[0][i], jnp.where(is1, mats[1][i], rest)) * mask

    return pick(0), pick(1), pick(2), pick(3) * dt, pick(4) if with_mass else None


def plane_modes(u, ux):
    s, d = u + ux, ux - u
    sy, dy = pltpu.roll(s, 255, 1), pltpu.roll(d, 255, 1)
    return [s + sy, sy - s, d + dy, dy - d]


def cell_forces(lower, upper, l1, m1, k3, th):
    z, x, y = (
        {
            (i, j, k): (upper[c][q] - lower[c][q]) if i else (upper[c][q] + lower[c][q])
            for q, (j, k) in enumerate(QUADS)
            for i in (0, 1)
            if i + j + k
        }
        for c in range(3)
    )
    l2, m2 = l1 * (1.0 / 3.0), m1 * (1.0 / 3.0)
    p0 = l1 * (z[1, 0, 0] + x[0, 1, 0] + y[0, 0, 1]) - th
    m1x2 = m1 + m1
    zx = m1 * (x[1, 0, 0] + z[0, 1, 0])
    zy = m1 * (y[1, 0, 0] + z[0, 0, 1])
    xy = m1 * (y[0, 1, 0] + x[0, 0, 1])
    pz = l2 * (x[1, 1, 0] + y[1, 0, 1])
    px = l2 * (z[1, 1, 0] + y[0, 1, 1])
    py = l2 * (z[1, 0, 1] + x[0, 1, 1])
    tw = z[0, 1, 1] + x[1, 0, 1] + y[1, 1, 0]
    fz = {
        (1, 0, 0): p0 + m1x2 * z[1, 0, 0],
        (0, 1, 0): zx,
        (0, 0, 1): zy,
        (1, 1, 0): px + m1 * z[1, 1, 0],
        (1, 0, 1): py + m1 * z[1, 0, 1],
        (0, 1, 1): m2 * (tw + z[0, 1, 1]),
        (1, 1, 1): k3 * z[1, 1, 1],
    }
    fx = {
        (0, 1, 0): p0 + m1x2 * x[0, 1, 0],
        (1, 0, 0): zx,
        (0, 0, 1): xy,
        (1, 1, 0): pz + m1 * x[1, 1, 0],
        (0, 1, 1): py + m1 * x[0, 1, 1],
        (1, 0, 1): m2 * (tw + x[1, 0, 1]),
        (1, 1, 1): k3 * x[1, 1, 1],
    }
    fy = {
        (0, 0, 1): p0 + m1x2 * y[0, 0, 1],
        (1, 0, 0): zy,
        (0, 1, 0): xy,
        (1, 0, 1): pz + m1 * y[1, 0, 1],
        (0, 1, 1): px + m1 * y[0, 1, 1],
        (1, 1, 0): m2 * (tw + y[1, 1, 0]),
        (1, 1, 1): k3 * y[1, 1, 1],
    }
    low, high = [], []
    for f in (fz, fx, fy):
        low_c, high_c = [], []
        for j, k in QUADS:
            d = f[1, j, k]
            if j + k:
                s = f[0, j, k]
                low_c.append(s - d)
                high_c.append(s + d)
            else:
                low_c.append(-d)
                high_c.append(d)
        low.append(low_c)
        high.append(high_c)
    return low, high


def fold_y(a, b):
    return (a - b) + pltpu.roll(a + b, 1, 1)


def column_forces(layers, zg, valid, mats, inside, side, left, right, lab, dt, with_mass):
    rows = lab.shape[0]
    shape = (rows, 256)
    ok = (zg >= 0) & (zg <= layers * 8 - 2) & (zg != layers // 2 * 8 + 3) & (iota(shape, 1) < 255)
    mask = jnp.where(ok & valid & inside, 1.0, 0.0)
    *fields, rho = cell_fields(mats, lab, dt, mask, with_mass)
    if with_mass:
        rho = rho + pltpu.roll(rho, 1, 1)
        rho = rho + pltpu.roll(rho, 1, 0)
    return column_part(fields, side, left, right), rho


def column_part(fields, side, left, right):
    rows = left[0].shape[0]
    lower = [plane_modes(left[c], right[c]) for c in range(3)]
    upper = [[pltpu.roll(a, rows - 1, 0) for a in comp] for comp in lower]
    low, high = cell_forces(lower, upper, *fields)
    forces = []
    for c in range(3):
        node = [low[c][q] + pltpu.roll(high[c][q], 1, 0) for q in range(4)]
        t0, t1 = fold_y(node[0], node[1]), fold_y(node[2], node[3])
        forces.append(t0 + side * t1)
    return forces


def block_forces(layers, cells, group, zbase, mats, u, lab, dt, modes, saved, saved_m, force, mass):
    shape = (16, 256)
    row, lane = iota(shape, 0), iota(shape, 1)
    in_plane = jnp.where((lane < 255) & (row < 15), 1.0, 0.0)

    def forward(e, c):
        a = u[c, e]
        return plane_modes(a, pltpu.roll(a, 15, 0))

    for c in range(3):
        for q, value in enumerate(forward(0, c)):
            modes[4 * c + q] = value
            saved[4 * c + q] = jnp.zeros(shape, F32)
    if mass is not None:
        saved_m[...] = jnp.zeros(shape, F32)

    def fold(e, node):
        for c in range(3):
            t0, t1 = fold_y(node[c][0], node[c][1]), fold_y(node[c][2], node[c][3])
            force[c, e] = (t0 - t1) + pltpu.roll(t0 + t1, 1, 0)

    def body(i, carry):
        lower = [[modes[4 * c + q] for q in range(4)] for c in range(3)]
        held = [[saved[4 * c + q] for q in range(4)] for c in range(3)]
        held_m = None if mass is None else saved_m[...]
        for g in range(group):
            e = i * group + g
            zg = zbase + e
            ok = (zg >= 0) & (zg <= layers * 8 - 2) & (zg != layers // 2 * 8 + 3)
            mask = in_plane * jnp.where(ok, 1.0, 0.0)
            l1, m1, k3, th, rho = cell_fields(mats, lab[e].astype(F32), dt[e], mask, mass is not None)
            upper = [forward(e + 1, c) for c in range(3)]
            low, high = cell_forces(lower, upper, l1, m1, k3, th)
            fold(e, [[low[c][q] + held[c][q] for q in range(4)] for c in range(3)])
            lower, held = upper, high
            if mass is not None:
                rho = rho + pltpu.roll(rho, 1, 1)
                rho = rho + pltpu.roll(rho, 1, 0)
                mass[e] = rho + held_m
                held_m = rho
        for c in range(3):
            for q in range(4):
                modes[4 * c + q] = lower[c][q]
                saved[4 * c + q] = held[c][q]
        if mass is not None:
            saved_m[...] = held_m
        return carry

    lax.fori_loop(0, cells // group, body, 0)
    fold(cells, [[saved[4 * c + q] for q in range(4)] for c in range(3)])
    if mass is not None:
        mass[cells] = saved_m[...]


def two_layers(layers, z, mats, nodes, lab, dt):
    shape = (16, 256)
    in_plane = jnp.where((iota(shape, 1) < 255) & (iota(shape, 0) < 15), 1.0, 0.0)
    modes = [[plane_modes(a, pltpu.roll(a, 15, 0)) for a in node] for node in nodes]
    parts, masses = [], []
    for i in (0, 1):
        zg = z + i
        ok = (zg >= 0) & (zg <= layers * 8 - 2) & (zg != layers // 2 * 8 + 3)
        mask = in_plane * jnp.where(ok, 1.0, 0.0)
        l1, m1, k3, th, rho = cell_fields(mats, lab[i], dt[i], mask, True)
        parts.append(cell_forces(modes[i], modes[i + 1], l1, m1, k3, th))
        rho = rho + pltpu.roll(rho, 1, 1)
        masses.append(rho + pltpu.roll(rho, 1, 0))
    (low0, high0), (low1, high1) = parts
    middle = [[high0[c][q] + low1[c][q] for q in range(4)] for c in range(3)]
    return (low0, middle, high1), (masses[0], masses[0] + masses[1], masses[1])


def fold_node(node):
    t0, t1 = fold_y(node[0], node[1]), fold_y(node[2], node[3])
    return (t0 - t1) + pltpu.roll(t0 + t1, 1, 0)


def with_columns(a, first, last):
    row = iota((8, 256), 0)
    top = a[0:8] + jnp.where(row == 0, jnp.broadcast_to(first, (8, 256)), 0.0)
    bottom = a[8:16] + jnp.where(row == 7, jnp.broadcast_to(last, (8, 256)), 0.0)
    return jnp.concatenate([top, bottom], axis=0)


def split3(a):
    hi = a.astype(BF16)
    rest = a - hi.astype(F32)
    mid = rest.astype(BF16)
    lo = (rest - mid.astype(F32)).astype(BF16)
    return jnp.concatenate([hi, mid, lo], axis=0)


def join3(a):
    n = a.shape[0] // 3
    return (a[:n] + a[n : 2 * n]) + a[2 * n :]


def one_hots(position):
    pos = position.astype(jnp.int32)
    n = pos.shape[1]
    y, x = pos & 255, pos >> 8
    ohy = jnp.where(iota((256, n), 0) == y, 1.0, 0.0).astype(BF16)
    ohx = jnp.where(iota((16, n), 0) == x, 1.0, 0.0)
    return ohy, ohx


def gather(face, ohy, ohx):
    n = ohx.shape[1]
    rows = join3(jnp.dot(split3(face), ohy, preferred_element_type=F32))
    return jnp.sum(rows.reshape(3, 16, n) * ohx[None], axis=1)


def scatter(values, ohy, ohx):
    n = ohx.shape[1]
    rows = (values[:, None, :] * ohx[None]).reshape(48, n)
    out = lax.dot_general(split3(rows), ohy, (((1,), (1,)), ((), ())), preferred_element_type=F32)
    return join3(out).reshape(3, 16, 256)


def fill_lists(own, near, far, opp, lists):
    sources = {
        NEAR: (near, LISTS + 4 * (2 - role_offset(NEAR))),
        FAR1: (far, MATE_FAR1),
        OWN: (own, LISTS + 8),
        FAR2: (far, OWN_OPP2),
        OPP2: (opp, SKIP_LIST),
    }
    for role, (ref, base) in sources.items():
        cols = slice(128 * role, 128 * role + 128)
        row = LISTS + 4 * (2 + role_offset(role))
        for i in range(3):
            mine, other = own[pl.ds(row + i, 1), :], ref[pl.ds(base + i, 1), :]
            for half in (0, 1):
                part = slice(128 * half, 128 * half + 128)
                lists[2 * i + half : 2 * i + half + 1, cols] = mine[:, part]
                if i + half:
                    lists[5 + 2 * i + half : 6 + 2 * i + half, cols] = other[:, part]


def first_block(layers, u, dt, lab, par, force, mass, modes, saved, saved_m):
    zbase = lax.axis_index("layer") * 8
    block_forces(layers, 7, 7, zbase, material_scalars(par), u, lab, dt, modes, saved, saved_m, force, mass)


def first_inner(
    blocks, layers, u, v, par, own, cols, force, mass, u1, v1, dtm, col_f, col_m
):
    here = lax.axis_index("plane")
    mats = material_scalars(par)
    row = iota((8, 256), 0)
    for at, inside, side in ((0, here > 0, 1), (1, here < blocks - 1, -1)):
        first = COL_LO if at == 0 else COL_HI
        mine = [own[first + 8 * c : first + 8 * c + 8, :] for c in range(3)]
        beyond = COL_BEYOND if at else 0
        theirs = [cols[beyond + 8 * c : beyond + 8 * c + 8, :] for c in range(3)]
        left, right = (mine, theirs) if at else (theirs, mine)
        ref = own if at else cols
        forces, rho = column_forces(
            layers, row + lax.axis_index("layer") * 8, row < 7, mats, inside, side, left, right,
            ref[COL_LAB : COL_LAB + 8, :], ref[COL_DT : COL_DT + 8, :], True,
        )
        for c in range(3):
            col_f[at, c] = forces[c]
        col_m[at] = rho
    for i in range(6):
        z = i + 1
        rate = DT / (LUMPED + with_columns(mass[z], col_m[0, z : z + 1, :], col_m[1, z : z + 1, :]))
        dtm[i] = rate
        for c in range(3):
            pull = with_columns(force[c, z], col_f[0, c, z : z + 1, :], col_f[1, c, z : z + 1, :])
            speed = v[c, z] - rate * pull
            v1[c, i] = speed
            u1[c, i] = u[c, z] + DT * speed


def first_contact(layers, own, near, far, opp, u1, v1, dtm, u_face, v_face, out, lists):
    @pl.when(lax.axis_index("layer") == layers // 2)
    def _():
        fill_lists(own, near, far, opp, lists)
        sol_y, sol_x = one_hots(lists[0:1, :])
        land_y, land_x = one_hots(lists[6:7, :])
        far_y, far_x = one_hots(lists[1:2, :])
        own_pad = own[PAD : PAD + 48, :]
        pads = {
            NEAR: near[PAD : PAD + 48, :],
            FAR1: far[MATE_PAD : MATE_PAD + 48, :],
            OWN: own_pad,
            FAR2: far[OWN_PAD : OWN_PAD + 48, :],
            OPP2: opp[SKIP_PAD : SKIP_PAD + 48, :],
        }
        far_pad = []
        for role in range(5):
            part = slice(128 * role, 128 * role + 128)
            far_pad.append(gather(pads[role], far_y[:, part], far_x[:, part]))
        on_bump = lists[2:3, :] * (jnp.concatenate(far_pad, axis=1) - lists[3:6, :])
        on_pad = lists[7:8, :] * (lists[8:11, :] - gather(own_pad, land_y, land_x))
        extra = (scatter(on_pad, land_y, land_x), scatter(on_bump, sol_y, sol_x))
        faces = []
        for face in (0, 1):
            new = []
            for c in range(3):
                change = dtm[2 + face] * extra[face][c]
                v_face[face, c] = v1[c, 2 + face] + change
                new.append(u1[c, 2 + face] + DT * change)
                u_face[face, c] = new[c]
            faces.append(jnp.concatenate(new, axis=0))
        lists[3:6, :] = gather(faces[1], sol_y, sol_x)
        lists[8:11, :] = gather(faces[0], land_y, land_x)
        for role in range(5):
            part = slice(128 * role, 128 * role + 128)
            for i, row in enumerate((3, 4, 5, 8, 9, 10)):
                at, half = 4 * role + i // 2, i % 2
                out[at : at + 1, 128 * half : 128 * half + 128] = lists[row : row + 1, part]


def first_step(
    blocks, layers,
    u, v, dt, lab, par, own, cols, zb, za, force, mass, in_f, in_m, ui, vi, dtmi, u_face, v_face,
    u1, v1, dtm, ends,
    col, col_lab, col_dt, col_f, col_m,
):
    layer, here = lax.axis_index("layer"), lax.axis_index("plane")
    mats = material_scalars(par)
    for c in range(3):
        for at, first, zu, zd in ((0, 0, ZU_CL, ZD_CL), (3, COL_BEYOND, ZU_CH, ZD_CH)):
            col[at, c, 0:2, :] = zb[zu + 2 * c : zu + 2 * c + 2, :]
            col[at, c, 2:3, :] = cols[first + 8 * c : first + 8 * c + 1, :]
            col[at, c, 3:4, :] = cols[first + 8 * c + 7 : first + 8 * c + 8, :]
            col[at, c, 4:6, :] = za[zd + 2 * c : zd + 2 * c + 2, :]
            col[at, c, 6:8, :] = jnp.zeros((2, 256), F32)
        for at, first, x in ((1, COL_LO, 0), (2, COL_HI, 15)):
            for zz in (0, 1):
                row = 16 * (2 * c + zz) + x
                col[at, c, zz : zz + 1, :] = zb[ZU_U + row : ZU_U + row + 1, :]
                col[at, c, 4 + zz : 5 + zz, :] = za[ZD_U + row : ZD_U + row + 1, :]
            col[at, c, 2:3, :] = own[first + 8 * c : first + 8 * c + 1, :]
            col[at, c, 3:4, :] = own[first + 8 * c + 7 : first + 8 * c + 8, :]
            col[at, c, 6:8, :] = jnp.zeros((2, 256), F32)
    for ref, first, zu, zd, zuf, zdf in (
        (col_lab, COL_LAB, ZU_CLAB, ZD_CLAB, ZU_LAB, ZD_LAB),
        (col_dt, COL_DT, ZU_CDT, ZD_CDT, ZU_DT, ZD_DT),
    ):
        for at in (0, 1):
            ref[at] = jnp.zeros((8, 256), F32)
        ref[0, 0:2, :] = zb[zu : zu + 2, :]
        ref[0, 3:4, :] = cols[first + 7 : first + 8, :]
        ref[0, 4:5, :] = za[zd : zd + 1, :]
        ref[1, 0:1, :] = zb[zuf + 15 : zuf + 16, :]
        ref[1, 1:2, :] = zb[zuf + 31 : zuf + 32, :]
        ref[1, 3:4, :] = own[COL_HI + first + 7 : COL_HI + first + 8, :]
        ref[1, 4:5, :] = za[zdf + 15 : zdf + 16, :]
    row = iota((8, 256), 0)
    zg = layer * 8 + jnp.where(row < 3, row - 2, row + 4)
    valid = (row < 5) & (row != 2)
    for at, inside, side in ((0, here > 0, 1), (1, here < blocks - 1, -1)):
        left = [col[2 * at, c] for c in range(3)]
        right = [col[2 * at + 1, c] for c in range(3)]
        forces, rho = column_forces(
            layers, zg, valid, mats, inside, side, left, right, col_lab[at], col_dt[at], True
        )
        for c in range(3):
            col_f[at, c] = forces[c]
        col_m[at] = rho

    def face(ref, row):
        return ref[row : row + 16, :]

    below = [[face(zb, ZU_U + 16 * (2 * c + zz)) for c in range(3)] for zz in (0, 1)]
    above = [[face(za, ZD_U + 16 * (2 * c + zz)) for c in range(3)] for zz in (0, 1)]
    first, last = [u[c, 0] for c in range(3)], [u[c, 7] for c in range(3)]
    low_f, low_m = two_layers(
        layers, layer * 8 - 2, mats, below + [first],
        (face(zb, ZU_LAB), face(zb, ZU_LAB + 16)), (face(zb, ZU_DT), face(zb, ZU_DT + 16)),
    )
    high_f, high_m = two_layers(
        layers, layer * 8 + 7, mats, [last] + above,
        (lab[7].astype(F32), face(za, ZD_LAB)), (dt[7], face(za, ZD_DT)),
    )
    v_below = [face(zb, ZU_V + 16 * c) for c in range(3)]
    v_above = [face(za, ZD_V + 16 * c) for c in range(3)]
    for i, z, at, pulls, weight, place, speeds in (
        (0, -1, 1, low_f[1], low_m[1], below[1], v_below),
        (1, 0, 2, low_f[2], low_m[2], first, [v[c, 0] for c in range(3)]),
        (8, 7, 3, high_f[0], high_m[0], last, [v[c, 7] for c in range(3)]),
        (9, 8, 4, high_f[1], high_m[1], above[0], v_above),
    ):
        inner = 0 <= z < 8
        edges = [col_m[side, at : at + 1, :] for side in (0, 1)]
        if inner:
            weight = weight + mass[z]
            edges = [edges[side] + in_m[side, z : z + 1, :] for side in (0, 1)]
        rate = DT / (LUMPED + with_columns(weight, *edges))
        dtm[i] = rate
        for c in range(3):
            pull = fold_node(pulls[c])
            edges = [col_f[side, c, at : at + 1, :] for side in (0, 1)]
            if inner:
                pull = pull + force[c, z]
                edges = [edges[side] + in_f[side, c, z : z + 1, :] for side in (0, 1)]
            speed = speeds[c] - rate * with_columns(pull, *edges)
            v1[c, i] = speed
            u1[c, i] = place[c] + DT * speed
    dtm[2:8] = dtmi[...]
    for c in range(3):
        u1[c, 2:8] = ui[c]
        v1[c, 2:8] = vi[c]

    @pl.when(layer == layers // 2)
    def _():
        for c in range(3):
            for i in (0, 1):
                u1[c, 4 + i] = u_face[i, c]
                v1[c, 4 + i] = v_face[i, c]

    for x, row in ((15, NEW_HI), (0, NEW_LO)):
        for c in range(3):
            ends[row + 16 * c : row + 16 * c + 8, :] = u1[c, 0:8, x, :]
            ends[row + 16 * c + 8 : row + 16 * c + 16, :] = jnp.zeros((8, 256), F32)
            ends[row + 16 * c + 8 : row + 16 * c + 10, :] = u1[c, 8:10, x, :]


def pack_new_cross(ends, values, mate, out):
    out[0:48, :] = jnp.where(on_even(), ends[NEW_LO : NEW_LO + 48, :], ends[NEW_HI : NEW_HI + 48, :])
    for row, src, role in ((CROSS_OWN, mate, OPP2), (CROSS_MATE, values, FAR1), (CROSS_ON, values, FAR2)):
        out[row : row + 4, :] = src[4 * role : 4 * role + 4, :]
    out[60:64, :] = jnp.zeros((4, 256), F32)


def pack_last(ends, far, out):
    out[0:48, :] = jnp.where(on_even(), ends[NEW_HI : NEW_HI + 48, :], ends[NEW_LO : NEW_LO + 48, :])
    out[48:64, :] = far[48:64, :]


def second_block(blocks, layers, u, dt, lab, par, zb, cols, force, fields, le, de, col, modes, saved):
    layer, here = lax.axis_index("layer"), lax.axis_index("plane")
    mats = material_scalars(par)
    le[0] = zb[ZU_LAB + 16 : ZU_LAB + 32, :]
    de[0] = zb[ZU_DT + 16 : ZU_DT + 32, :]
    le[1:9] = lab[...].astype(F32)
    de[1:9] = dt[...]
    row = iota((16, 256), 0)
    zg = row + (layer * 8 - 1)
    ok = (zg >= 0) & (zg <= layers * 8 - 2) & (zg != layers // 2 * 8 + 3) & (row < 9) & (iota((16, 256), 1) < 255)
    for at in (0, 1):
        right_side = on_even() if at else jnp.logical_not(on_even())
        for i, (field, first, zu, zuf) in enumerate(
            ((lab, COL_LAB, ZU_CLAB, ZU_LAB), (dt, COL_DT, ZU_CDT, ZU_DT))
        ):
            col[i, 8:16, :] = jnp.zeros((8, 256), F32)
            col[i, 0:1, :] = jnp.where(right_side, zb[zuf + 31 : zuf + 32, :], zb[zu + 1 : zu + 2, :])
            col[i, 1:9, :] = jnp.where(right_side, field[:, 15, :].astype(F32), cols[first : first + 8, :])
        inside = jnp.where(right_side, here < blocks - 1, here > 0)
        mask = jnp.where(ok & inside, 1.0, 0.0)
        for i, value in enumerate(cell_fields(mats, col[0], col[1], mask, False)[:4]):
            fields[at, i] = value
    block_forces(layers, 9, 3, layer * 8 - 1, mats, u, le, de, modes, saved, None, force, None)


def second_column(at, fields, ends, theirs):
    right_side = on_even() if at else jnp.logical_not(on_even())
    left, right = [], []
    for c in range(3):
        hi, lo, other = NEW_HI + 16 * c, NEW_LO + 16 * c, theirs[16 * c : 16 * c + 16, :]
        left.append(jnp.where(right_side, ends[hi : hi + 16, :], other))
        right.append(jnp.where(right_side, other, ends[lo : lo + 16, :]))
    side = jnp.where(right_side, -1.0, 1.0)
    return column_part([fields[at, i] for i in range(4)], side, left, right)


def second_ties(lists, part, places):
    def values(i):
        half = slice(128 * (i % 2), 128 * (i % 2) + 128)
        own_row = (3, 4, 5, 8, 9, 10)[i]
        parts = [
            lists[own_row : own_row + 1, 256:384] if place is None
            else place[0][place[1] + i // 2 : place[1] + i // 2 + 1, half]
            for place in places
        ]
        return jnp.concatenate(parts, axis=1) if len(parts) > 1 else parts[0]

    sol_y, sol_x = one_hots(lists[0:1, part])
    land_y, land_x = one_hots(lists[6:7, part])
    far_bump = jnp.concatenate([values(i) for i in range(3)], axis=0)
    far_pad = jnp.concatenate([values(i) for i in range(3, 6)], axis=0)
    on_bump = lists[2:3, part] * (far_pad - lists[3:6, part])
    on_pad = lists[7:8, part] * (far_bump - lists[8:11, part])
    return scatter(on_pad, land_y, land_x), scatter(on_bump, sol_y, sol_x)


def second_step(layers, u, v, dtm, force, fields, ends, far, lists, mate, u2, v2, col_f):
    on_face = lax.axis_index("layer") == layers // 2
    places = ((mate, 4 * NEAR), (far, CROSS_MATE), None, (far, CROSS_OWN))
    extra = second_ties(lists, slice(0, 512), places)
    even = on_even()
    forces = second_column(0, fields, ends, far)
    for c in range(3):
        col_f[0, c] = jnp.where(even, forces[c], 0.0)
        col_f[1, c] = jnp.where(even, 0.0, forces[c])
    for z in range(8):
        e = z + 1
        rate = dtm[e]
        for c in range(3):
            pull = with_columns(force[c, e], col_f[0, c, e : e + 1, :], col_f[1, c, e : e + 1, :])
            if z in (3, 4):
                pull = pull - jnp.where(on_face, extra[z - 3][c], 0.0)
            speed = v[c, e] - rate * pull
            v2[c, z] = speed
            u2[c, z] = u[c, e] + DT * speed


def second_contact(
    layers, u_in, v_in, dtm, lists, opp, fields, ends, u2, v2, u, v, col_f, sems
):
    even = on_even()
    on_face = lax.axis_index("layer") == layers // 2
    forces = second_column(1, fields, ends, opp)
    for c in range(3):
        col_f[0, c] = jnp.where(even, 0.0, forces[c])
        col_f[1, c] = jnp.where(even, forces[c], 0.0)

    def update(z, extra):
        e = z + 1
        rate = dtm[e]
        for c in range(3):
            pull = with_columns(jnp.zeros((16, 256), F32), col_f[0, c, e : e + 1, :], col_f[1, c, e : e + 1, :])
            if extra is not None:
                pull = pull - jnp.where(on_face, extra[c], 0.0)
            change = rate * pull
            v[c, z] = v_in[c, z] - change
            u[c, z] = u_in[c, z] - DT * change

    def copy_out(first, last):
        for src, dst in ((u, u2), (v, v2)):
            copy = pltpu.make_async_copy(src.at[:, first:last], dst.at[:, first:last], sems.at[len(copies)])
            copy.start()
            copies.append(copy)

    copies = []
    for first in (0, 5):
        for z in range(first, first + 3):
            update(z, None)
        copy_out(first, first + 3)
    extra = second_ties(lists, slice(512, 640), ((opp, CROSS_ON),))
    for z in (3, 4):
        update(z, extra[z - 3])
    copy_out(3, 5)
    for copy in copies:
        copy.wait()


VM = pl.BlockSpec(memory_space=pltpu.VMEM)
SM = pl.BlockSpec(memory_space=pltpu.SMEM)
HBM = pl.BlockSpec(memory_space=pltpu.HBM)


def call(kernel, in_specs, outs, scratch, name, flops, vmem=32, out_spec=VM):
    return pl.pallas_call(
        kernel,
        out_shape=[jax.ShapeDtypeStruct(shape, F32) for shape in outs],
        in_specs=in_specs,
        out_specs=[out_spec] * len(outs),
        scratch_shapes=[pltpu.VMEM(s, F32) if isinstance(s, tuple) else s for s in scratch],
        compiler_params=pltpu.CompilerParams(vmem_limit_bytes=vmem * 1024 * 1024),
        cost_estimate=pl.CostEstimate(flops=flops, bytes_accessed=flops // 25, transcendentals=0),
        name=name,
    )


def local(u, v, dt, lab, par, sol, land, stiff, tally):
    blocks, layers = lax.axis_size("plane"), lax.axis_size("layer")
    swaps = [(s, s ^ 1) for s in range(blocks)]
    crossings = [(s, s + 2 - 4 * (s % 2)) for s in range(blocks) if 0 <= s + 2 - 4 * (s % 2) < blocks]
    face_swaps = [(a * layers + layers // 2, b * layers + layers // 2) for a, b in swaps]

    def along_layer(value, steps):
        pairs = [(s, s + steps) for s in range(layers) if 0 <= s + steps < layers]
        return lax.ppermute(value, "layer", pairs)

    own = call(
        functools.partial(pack_export, blocks, layers),
        [HBM] * 7,
        [(EXPORT_ROWS, 256)],
        [u.shape, dt.shape, pltpu.VMEM(lab.shape, jnp.int32)]
        + [pltpu.VMEM((5, 1, 128), jnp.int32)] * 2
        + [(5, 1, 128), pltpu.SMEM((1, 5), jnp.int32), pltpu.VMEM((8, 640), jnp.int32)]
        + [pltpu.VMEM((256, 640), BF16), (16, 640), pltpu.SemaphoreType.DMA((7,))],
        "pack_export",
        100_000,
        63,
    )(u, dt, lab, sol.reshape(5, 1, 128), land.reshape(5, 1, 128), stiff.reshape(5, 1, 128), tally)[0]
    near = lax.ppermute(own, "plane", swaps)
    own = call(stage, [HBM], [own.shape], [pltpu.SemaphoreType.DMA], "stage", 100_000)(own)[0]
    cross, skip = call(pack_cross, [VM] * 2, [(CROSS_ROWS, 256), (SKIP_ROWS, 256)], [], "pack_cross", 1_000)(own, near)
    far = lax.ppermute(cross, "plane", crossings)
    skips = [(s * layers + layers // 2, t * layers + layers // 2) for t, s in crossings]
    opp = lax.ppermute(skip, ("plane", "layer"), skips)
    modes = [(12, 16, 256), (12, 16, 256)]
    plane = (16, 256)
    force, mass = call(
        functools.partial(first_block, layers),
        [VM] * 3 + [SM],
        [(3, 8, 16, 256), (8, 16, 256)],
        modes + [plane],
        "first_block",
        50_000_000,
    )(u, dt, lab, par)
    far, force, mass = lax.optimization_barrier((far, force, mass))
    up, dn, cols = call(
        pack_layer, [VM] * 6, [(ZU_ROWS, 256), (ZD_ROWS, 256), (COLS_ROWS, 256)], [], "pack_layer", 1_000
    )(u, v, dt, lab, near, far)
    zb, za = along_layer(up, 1), along_layer(dn, -1)
    u1, v1, dtm, in_f, in_m = call(
        functools.partial(first_inner, blocks, layers),
        [VM] * 2 + [SM] + [VM] * 4,
        [(3, 6, 16, 256), (3, 6, 16, 256), (6, 16, 256), (2, 3, 8, 256), (2, 8, 256)],
        [],
        "first_inner",
        1_000,
    )(u, v, par, own, cols, force, mass)
    opp, u1, v1 = lax.optimization_barrier((opp, u1, v1))
    u_face, v_face, values, lists = call(
        functools.partial(first_contact, layers),
        [VM] * 7,
        [(2, 3, 16, 256), (2, 3, 16, 256), (VALUES_ROWS, 256), (16, 640)],
        [],
        "first_contact",
        10_000_000,
    )(own, near, far, opp, u1, v1, dtm)
    mate = lax.ppermute(values, ("plane", "layer"), face_swaps)

    two = (2, 8, 256)
    u1, v1, dtm, ends = call(
        functools.partial(first_step, blocks, layers),
        [VM] * 4 + [SM] + [VM] * 13,
        [(3, 10, 16, 256), (3, 10, 16, 256), (10, 16, 256), (NEW_ROWS, 256)],
        [(4, 3, 8, 256), two, two, (2, 3, 8, 256), two],
        "first_step",
        20_000_000,
    )(u, v, dt, lab, par, own, cols, zb, za, force, mass, in_f, in_m, u1, v1, dtm, u_face, v_face)
    across = [(s, s + 1) for s in range(1, blocks - 1, 2)] + [(s, s - 1) for s in range(2, blocks, 2)]
    cross = call(pack_new_cross, [VM] * 3, [(NEW_CROSS_ROWS, 256)], [], "pack_new_cross", 100_000)(ends, values, mate)[0]
    far = lax.ppermute(cross, "plane", across)
    force, fields = call(
        functools.partial(second_block, blocks, layers),
        [VM] * 3 + [SM] + [VM] * 2,
        [(3, 10, 16, 256), (2, 4, 16, 256)],
        [(9, 16, 256), (9, 16, 256), (2, 16, 256)] + modes,
        "second_block",
        50_000_000,
    )(u1, dt, lab, par, zb, cols)
    far, force = lax.optimization_barrier((far, force))
    last = call(pack_last, [VM] * 2, [(NEW_CROSS_ROWS, 256)], [], "pack_last", 100_000)(ends, far)[0]
    opp = lax.ppermute(last, "plane", swaps)
    u2, v2 = call(
        functools.partial(second_step, layers), [VM] * 9, [(3, 8, 16, 256)] * 2, [(2, 3, 16, 256)], "second_step", 20_000_000
    )(u1, v1, dtm, force, fields, ends, far, lists, mate)
    return tuple(
        call(
            functools.partial(second_contact, layers),
            [VM] * 7,
            [(3, 8, 16, 256)] * 2,
            [(3, 8, 16, 256)] * 2 + [(2, 3, 16, 256), pltpu.SemaphoreType.DMA((6,))],
            "second_contact",
            10_000_000,
            out_spec=HBM,
        )(u2, v2, dtm, lists, opp, fields, ends)
    )


def solution(mesh):
    in_specs = (
        P(None, "layer", "plane", None),
        P(None, "layer", "plane", None),
        P("layer", "plane", None),
        P("layer", "plane", None),
        P(),
        P("plane", None, None),
        P("plane", None, None),
        P("plane", None, None),
        P("plane", None),
    )
    out_specs = (P(None, "layer", "plane", None), P(None, "layer", "plane", None))
    return jax.shard_map(local, mesh=mesh, in_specs=in_specs, out_specs=out_specs, check_vma=False)
```
